32 devices in a mesh: dp: 8 (over z, x), tensor: 4 (over y, core).
Axes of the slice: x: 2, y: 2, z: 4, core: 2. Of those that a mesh axis runs over, the one named last changes fastest.
Arguments:
- tokens: bfloat16 [12608, 512], P(('dp', 'tensor')), may hold values from -6 to 6
- cotangent: bfloat16 [12608, 512], P(('dp', 'tensor')), may hold values from -6 to 6
- norm_gain: float32 [2, 512], replicated, may hold values from 0.1 to 1.9
- qkv_weight: bfloat16 [3, 512, 512], P(None, 'dp', 'tensor'), may hold values from -0.25 to 0.25
- out_weight: bfloat16 [512, 512], P('dp', 'tensor'), may hold values from -1 to 1
- expert_in: bfloat16 [8, 512, 2048], P(None, 'dp', 'tensor'), may hold values from -0.25 to 0.25
- expert_out: bfloat16 [8, 512, 2048], P(None, 'dp', 'tensor'), may hold values from -1 to 1
- router_weight: bfloat16 [512, 8], replicated, may hold values from -0.125 to 0.125
- down_in: bfloat16 [5, 8, 512, 16], replicated, may hold values from -0.25 to 0.25
- up_heads: bfloat16 [3, 8, 16, 512], P(None, None, None, 'tensor'), may hold values from -1.5 to 1.5
- up_hidden: bfloat16 [8, 16, 2048], P(None, None, 'tensor'), may hold values from -1.5 to 1.5
- up_router: bfloat16 [8, 16, 8], replicated, may hold values from -0.75 to 0.75
- down_heads: bfloat16 [8, 512, 16], P(None, 'tensor'), may hold values from -0.25 to 0.25
- down_hidden: bfloat16 [8, 2048, 16], P(None, 'tensor'), may hold values from -0.125 to 0.125
- up_attn_out: bfloat16 [8, 16, 512], replicated, may hold values from -6 to 6
- up_expert_out: bfloat16 [8, 16, 512], replicated, may hold values from -12 to 12
- routes: int32 [12608, 2], P('dp'), may hold values from 0 to 7, all different within a row
- priority: int32 [8, 1576], P('dp'), may hold values from 0 to 1575, each once within a row
- adapter_index: int32 [64], P('dp'), may hold values from 0 to 7
Outputs:
- block_out: float32 [12608, 512], P(('dp', 'tensor'))
- input_grad: float32 [12608, 512], P(('dp', 'tensor'))
- grad_down_in: float32 [5, 8, 512, 16], replicated
- grad_up_heads: float32 [3, 8, 16, 512], P(None, None, None, 'tensor')
- grad_up_hidden: float32 [8, 16, 2048], P(None, None, 'tensor')
- grad_up_router: float32 [8, 16, 8], replicated
- grad_down_heads: float32 [8, 512, 16], P(None, 'tensor')
- grad_down_hidden: float32 [8, 2048, 16], P(None, 'tensor')
- grad_up_attn_out: float32 [8, 16, 512], replicated
- grad_up_expert_out: float32 [8, 16, 512], replicated
The draws below stay inside these ranges and needn't reach their ends.
Inputs may be any that keep to these rules, and one draw needn't show every extreme that they name: `routes`: each row names two different experts. `priority`: each row holds every number from 0 to 1575 once.
All inputs are finite; a program needn't handle non-finite values.
Results may differ from the reference program's by a relative error of at most 0.023.
The reference program's roundings to bfloat16 on the way count: a program that leaves them out, or rounds other values in their place, can miss the bound.
Values may be sent and summed in bfloat16 or wider, within the bound.
No kernel may reach another device: no remote copies, remote signals or barrier semaphores. Data moves between devices by JAX's collectives and lax.ppermute only.
A program may use at most 192 MiB of HBM per device.

```python
import jax
import jax.numpy as jnp
from jax import lax

D = 512
HEADS = 8
FF = 2048
RANK = 16
ADAPTERS = 8
SEQ = 197
IMG_DP = 8
EXPERTS = 8
HEAD_DIM = 64
GROUP = 1576
CAP = 394
GROUPS = 8
IMAGES = 64
TOKENS = 12608


def with_ends(values, key, low, largest):
    shape = values.shape
    index_at = [jax.random.randint(jax.random.fold_in(key, axis), (), 0, shape[axis]) for axis in range(len(shape))]
    values = values.at[tuple(index_at)].set(low)
    longest = shape.index(max(shape))
    index_at[longest] = (index_at[longest] + 1) % shape[longest]
    return values.at[tuple(index_at)].set(largest)


def shard_levels(rng, shape, shards, least, high):
    level, own = 1.0, jax.random.fold_in(rng, 6)
    for dim, blocks in shards:
        heights = jnp.exp(jax.random.uniform(jax.random.fold_in(own, dim), (blocks,), jnp.float32, least / len(shards), high / len(shards)))
        level = level * jnp.repeat(heights, shape[dim] // blocks).reshape([-1 if axis == dim else 1 for axis in range(len(shape))])
    return level


def different_ones(rng, rows, number_of, top, lift):
    order = jax.random.permutation(jax.random.fold_in(rng, 1), number_of)
    favour = order
    for power in range(3):
        favour = favour * favour // number_of
    favour = favour * lift // number_of
    tickets = jax.random.randint(jax.random.fold_in(rng, 2), (rows, number_of), 0, 4096) + favour
    sure = jax.random.permutation(jax.random.fold_in(rng, 3), rows)[jnp.arange(number_of) % rows]
    tickets = jnp.where(jnp.arange(rows)[:, None] == sure[None, :], 1 << 14, tickets)
    score = tickets * number_of + jnp.arange(number_of)
    return lax.top_k(score.astype(jnp.int32), top)[1].astype(jnp.int32)


def centred(stream_key, extent, deviation, most, cuts=(), kind=jnp.bfloat16):
    values = deviation * jax.random.normal(stream_key, extent, jnp.float32)
    if cuts:
        values = values * shard_levels(stream_key, extent, cuts, -0.22, 0.18)
    return jnp.clip(values, -most, most).astype(kind)


def setup_inputs(seed: int = 0) -> dict:
    streams_of = jax.random.split(jax.random.key(seed), 20)
    tokens = centred(streams_of[0], (TOKENS, D), 1.0, 6.0, ((0, 32),))
    cotangent = centred(streams_of[1], (TOKENS, D), 1.0, 6.0, ((0, 32),))
    norm_gain = jnp.clip(1.0 + 0.18 * jax.random.normal(streams_of[2], (2, D), jnp.float32), 0.1, 1.9)
    qkv_weight = centred(streams_of[3], (3, D, D), D ** -0.5, 0.25, ((1, 8), (2, 4)))
    out_weight = centred(streams_of[4], (D, D), (4.0 * D ** -0.5), 1.0, ((0, 8), (1, 4)))
    expert_in = centred(streams_of[5], (EXPERTS, D, FF), D ** -0.5, 0.25, ((1, 8), (2, 4)))
    expert_out = centred(streams_of[6], (EXPERTS, D, FF), (8.0 * FF ** -0.5), 1.0, ((1, 8), (2, 4)))
    router_weight = centred(streams_of[7], (D, EXPERTS), (0.5 * D ** -0.5), 0.125)
    down_in = centred(streams_of[8], (5, ADAPTERS, D, RANK), D ** -0.5, 0.25)
    up_heads = centred(streams_of[9], (3, ADAPTERS, RANK, D), RANK ** -0.5, 1.5, ((3, 4),))
    up_hidden = centred(streams_of[10], (ADAPTERS, RANK, FF), RANK ** -0.5, 1.5, ((2, 4),))
    up_router = centred(streams_of[11], (ADAPTERS, RANK, EXPERTS), (0.5 * RANK ** -0.5), 0.75)
    down_heads = centred(streams_of[12], (ADAPTERS, D, RANK), D ** -0.5, 0.25, ((1, 4),))
    down_hidden = centred(streams_of[13], (ADAPTERS, FF, RANK), FF ** -0.5, 0.125, ((1, 4),))
    up_attn_out = centred(streams_of[14], (ADAPTERS, RANK, D), (4.0 * RANK ** -0.5), 6.0)
    up_expert_out = centred(streams_of[15], (ADAPTERS, RANK, D), (8.0 * RANK ** -0.5), 12.0)
    routes = different_ones(streams_of[16], TOKENS, EXPERTS, 2, 2048)
    priority = jax.vmap(lambda own: jax.random.permutation(own, GROUP))(jax.random.split(streams_of[17], GROUPS)).reshape((GROUPS, GROUP)).astype(jnp.int32)
    adapter_index = with_ends(jax.random.randint(streams_of[18], (IMAGES,), 0, ADAPTERS), jax.random.fold_in(streams_of[18], 1), 0, ADAPTERS - 1).astype(jnp.int32)
    return {"tokens": tokens, "cotangent": cotangent, "norm_gain": norm_gain, "qkv_weight": qkv_weight, "out_weight": out_weight, "expert_in": expert_in, "expert_out": expert_out, "router_weight": router_weight, "down_in": down_in, "up_heads": up_heads, "up_hidden": up_hidden, "up_router": up_router, "down_heads": down_heads, "down_hidden": down_hidden, "up_attn_out": up_attn_out, "up_expert_out": up_expert_out, "routes": routes, "priority": priority, "adapter_index": adapter_index}


EPS = 1e-06
HIGH = lax.Precision.HIGHEST

@jax.custom_vjp
def low(v):
    return lax.optimization_barrier(v.astype(jnp.bfloat16)).astype(jnp.float32)

@jax.custom_vjp
def low_back(v):
    return v

def low_keep(v):
    return (low(v), None)

def low_pass(kept, grad):
    return (grad,)

def back_keep(v):
    return (v, None)

def back_low(kept, grad):
    return (low(grad),)
low.defvjp(low_keep, low_pass)
low_back.defvjp(back_keep, back_low)

def precise_dot(left, right):
    return jnp.dot(left, right, precision=HIGH)

def columns(array):
    return array.transpose(1, 0, 2).reshape(array.shape[1], array.shape[0] * array.shape[2])

def stacked(array):
    return array.reshape(array.shape[0] * array.shape[1], array.shape[2])

def normalize(value, gain):
    center = value - lax.optimization_barrier(jnp.mean(value, -1, keepdims=True))
    spread = lax.optimization_barrier(jnp.mean(center * center, -1, keepdims=True))
    return center * lax.rsqrt(spread + EPS) * gain

def assign_slots(routes, priority):
    count = routes.shape[0]
    order = jnp.zeros((count,), jnp.int32).at[priority].set(jnp.arange(count, dtype=jnp.int32))
    ranked = routes[order]
    choose = (ranked[:, :, None] == jnp.arange(EXPERTS, dtype=jnp.int32)[None, None, :]).astype(jnp.int32)
    flat = choose.transpose(1, 0, 2).reshape(2 * count, EXPERTS)
    earlier = (jnp.cumsum(flat, axis=0) - flat).astype(jnp.int32)
    place = lax.optimization_barrier(jnp.sum(earlier * flat, axis=-1)).astype(jnp.int32).reshape(2, count).T
    place = jnp.zeros((count, 2), jnp.int32).at[order].set(place)
    keep = place < CAP
    total = EXPERTS * CAP
    slot = jnp.where(keep, routes * CAP + place, total).astype(jnp.int32)
    owners = jnp.repeat(jnp.arange(count, dtype=jnp.int32), 2)
    owner = jnp.full((total + 1,), count, jnp.int32).at[slot.reshape(-1)].set(owners)
    return (slot, keep.astype(jnp.float32), owner[:total])

def block(value, adapters, frozen, routes, priority, images):
    down_in, up_heads, up_hidden, up_router, down_heads, down_hidden, up_aout, up_eout = adapters
    gains, wqkv, wout, win, wexo, wrouter = frozen
    count = value.shape[0]
    code_width = ADAPTERS * RANK
    image_mask = (images[:, None] == (jnp.arange(code_width, dtype=jnp.int32) // RANK)[None, :]).astype(jnp.float32)
    mask = jnp.repeat(image_mask, SEQ, axis=0)
    normed = low(normalize(value, gains[0]))
    parts = []
    for member in range(3):
        code = mask * precise_dot(normed, columns(down_in[member]))
        parts.append(low_back(low(precise_dot(normed, wqkv[member]) + precise_dot(code, stacked(up_heads[member])))))
    shape = (count // SEQ, SEQ, HEADS, HEAD_DIM)
    query = parts[0].reshape(shape)
    keys = parts[1].reshape(shape)
    values = parts[2].reshape(shape)
    scale = HEAD_DIM ** (-0.5)
    scores = low_back(jnp.einsum('ishd,ithd->ihst', query, keys, precision=HIGH) * scale)
    weights = low(jax.nn.softmax(scores, axis=-1))
    mixed = jnp.einsum('ihst,ithd->ishd', weights, values, precision=HIGH).reshape(count, D)
    mixed = low_back(low(mixed))
    head_code = mask * precise_dot(mixed, columns(down_heads))
    attended = precise_dot(mixed, wout.T) + precise_dot(head_code, stacked(up_aout))
    middle = value + low_back(attended)
    normed2 = low(normalize(middle, gains[1]))
    route_code = mask * precise_dot(normed2, columns(down_in[4]))
    logits = precise_dot(normed2, wrouter) + precise_dot(route_code, stacked(up_router))
    probs = jax.nn.softmax(logits, axis=-1)
    gates = jnp.take_along_axis(probs, routes, axis=1)
    slot, keep, owner = assign_slots(routes, priority)
    hidden_code = mask * precise_dot(normed2, columns(down_in[3]))
    pad_rows = jnp.concatenate([normed2, jnp.zeros((1, D), jnp.float32)], 0)
    pad_code = jnp.concatenate([hidden_code, jnp.zeros((1, code_width), jnp.float32)], 0)
    pad_mask = jnp.concatenate([mask, jnp.zeros((1, code_width), jnp.float32)], 0)
    sent = pad_rows[owner].reshape(EXPERTS, CAP, D)
    sent_code = pad_code[owner]
    slot_mask = pad_mask[owner]
    before = jnp.einsum('ecd,edf->ecf', sent, win, precision=HIGH).reshape(EXPERTS * CAP, FF)
    before = before + precise_dot(sent_code, stacked(up_hidden))
    active = low(jax.nn.gelu(low_back(before), approximate=True))
    out_code = slot_mask * precise_dot(active, columns(down_hidden))
    returned = jnp.einsum('ecf,edf->ecd', active.reshape(EXPERTS, CAP, FF), wexo, precision=HIGH).reshape(EXPERTS * CAP, D)
    returned = low_back(returned + precise_dot(out_code, stacked(up_eout)))
    padded = jnp.concatenate([returned, jnp.zeros((1, D), jnp.float32)], 0)
    mixture = keep[:, 0:1] * gates[:, 0:1] * padded[slot[:, 0]] + keep[:, 1:2] * gates[:, 1:2] * padded[slot[:, 1]]
    return middle + mixture

def reference(tokens, cotangent, norm_gain, qkv_weight, out_weight, expert_in, expert_out, router_weight, down_in, up_heads, up_hidden, up_router, down_heads, down_hidden, up_attn_out, up_expert_out, routes, priority, adapter_index):
    frozen = tuple((item.astype(jnp.float32) for item in (norm_gain, qkv_weight, out_weight, expert_in, expert_out, router_weight)))
    adapters = tuple((item.astype(jnp.float32) for item in (down_in, up_heads, up_hidden, up_router, down_heads, down_hidden, up_attn_out, up_expert_out)))
    groups = priority.shape[0]
    inputs = (tokens.astype(jnp.float32).reshape(groups, GROUP, D), cotangent.astype(jnp.float32).reshape(groups, GROUP, D), routes.reshape(groups, GROUP, 2), priority, adapter_index.reshape(groups, IMG_DP))

    def step(totals, item):
        value, upstream, group_routes, group_priority, images = item

        def forward(entry, weights):
            return block(entry, weights, frozen, group_routes, group_priority, images)
        result, pullback = jax.vjp(forward, value, adapters)
        entry_grad, weight_grads = pullback(upstream)
        return (tuple((total + grad for total, grad in zip(totals, weight_grads))), (result, entry_grad))
    zeros = tuple((jnp.zeros(item.shape, jnp.float32) for item in adapters))
    totals, (results, entry_grads) = lax.scan(step, zeros, inputs)
    return (results.reshape(-1, D), entry_grads.reshape(-1, D), totals[0], totals[1], totals[2], totals[3], totals[4], totals[5], totals[6], totals[7])
```

```python
from functools import partial

import jax
import jax.numpy as jnp
from jax import lax
from jax.experimental import pallas as pl
from jax.experimental.pallas import tpu as pltpu
from jax.sharding import PartitionSpec as P

HEADS = 8
RANK = 16
ADAPTERS = 8
SEQ = 197
EXPERTS = 8
HEAD_DIM = 64
CAP = 394

EPS = 1e-06
CODE = ADAPTERS * RANK
ROWS = 208
SLOTS = 400
SCALE = HEAD_DIM ** (-0.5)
F32 = jnp.float32
BF16 = jnp.bfloat16
VMEM_LIMIT = 56 * 1024 * 1024


def dot(left, right):
    return lax.dot_general(left, right, (((1,), (0,)), ((), ())), preferred_element_type=F32)


def dot_t(left, right):
    return lax.dot_general(left, right, (((1,), (1,)), ((), ())), preferred_element_type=F32)


def tdot(left, right):
    return lax.dot_general(left, right, (((0,), (0,)), ((), ())), preferred_element_type=F32)


def lanes(shape):
    return lax.broadcasted_iota(jnp.int32, shape, len(shape) - 1)


def sublanes(shape):
    return lax.broadcasted_iota(jnp.int32, shape, len(shape) - 2)


def norm_rows(value, gain):
    center = value - jnp.mean(value, -1, keepdims=True)
    spread = jnp.mean(center * center, -1, keepdims=True)
    return center * lax.rsqrt(spread + EPS) * gain


def norm_back(value, gain, grad):
    center = value - jnp.mean(value, -1, keepdims=True)
    rate = lax.rsqrt(jnp.mean(center * center, -1, keepdims=True) + EPS)
    unit = center * rate
    grad = grad * gain
    along = jnp.mean(grad * unit, -1, keepdims=True)
    return rate * (grad - jnp.mean(grad, -1, keepdims=True) - unit * along)


def gelu_pair(value):
    square = value * value
    inner = 0.7978845608028654 * value * (1.0 + 0.044715 * square)
    bent = jnp.tanh(inner)
    half = 0.5 * (1.0 + bent)
    slope = half + 0.5 * value * (1.0 - bent * bent) * (
        0.7978845608028654 * (1.0 + 3.0 * 0.044715 * square)
    )
    return value * half, slope


def call(body, outs, scratch=(), smem=0, grid=None, in_specs=None, out_specs=None, cost=None):
    options = {}
    if grid is not None:
        options = dict(grid=grid, in_specs=in_specs, out_specs=out_specs)
    elif smem:
        def build(*args):
            specs = [pl.BlockSpec(memory_space=pltpu.SMEM)] * smem
            specs += [pl.BlockSpec(memory_space=pltpu.VMEM)] * (len(args) - smem)
            return call(body, outs, scratch, 0, (), specs, None, cost)(*args)

        return build
    if grid == ():
        options = dict(in_specs=in_specs)
    return pl.pallas_call(
        body,
        out_shape=outs,
        scratch_shapes=list(scratch),
        compiler_params=pltpu.CompilerParams(vmem_limit_bytes=VMEM_LIMIT),
        cost_estimate=cost,
        **options,
    )


def like(shape, dtype):
    return jax.ShapeDtypeStruct(shape, dtype)


def cost(flops, size):
    return pl.CostEstimate(flops=int(flops), bytes_accessed=int(size), transcendentals=0)


def image_mask(adapter, index):
    return jnp.where(lanes((1, CODE)) // RANK == adapter[index], 1.0, 0.0)


def route_kernel(cot, rrow, rcol, prow, pcol, dy, pos_row, pos_col, wide):
    images = dy.shape[0] // ROWS
    total = prow.shape[1]
    wide[...] = jnp.zeros_like(wide)
    wide[0 : cot.shape[0], :] = cot[...].astype(F32)
    dy[...] = jnp.zeros_like(dy)
    for image in range(images):
        part = wide[image * SEQ : image * SEQ + ROWS, :]
        part = jnp.where(sublanes((ROWS, 1)) < SEQ, part, 0.0)
        dy[image * ROWS : (image + 1) * ROWS, :] = part.astype(BF16)
    kinds = sublanes((2 * EXPERTS, total))
    first = jnp.where(rrow[0:1, :] == kinds, 1.0, 0.0)
    second = jnp.where(rrow[1:2, :] == kinds, 1.0, 0.0)
    before_row = jnp.sum(first, axis=1, keepdims=True)
    first_low = first.astype(BF16)
    second_low = second.astype(BF16)
    step = 128
    for at in range(0, total, step):
        earlier = jnp.where(pcol[...] < prow[:, at : at + step], 1.0, 0.0).astype(BF16)
        place = jnp.where(
            first[:, at : at + step] > 0.5,
            dot(first_low, earlier),
            jnp.where(
                second[:, at : at + step] > 0.5, dot(second_low, earlier) + before_row, -1.0
            ),
        )
        pos_row[:, at : at + step] = jnp.where(place < CAP, place, -1.0)
    kinds = lanes((total, 2 * EXPERTS))
    before_col = jnp.sum(
        jnp.where(rcol[:, 0:1] == kinds, 1.0, 0.0), axis=0, keepdims=True
    )
    kinds = lanes((ROWS, 2 * EXPERTS))
    for at in range(0, total, ROWS):
        earlier = jnp.where(prow[...] < pcol[at : at + ROWS, :], 1.0, 0.0).astype(BF16)
        place = jnp.where(
            rcol[at : at + ROWS, 0:1] == kinds,
            dot_t(earlier, first_low),
            jnp.where(
                rcol[at : at + ROWS, 1:2] == kinds,
                dot_t(earlier, second_low) + before_col,
                -1.0,
            ),
        )
        pos_col[at : at + ROWS, :] = jnp.where(place < CAP, place, -1.0)


def assemble_kernel(count, *refs):
    parts, extra, out = refs[:count], refs[count], refs[count + 1]
    me = lax.axis_index("dp")
    feats = parts[0].shape[1]
    for step in range(count):
        owner = lax.rem(me - step + count, count)
        rows = pl.ds(pl.multiple_of(owner * feats, feats), feats)
        for member in range(4):
            out[member, rows, :] = parts[step][member]
    out[4] = extra[...]


def forward_kernel(
    adapter, tokens, gain, own, core, side, both, down, up_out,
    weights, x_out, normed_out, code_out, qkv_out, prob_out, mixed_out, hcode_out,
    middle_out, normed2_out, wide,
):
    me = lax.axis_index("tensor")
    for step, part in enumerate((own, core, side, both)):
        cols = pl.ds(pl.multiple_of(lax.bitwise_xor(me, step) * 128, 128), 128)
        weights[:, :, cols] = part[...]
    images = x_out.shape[0] // ROWS
    width = tokens.shape[1]
    wide[...] = jnp.zeros_like(wide)
    wide[0 : tokens.shape[0], :] = tokens[...].astype(F32)
    for image in range(images):
        at = image * ROWS
        rows = slice(at, at + ROWS)
        mask = image_mask(adapter, me * images + image)
        real = sublanes((ROWS, 1)) < SEQ
        x = jnp.where(real, wide[image * SEQ : image * SEQ + ROWS, :], 0.0)
        x_out[rows, :] = x
        normed = norm_rows(x, gain[0:1, :]).astype(BF16)
        normed_out[rows, :] = normed
        for member in range(3):
            code = (mask * dot_t(normed, down[member])).astype(BF16)
            code_out[rows, member * CODE : (member + 1) * CODE] = code
            up = weights[4, member * CODE : (member + 1) * CODE, :]
            proj = dot(normed, weights[member]) + dot(code, up)
            qkv_out[rows, member * width : (member + 1) * width] = proj.astype(BF16)
        low_half = lanes((1, 128)) < HEAD_DIM
        half = (low_half, jnp.logical_not(low_half))
        real_key = lanes((1, ROWS)) < SEQ
        for pair in range(HEADS // 2):
            cols = pair * 128
            q = qkv_out[rows, cols : cols + 128].astype(F32) * SCALE
            k = qkv_out[rows, width + cols : width + cols + 128]
            v = qkv_out[rows, 2 * width + cols : 2 * width + cols + 128].astype(F32)
            mixed = jnp.zeros((ROWS, 128), F32)
            for head in range(2):
                score = dot_t(jnp.where(half[head], q, 0.0).astype(BF16), k)
                score = jnp.where(real_key, score, -1e30)
                raised = jnp.exp(score - jnp.max(score, -1, keepdims=True))
                prob = raised / jnp.sum(raised, -1, keepdims=True)
                prob_out[(image * HEADS // 2 + pair) * 2 + head] = prob
                mixed = mixed + dot(
                    prob.astype(BF16), jnp.where(half[head], v, 0.0).astype(BF16)
                )
            mixed_out[rows, cols : cols + 128] = mixed.astype(BF16)
        mixed = mixed_out[rows, :]
        hcode = (mask * dot_t(mixed, weights[4, 3 * CODE : 4 * CODE, :])).astype(BF16)
        hcode_out[rows, :] = hcode
        middle = x + dot_t(mixed, weights[3]) + dot(hcode, up_out[...])
        middle_out[rows, :] = middle
        normed2_out[rows, :] = norm_rows(middle, gain[1:2, :]).astype(BF16)


def dispatch_kernel(
    adapter, own, core, side, both, dy_own, dy_core, dy_side, dy_both,
    pos_row, down, router, up_router,
    slots, rows_out, rcode_out, prob_out,
):
    step = pl.program_id(0)
    me = lax.axis_index("tensor")
    count = own.shape[0]
    images = count // ROWS
    width = own.shape[1]

    @pl.when(step == 0)
    def _():
        for index, (part, dy) in enumerate(
            ((own, dy_own), (core, dy_core), (side, dy_side), (both, dy_both))
        ):
            spot = lax.bitwise_xor(me, index)
            rows = pl.ds(pl.multiple_of(spot * count, count), count)
            rows_out[rows, 0:width] = part[...]
            rows_out[rows, width : 2 * width] = dy[...]
            for image in range(images):
                mask = image_mask(adapter, spot * images + image)
                rows = pl.ds(pl.multiple_of(spot * count + image * ROWS, ROWS), ROWS)
                normed = part[image * ROWS : (image + 1) * ROWS, :]
                rcode = (mask * dot_t(normed, down[4])).astype(BF16)
                rcode_out[rows, :] = rcode
                logits = dot_t(normed, router[...]) + dot_t(rcode, up_router[...])
                lane = lanes((1, 128))
                logits = jnp.where(lane < 2 * EXPERTS, logits, -1e30)
                raised = jnp.exp(logits - jnp.max(logits, -1, keepdims=True))
                mass = jnp.sum(jnp.where(lane < EXPERTS, raised, 0.0), -1, keepdims=True)
                prob = raised / mass
                prob_out[rows, :] = prob
                high = prob.astype(BF16).astype(F32)
                aux = jnp.where(lane < EXPERTS, high, prob - high)
                rows_out[rows, 2 * width : 2 * width + 128] = aux.astype(BF16)
                rows_out[rows, 2 * width + 128 : 2 * width + 256] = jnp.broadcast_to(
                    mask, (ROWS, CODE)
                ).astype(BF16)

    pos = pos_row[pl.ds(step, 1), :]
    chosen = jnp.where(
        sublanes((SLOTS, pos.shape[1])).astype(F32) == pos, 1.0, 0.0
    ).astype(BF16)
    slots[0] = dot(chosen, rows_out[...]).astype(BF16)


def expert_kernel(
    slots, w_in, w_out, up_hid, down_hid, up_exo, down,
    rows_ref, rcode, prob, pos_col, router, up_router, adapter,
    mix_keep, mix_send, grad_keep, grad_send,
    g_up_hid, g_down_hid, g_up_exo, g_down3, g_down4, g_router,
    total,
):
    step = pl.program_id(0)
    last = pl.num_programs(0) - 1
    width = w_in.shape[1]
    lane = lanes((1, 128))

    @pl.when(step == 0)
    def _():
        total[...] = jnp.zeros_like(total)
        g_up_hid[...] = jnp.zeros_like(g_up_hid)
        g_down_hid[...] = jnp.zeros_like(g_down_hid)
        g_up_exo[...] = jnp.zeros_like(g_up_exo)
        g_down3[...] = jnp.zeros_like(g_down3)

    x = slots[0, :, 0:width]
    dy = slots[0, :, width : 2 * width].astype(F32)
    aux = slots[0, :, 2 * width : 2 * width + 128].astype(F32)
    mask = slots[0, :, 2 * width + 128 : 2 * width + 256].astype(F32)
    here = lax.rem(lane, EXPERTS) == step
    here = jnp.logical_and(here, lane < 2 * EXPERTS)
    gate = jnp.sum(jnp.where(here, aux, 0.0), -1, keepdims=True)
    hcode = (mask * dot_t(x, down[3])).astype(BF16)
    before = dot(x, w_in[0]) + dot(hcode, up_hid[...])
    active, slope = gelu_pair(before)
    active = active.astype(BF16)
    ocode = (mask * dot_t(active, down_hid[...])).astype(BF16)
    returned = dot_t(active, w_out[0]) + dot(ocode, up_exo[...])
    gate_grad = jnp.sum(returned * dy, -1, keepdims=True)
    back = (gate * dy).astype(BF16)
    ocode_grad = (mask * dot_t(back, up_exo[...])).astype(BF16)
    active_grad = dot(back, w_out[0]) + dot(ocode_grad, down_hid[...])
    before_grad = (slope * active_grad).astype(BF16)
    hcode_grad = (mask * dot_t(before_grad, up_hid[...])).astype(BF16)
    x_grad = dot_t(before_grad, w_in[0]) + dot(hcode_grad, down[3])
    g_up_exo[...] += tdot(ocode, back)
    g_down_hid[...] += tdot(ocode_grad, active)
    g_up_hid[...] += tdot(hcode, before_grad)
    g_down3[...] += tdot(hcode_grad, x)
    high = gate_grad.astype(BF16).astype(F32)
    spread = jnp.where(here, jnp.where(lane < EXPERTS, high, gate_grad - high), 0.0)
    ending = jnp.concatenate(
        [(gate * returned).astype(BF16), x_grad.astype(BF16), spread.astype(BF16)], 1
    )
    tall = pos_col.shape[0]
    part = 4 * ROWS
    for at in range(0, tall, part):
        spot = jnp.sum(
            jnp.where(lanes((1, 2 * EXPERTS)) == step, pos_col[at : at + part, :], 0.0),
            -1,
            keepdims=True,
        )
        chosen = jnp.where(lanes((part, SLOTS)).astype(F32) == spot, 1.0, 0.0).astype(BF16)
        total[at : at + part, :] += dot(chosen, ending)

    @pl.when(step == last)
    def _():
        me = lax.axis_index("tensor")
        count = mix_keep.shape[1]
        images = count // ROWS
        g_down4[...] = jnp.zeros_like(g_down4)
        g_router[...] = jnp.zeros_like(g_router)
        for index in range(4):
            spot = lax.bitwise_xor(me, index)
            mix_out = (mix_keep, mix_send)[index % 2]
            grad_out = (grad_keep, grad_send)[index % 2]
            for image in range(images):
                rows = pl.ds(pl.multiple_of(spot * count + image * ROWS, ROWS), ROWS)
                local = slice(image * ROWS, (image + 1) * ROWS)
                mask = image_mask(adapter, spot * images + image)
                mix_out[index // 2, local, :] = total[rows, 0:width].astype(BF16)
                gates = total[rows, 2 * width : 2 * width + 128]
                probs = jnp.where(lane < 2 * EXPERTS, prob[rows, :], 0.0)
                mean = jnp.sum(probs * gates, -1, keepdims=True)
                logit = (probs * (gates - jnp.where(lane < EXPERTS, mean, 0.0))).astype(BF16)
                rcode_grad = (mask * dot(logit, up_router[...])).astype(BF16)
                grad = total[rows, width : 2 * width] + dot(logit, router[...])
                grad = grad + dot(rcode_grad, down[4])
                grad_out[index // 2, local, :] = grad.astype(BF16)
                g_router[...] += tdot(rcode[rows, :], logit)
                g_down4[...] += tdot(rcode_grad, rows_ref[rows, 0:width])


def backward_kernel(
    adapter, dy, middle, grad_a, grad_b, gain, weights, down, up_out,
    x_in, normed_in, code_in, qkv_in, prob_in, mixed_in, hcode_in,
    input_grad, g_up_out, g_down_heads, g_up_heads, g_down_qkv,
    mixed_grad, proj_grad, wide,
):
    me = lax.axis_index("tensor")
    images = dy.shape[0] // ROWS
    width = dy.shape[1]
    g_up_out[...] = jnp.zeros_like(g_up_out)
    g_down_heads[...] = jnp.zeros_like(g_down_heads)
    g_up_heads[...] = jnp.zeros_like(g_up_heads)
    g_down_qkv[...] = jnp.zeros_like(g_down_qkv)
    for image in range(images):
        at = image * ROWS
        rows = slice(at, at + ROWS)
        mask = image_mask(adapter, me * images + image)
        summed = grad_a[rows, :].astype(F32) + grad_b[rows, :].astype(F32)
        middle_grad = dy[rows, :].astype(F32) + norm_back(
            middle[rows, :], gain[1:2, :], summed
        )
        wide[0:ROWS, :] = middle_grad
        low = middle_grad.astype(BF16)
        hcode_grad = (mask * dot_t(low, up_out[...])).astype(BF16)
        down_heads = weights[4, 3 * CODE : 4 * CODE, :]
        mixed_grad[...] = (dot(low, weights[3]) + dot(hcode_grad, down_heads)).astype(BF16)
        g_up_out[...] += tdot(hcode_in[rows, :], low)
        g_down_heads[...] += tdot(hcode_grad, mixed_in[rows, :])
        low_half = lanes((1, 128)) < HEAD_DIM
        half = (low_half, jnp.logical_not(low_half))
        for pair in range(HEADS // 2):
            cols = pair * 128
            q = qkv_in[rows, cols : cols + 128].astype(F32) * SCALE
            k = qkv_in[rows, width + cols : width + cols + 128].astype(F32) * SCALE
            v = qkv_in[rows, 2 * width + cols : 2 * width + cols + 128]
            m = mixed_grad[:, cols : cols + 128].astype(F32)
            q_grad = jnp.zeros((ROWS, 128), F32)
            k_grad = jnp.zeros((ROWS, 128), F32)
            v_grad = jnp.zeros((ROWS, 128), F32)
            for head in range(2):
                prob = prob_in[(image * HEADS // 2 + pair) * 2 + head]
                m_head = jnp.where(half[head], m, 0.0).astype(BF16)
                v_grad = v_grad + tdot(prob.astype(BF16), m_head)
                weight_grad = dot_t(m_head, v)
                along = jnp.sum(prob * weight_grad, -1, keepdims=True)
                score = (prob * (weight_grad - along)).astype(BF16)
                q_grad = q_grad + dot(score, jnp.where(half[head], k, 0.0).astype(BF16))
                k_grad = k_grad + tdot(score, jnp.where(half[head], q, 0.0).astype(BF16))
            proj_grad[:, cols : cols + 128] = q_grad.astype(BF16)
            proj_grad[:, width + cols : width + cols + 128] = k_grad.astype(BF16)
            proj_grad[:, 2 * width + cols : 2 * width + cols + 128] = v_grad.astype(BF16)
        normed = normed_in[rows, :]
        normed_grad = jnp.zeros((ROWS, width), F32)
        for member in range(3):
            grad = proj_grad[:, member * width : (member + 1) * width]
            up = weights[4, member * CODE : (member + 1) * CODE, :]
            code_grad = (mask * dot_t(grad, up)).astype(BF16)
            code = code_in[rows, member * CODE : (member + 1) * CODE]
            g_up_heads[member] += tdot(code, grad)
            g_down_qkv[member] += tdot(code_grad, normed)
            normed_grad = normed_grad + dot_t(grad, weights[member])
            normed_grad = normed_grad + dot(code_grad, down[member])
        result = wide[0:ROWS, :] + norm_back(x_in[rows, :], gain[0:1, :], normed_grad)
        wide[ROWS : 2 * ROWS, :] = result
        input_grad[image * SEQ : (image + 1) * SEQ, :] = wide[ROWS : ROWS + SEQ, :]


def finish_kernel(middle, part_a, part_b, out, wide):
    images = middle.shape[0] // ROWS
    for image in range(images):
        rows = slice(image * ROWS, (image + 1) * ROWS)
        wide[...] = (
            middle[rows, :] + part_a[rows, :].astype(F32) + part_b[rows, :].astype(F32)
        )
        out[image * SEQ : (image + 1) * SEQ, :] = wide[0:SEQ, :]


def swap(value, bit):
    size = lax.axis_size("tensor")
    return lax.ppermute(value, "tensor", [(at, at ^ bit) for at in range(size)])


def gather_four(value):
    core = swap(value, 1)
    side = swap(value, 2)
    return value, core, side, swap(side, 1)


def reduce_pair(keep, send):
    came = swap(send, 1)
    mine = keep[0].astype(F32) + came[0].astype(F32)
    other = (keep[1].astype(F32) + came[1].astype(F32)).astype(BF16)
    return mine.astype(BF16), swap(other, 2)


def gather_dp(block, extra):
    size = lax.axis_size("dp")
    feats = block.shape[1]
    if size == 8 and feats % 16 == 0:
        parts = [block]
        for step in range(1, size):
            parts.append(
                lax.ppermute(block, "dp", [(at, (at + step) % size) for at in range(size)])
            )
        return call(
            partial(assemble_kernel, size), like((5, size * feats, 128), BF16)
        )(*parts, extra)
    whole = lax.all_gather(block, "dp", axis=1, tiled=True)
    return jnp.concatenate([whole, extra[None]], 0)


def sum_all(value, axes):
    came = lax.all_to_all(value, axes, 0, 0)
    return jnp.sum(came.astype(F32), 0)


def per_device(
    tokens,
    cotangent,
    norm_gain,
    qkv_weight,
    out_weight,
    expert_in,
    expert_out,
    router_weight,
    down_in,
    up_heads,
    up_hidden,
    up_router,
    down_heads,
    down_hidden,
    up_attn_out,
    up_expert_out,
    routes,
    priority,
    adapter_index,
):
    width = tokens.shape[1]
    local = tokens.shape[0]
    images = local // SEQ
    group_images = routes.shape[0] // SEQ
    count = images * ROWS
    tall = group_images * ROWS
    hidden = expert_in.shape[2]
    dp = lax.axis_size("dp")
    tensor = lax.axis_size("tensor")

    block = jnp.concatenate([qkv_weight, out_weight[None]], 0)
    extra = jnp.concatenate(
        [
            up_heads.reshape(3 * CODE, up_heads.shape[3]),
            down_heads.swapaxes(1, 2).reshape(CODE, down_heads.shape[1]),
        ],
        0,
    )
    mine = gather_dp(block, extra)
    four = gather_four(mine)
    in_full = lax.all_gather(expert_in, "dp", axis=1, tiled=True)
    exo_full = lax.all_gather(expert_out, "dp", axis=1, tiled=True)

    down = down_in.swapaxes(2, 3).reshape(5, CODE, width)
    down_hid = down_hidden.swapaxes(1, 2).reshape(CODE, hidden)
    up_hid = up_hidden.reshape(CODE, hidden)
    up_out = up_attn_out.reshape(CODE, width)
    up_exo = up_expert_out.reshape(CODE, width)
    router = jnp.pad(jnp.tile(router_weight.T, (2, 1)), ((0, 128 - 2 * EXPERTS), (0, 0)))
    router_up = up_router.transpose(2, 0, 1).reshape(EXPERTS, CODE)
    router_up = jnp.pad(jnp.tile(router_up, (2, 1)), ((0, 128 - 2 * EXPERTS), (0, 0)))

    spare = ROWS - SEQ
    route_row = jnp.pad(
        routes.T.reshape(2, group_images, SEQ), ((0, 0), (0, 0), (0, spare)), constant_values=-1
    ).reshape(2, tall)
    rank_row = jnp.pad(
        priority.reshape(group_images, SEQ), ((0, 0), (0, spare)), constant_values=1 << 20
    ).reshape(1, tall)
    dy, pos_row, pos_col = call(
        route_kernel,
        (
            like((count, width), BF16),
            like((2 * EXPERTS, tall), F32),
            like((tall, 2 * EXPERTS), F32),
        ),
        scratch=[pltpu.VMEM((count, width), F32)],
    )(cotangent, route_row, route_row.T, rank_row, rank_row.T)
    dy_four = gather_four(dy)

    (
        weights, x, normed, code, qkv, prob, mixed, hcode, middle, normed2,
    ) = call(
        forward_kernel,
        (
            like((5, width, width), BF16),
            like((count, width), F32),
            like((count, width), BF16),
            like((count, 3 * CODE), BF16),
            like((count, 3 * width), BF16),
            like((images * HEADS, ROWS, ROWS), F32),
            like((count, width), BF16),
            like((count, CODE), BF16),
            like((count, width), F32),
            like((count, width), BF16),
        ),
        scratch=[pltpu.VMEM((count, width), F32)],
        smem=1,
    )(adapter_index, tokens, norm_gain, *four, down, up_out)

    normed2_four = gather_four(normed2)
    row_wide = 2 * width + 256
    whole = lambda *shape: pl.BlockSpec(shape, lambda step: (0,) * len(shape))
    smem = pl.BlockSpec(memory_space=pltpu.SMEM)
    slots, rows, rcode, probs = call(
        dispatch_kernel,
        (
            like((EXPERTS, SLOTS, row_wide), BF16),
            like((tall, row_wide), BF16),
            like((tall, CODE), BF16),
            like((tall, 128), F32),
        ),
        grid=(EXPERTS,),
        in_specs=[smem]
        + [whole(count, width)] * 8
        + [
            whole(2 * EXPERTS, tall),
            whole(5, CODE, width),
            whole(128, width),
            whole(128, CODE),
        ],
        out_specs=(
            pl.BlockSpec((1, SLOTS, row_wide), lambda step: (step, 0, 0)),
            whole(tall, row_wide),
            whole(tall, CODE),
            whole(tall, 128),
        ),
    )(adapter_index, *normed2_four, *dy_four, pos_row, down, router, router_up)

    half = like((2, count, width), BF16)
    small = like((CODE, width), F32)
    each = lambda *shape: pl.BlockSpec((1,) + shape, lambda step: (step, 0, 0))
    (
        mix_keep, mix_send, grad_keep, grad_send,
        g_up_hid, g_down_hid, g_up_exo, g_down3, g_down4, g_router,
    ) = call(
        expert_kernel,
        (
            half, half, half, half,
            like((CODE, hidden), F32), like((CODE, hidden), F32), small, small, small,
            like((CODE, 128), F32),
        ),
        scratch=[pltpu.VMEM((tall, 2 * width + 128), F32)],
        grid=(EXPERTS,),
        in_specs=[
            each(SLOTS, row_wide),
            each(width, hidden),
            each(width, hidden),
            whole(CODE, hidden),
            whole(CODE, hidden),
            whole(CODE, width),
            whole(5, CODE, width),
            whole(tall, row_wide),
            whole(tall, CODE),
            whole(tall, 128),
            whole(tall, 2 * EXPERTS),
            whole(128, width),
            whole(128, CODE),
            smem,
        ],
        out_specs=(
            whole(2, count, width), whole(2, count, width),
            whole(2, count, width), whole(2, count, width),
            whole(CODE, hidden), whole(CODE, hidden), whole(CODE, width),
            whole(CODE, width), whole(CODE, width), whole(CODE, 128),
        ),
    )(
        slots, in_full, exo_full, up_hid, down_hid, up_exo, down,
        rows, rcode, probs, pos_col, router, router_up, adapter_index,
    )

    grad_a, grad_b = reduce_pair(grad_keep, grad_send)
    mix_a, mix_b = reduce_pair(mix_keep, mix_send)

    input_grad, g_up_out, g_down_heads, g_up_heads, g_down_qkv = call(
        backward_kernel,
        (
            like((local, width), F32), small, small,
            like((3, CODE, width), F32), like((3, CODE, width), F32),
        ),
        scratch=[
            pltpu.VMEM((ROWS, width), BF16),
            pltpu.VMEM((ROWS, 3 * width), BF16),
            pltpu.VMEM((2 * ROWS, width), F32),
        ],
        smem=1,
    )(
        adapter_index, dy, middle, grad_a, grad_b, norm_gain, weights, down, up_out,
        x, normed, code, qkv, prob, mixed, hcode,
    )
    block_out = call(
        finish_kernel,
        like((local, width), F32),
        scratch=[pltpu.VMEM((ROWS, width), F32)],
    )(middle, mix_a, mix_b)

    both = ("dp", "tensor")
    parts = dp * tensor
    router_rows = g_router[:, :EXPERTS] + g_router[:, EXPERTS : 2 * EXPERTS]
    shared = jnp.concatenate(
        [
            g_down_qkv.reshape(-1),
            g_down3.reshape(-1),
            g_down4.reshape(-1),
            g_up_out.reshape(-1),
            g_up_exo.reshape(-1),
            router_rows.reshape(-1),
        ]
    ).astype(BF16)
    length = shared.shape[0]
    piece = -(-length // (parts * 1024)) * 1024
    shared = jnp.pad(shared, (0, parts * piece - length)).reshape(parts, piece)
    shared = sum_all(shared, both).astype(BF16)
    shared = lax.all_gather(shared, both, axis=0, tiled=True).astype(F32)
    size = CODE * width
    as_down = lambda flat: flat.reshape(-1, ADAPTERS, RANK, width).swapaxes(2, 3)
    grad_down_in = as_down(shared[: 5 * size])
    grad_up_out = shared[5 * size : 6 * size].reshape(ADAPTERS, RANK, width)
    grad_up_exo = shared[6 * size : 7 * size].reshape(ADAPTERS, RANK, width)
    grad_up_router = shared[7 * size : 7 * size + CODE * EXPERTS].reshape(
        ADAPTERS, RANK, EXPERTS
    )

    cols = width // tensor
    heads = jnp.concatenate([g_up_heads.reshape(3 * CODE, width), g_down_heads], 0)
    heads = heads.astype(BF16).reshape(dp, 4 * CODE // dp, tensor, cols)
    heads = heads.transpose(0, 2, 1, 3).reshape(parts, 4 * CODE // dp, cols)
    heads = sum_all(heads, both).astype(BF16)
    hid = jnp.concatenate([g_up_hid, g_down_hid], 0).astype(BF16)
    hid = sum_all(hid.reshape(dp, 2 * CODE // dp, hidden), "dp").astype(BF16)
    split = jnp.concatenate([heads.reshape(-1), hid.reshape(-1)])
    split = lax.all_gather(split, "dp", axis=0).astype(F32)
    first = heads.size
    heads = split[:, :first].reshape(4 * CODE, cols)
    hid = split[:, first:].reshape(2 * CODE, hidden)
    grad_up_heads = heads[: 3 * CODE].reshape(3, ADAPTERS, RANK, cols)
    grad_down_heads = heads[3 * CODE :].reshape(ADAPTERS, RANK, cols).swapaxes(1, 2)
    grad_up_hidden = hid[:CODE].reshape(ADAPTERS, RANK, hidden)
    grad_down_hidden = hid[CODE:].reshape(ADAPTERS, RANK, hidden).swapaxes(1, 2)
    return (
        block_out,
        input_grad,
        grad_down_in,
        grad_up_heads,
        grad_up_hidden,
        grad_up_router,
        grad_down_heads,
        grad_down_hidden,
        grad_up_out,
        grad_up_exo,
    )


def solution(mesh):
    placed = (
        P(("dp", "tensor"), None),
        P(("dp", "tensor"), None),
        P(),
        P(None, "dp", "tensor"),
        P("dp", "tensor"),
        P(None, "dp", "tensor"),
        P(None, "dp", "tensor"),
        P(),
        P(),
        P(None, None, None, "tensor"),
        P(None, None, "tensor"),
        P(),
        P(None, "tensor", None),
        P(None, "tensor", None),
        P(),
        P(),
        P("dp", None),
        P("dp", None),
        P("dp"),
    )
    return jax.shard_map(
        per_device,
        mesh=mesh,
        in_specs=placed,
        out_specs=(
            P(("dp", "tensor"), None),
            P(("dp", "tensor"), None),
            P(),
            P(None, None, None, "tensor"),
            P(None, None, "tensor"),
            P(),
            P(None, "tensor", None),
            P(None, "tensor", None),
            P(),
            P(),
        ),
        check_vma=False,
    )
```

```python
from functools import partial

import jax
import jax.numpy as jnp
from jax import lax
from jax.experimental import pallas as pl
from jax.experimental.pallas import tpu as pltpu
from jax.sharding import PartitionSpec as P

HEADS = 8
RANK = 16
ADAPTERS = 8
SEQ = 197
EXPERTS = 8
HEAD_DIM = 64
CAP = 394

EPS = 1e-06
CODE = ADAPTERS * RANK
ROWS = 208
UNIT = 16
SCALE = HEAD_DIM ** (-0.5)
F32 = jnp.float32
BF16 = jnp.bfloat16
VMEM_LIMIT = 56 * 1024 * 1024


def dot(left, right):
    return lax.dot_general(left, right, (((1,), (0,)), ((), ())), preferred_element_type=F32)


def dot_t(left, right):
    return lax.dot_general(left, right, (((1,), (1,)), ((), ())), preferred_element_type=F32)


def tdot(left, right):
    return lax.dot_general(left, right, (((0,), (0,)), ((), ())), preferred_element_type=F32)


def lanes(shape):
    return lax.broadcasted_iota(jnp.int32, shape, len(shape) - 1)


def sublanes(shape):
    return lax.broadcasted_iota(jnp.int32, shape, len(shape) - 2)


def norm_rows(value, gain):
    center = value - jnp.mean(value, -1, keepdims=True)
    spread = jnp.mean(center * center, -1, keepdims=True)
    return center * lax.rsqrt(spread + EPS) * gain


def norm_back(value, gain, grad):
    center = value - jnp.mean(value, -1, keepdims=True)
    rate = lax.rsqrt(jnp.mean(center * center, -1, keepdims=True) + EPS)
    unit = center * rate
    grad = grad * gain
    along = jnp.mean(grad * unit, -1, keepdims=True)
    return rate * (grad - jnp.mean(grad, -1, keepdims=True) - unit * along)


def gelu_pair(value):
    square = value * value
    inner = 0.7978845608028654 * value * (1.0 + 0.044715 * square)
    bent = jnp.tanh(inner)
    half = 0.5 * (1.0 + bent)
    slope = half + 0.5 * value * (1.0 - bent * bent) * (
        0.7978845608028654 * (1.0 + 3.0 * 0.044715 * square)
    )
    return value * half, slope


def call(body, outs, scratch=(), smem=0, grid=None, in_specs=None, out_specs=None, cost=None):
    options = {}
    if grid is not None:
        options = dict(grid=grid, in_specs=in_specs, out_specs=out_specs)
    elif smem:
        def build(*args):
            specs = [pl.BlockSpec(memory_space=pltpu.SMEM)] * smem
            specs += [pl.BlockSpec(memory_space=pltpu.VMEM)] * (len(args) - smem)
            return call(body, outs, scratch, 0, (), specs, None, cost)(*args)

        return build
    if grid == ():
        options = dict(in_specs=in_specs)
    return pl.pallas_call(
        body,
        out_shape=outs,
        scratch_shapes=list(scratch),
        compiler_params=pltpu.CompilerParams(vmem_limit_bytes=VMEM_LIMIT),
        cost_estimate=cost,
        **options,
    )


def like(shape, dtype):
    return jax.ShapeDtypeStruct(shape, dtype)


def cost(micros):
    return pl.CostEstimate(
        flops=int(micros * 1.1e9), bytes_accessed=int(micros * 3.6e6), transcendentals=0
    )


def image_mask(adapter, index):
    return jnp.where(lanes((1, CODE)) // RANK == adapter[index], 1.0, 0.0)


def route_kernel(cot, rflat, rrow, prow, pcol, dy, place_out, table_out, wide):
    images = dy.shape[0] // ROWS
    chunks, unused, count = rrow.shape
    wide[...] = jnp.zeros_like(wide)
    wide[0 : cot.shape[0], :] = cot[...].astype(F32)
    for image in range(images):
        part = wide[image * SEQ : image * SEQ + ROWS, :]
        part = jnp.where(sublanes((ROWS, 1)) < SEQ, part, 0.0)
        dy[image * ROWS : (image + 1) * ROWS, :] = part.astype(BF16)
    kinds = sublanes((2 * EXPERTS, rflat.shape[1]))
    first = jnp.where(rflat[0:1, :] == kinds, 1.0, 0.0)
    second = jnp.where(rflat[1:2, :] == kinds, 1.0, 0.0)
    first_all = jnp.sum(first, axis=1, keepdims=True)
    first = first.astype(BF16)
    second = second.astype(BF16)
    kinds = sublanes((2 * EXPERTS, count))
    above = jnp.where(sublanes((count, count)) < lanes((count, count)), 1.0, 0.0).astype(BF16)
    square = (2 * EXPERTS, 2 * EXPERTS)
    below = jnp.where(lanes(square) < sublanes(square), 1.0, 0.0).astype(BF16)
    lane = lanes((2 * EXPERTS, 128))
    table = jnp.zeros((2 * EXPERTS, 128), F32)
    filled = jnp.zeros((2 * EXPERTS, 1), F32)
    for chunk in range(chunks):
        earlier = jnp.where(pcol[...] < prow[chunk], 1.0, 0.0).astype(BF16)
        is_first = rrow[chunk, 0:1, :] == kinds
        is_second = rrow[chunk, 1:2, :] == kinds
        place = jnp.where(is_first, dot(first, earlier), 1e9)
        place = jnp.where(is_second, dot(second, earlier) + first_all, place)
        kept = place < CAP
        held = jnp.where(kept, 1.0, 0.0)
        rank = dot(held.astype(BF16), above)
        units = jnp.sum(held, axis=1, keepdims=True)
        units = jnp.floor((units + (UNIT - 1)) * (1.0 / UNIT))
        start = dot(below, jnp.broadcast_to(units, (2 * EXPERTS, 128)).astype(BF16))[:, 0:1]
        spot = jnp.where(kept, start * UNIT + rank + 1.0, 0.0)
        place_out[chunk, 0:1, :] = (
            jnp.sum(jnp.where(is_first, spot, 0.0), axis=0, keepdims=True) - 1.0
        )
        place_out[chunk, 1:2, :] = (
            jnp.sum(jnp.where(is_second, spot, 0.0), axis=0, keepdims=True) - 1.0
        )
        table = jnp.where(lane == chunk, units, table)
        table = jnp.where(lane == chunks + chunk, start, table)
        table = jnp.where(lane == 2 * chunks + chunk, filled, table)
        filled = filled + units
    table = jnp.where(lane == 3 * chunks, filled, table)
    table_out[...] = table.astype(jnp.int32)


def assemble_kernel(count, *refs):
    parts, out, ids = refs[:count], refs[count], refs[count + 1]
    me = lax.axis_index("dp")
    feats = out.shape[2] // count
    for step in range(count):
        owner = lax.rem(me - step + count, count)
        rows = pl.ds(pl.multiple_of(owner * feats, feats), feats)
        for side in range(2):
            for member in range(4):
                out[side, member, rows, :] = parts[step][
                    side, member * feats : (member + 1) * feats, :
                ]
        ids[owner] = parts[step][0, 4 * feats : 4 * feats + 16, :]


def forward_kernel(
    adapter, tokens, gain, mine, other, own, core, side, both, down, up_out,
    weights, x_out, normed_out, code_out, qkv_out, prob_out, mixed_out, hcode_out,
    middle_out, normed2_out, wide,
):
    me = lax.axis_index("tensor")
    for step, part in enumerate((own, core, side, both)):
        cols = pl.ds(pl.multiple_of(lax.bitwise_xor(me, step) * 128, 128), 128)
        weights[4, :, cols] = part[...]
        weights[0:4, :, cols] = (mine, other)[step % 2][step // 2]
    images = x_out.shape[0] // ROWS
    width = tokens.shape[1]
    wide[...] = jnp.zeros_like(wide)
    wide[0 : tokens.shape[0], :] = tokens[...].astype(F32)
    for image in range(images):
        at = image * ROWS
        rows = slice(at, at + ROWS)
        mask = image_mask(adapter, me * images + image)
        real = sublanes((ROWS, 1)) < SEQ
        x = jnp.where(real, wide[image * SEQ : image * SEQ + ROWS, :], 0.0)
        x_out[rows, :] = x
        normed = norm_rows(x, gain[0:1, :]).astype(BF16)
        normed_out[rows, :] = normed
        for member in range(3):
            code = (mask * dot_t(normed, down[member])).astype(BF16)
            code_out[rows, member * CODE : (member + 1) * CODE] = code
            up = weights[4, member * CODE : (member + 1) * CODE, :]
            proj = dot(normed, weights[member]) + dot(code, up)
            qkv_out[rows, member * width : (member + 1) * width] = proj.astype(BF16)
        low_half = lanes((1, 128)) < HEAD_DIM
        half = (low_half, jnp.logical_not(low_half))
        real_key = lanes((1, ROWS)) < SEQ
        for pair in range(HEADS // 2):
            cols = pair * 128
            q = qkv_out[rows, cols : cols + 128].astype(F32) * SCALE
            k = qkv_out[rows, width + cols : width + cols + 128]
            v = qkv_out[rows, 2 * width + cols : 2 * width + cols + 128].astype(F32)
            mixed = jnp.zeros((ROWS, 128), F32)
            for head in range(2):
                score = dot_t(jnp.where(half[head], q, 0.0).astype(BF16), k)
                score = jnp.where(real_key, score, -1e30)
                raised = jnp.exp(score - jnp.max(score, -1, keepdims=True))
                prob = raised / jnp.sum(raised, -1, keepdims=True)
                prob_out[(image * HEADS // 2 + pair) * 2 + head] = prob
                mixed = mixed + dot(
                    prob.astype(BF16), jnp.where(half[head], v, 0.0).astype(BF16)
                )
            mixed_out[rows, cols : cols + 128] = mixed.astype(BF16)
        mixed = mixed_out[rows, :]
        hcode = (mask * dot_t(mixed, weights[4, 3 * CODE : 4 * CODE, :])).astype(BF16)
        hcode_out[rows, :] = hcode
        middle = x + dot_t(mixed, weights[3]) + dot(hcode, up_out[...])
        middle_out[rows, :] = middle
        normed2_out[rows, :] = norm_rows(middle, gain[1:2, :]).astype(BF16)


def move_units(table, chunk, expert, chunk_ref, expert_ref, forward):
    start = table[expert, 4 + chunk]
    target = table[expert, 8 + chunk]

    def move(unit, carry):
        here = pl.ds(pl.multiple_of((start + unit) * UNIT, UNIT), UNIT)
        there = pl.ds(pl.multiple_of((target + unit) * UNIT, UNIT), UNIT)
        if forward:
            expert_ref[there, :] = chunk_ref[here, :]
        else:
            chunk_ref[here, :] = expert_ref[there, :]
        return carry

    lax.fori_loop(0, table[expert, chunk], move, 0)


def clear_units(ref, start):
    def clear(unit, carry):
        rows = pl.ds(pl.multiple_of(unit * UNIT, UNIT), UNIT)
        ref[rows, :] = jnp.zeros((UNIT, ref.shape[1]), ref.dtype)
        return carry

    lax.fori_loop(start, ref.shape[0] // UNIT, clear, 0)


def dispatch_kernel(
    adapter, table, own, core, side, both, dy_own, dy_core, dy_side, dy_both,
    place, down, router, up_router,
    slots, normed_out, rcode_out, prob_out, rows, packed,
):
    me = lax.axis_index("tensor")
    count = own.shape[0]
    images = count // ROWS
    width = own.shape[1]
    lane = lanes((1, 128))
    for index, (part, dy) in enumerate(
        ((own, dy_own), (core, dy_core), (side, dy_side), (both, dy_both))
    ):
        chunk = lax.bitwise_xor(me, index)
        normed_out[index] = part[...]
        rows[:, 0:width] = part[...]
        rows[:, width : 2 * width] = dy[...]
        for image in range(images):
            which = adapter[chunk * images + image]
            mask = jnp.where(lane // RANK == which, 1.0, 0.0)
            local = slice(image * ROWS, (image + 1) * ROWS)
            normed = part[local, :]
            rcode = (mask * dot_t(normed, down[4])).astype(BF16)
            rcode_out[index, local, :] = rcode
            logits = dot_t(normed, router[...]) + dot_t(rcode, up_router[...])
            logits = jnp.where(lane < 2 * EXPERTS, logits, -1e30)
            raised = jnp.exp(logits - jnp.max(logits, -1, keepdims=True))
            mass = jnp.sum(jnp.where(lane < EXPERTS, raised, 0.0), -1, keepdims=True)
            prob = raised / mass
            prob_out[index, local, :] = prob
            high = prob.astype(BF16).astype(F32)
            aux = jnp.where(lane < EXPERTS, high, prob - high)
            aux = jnp.where(lane < 2 * EXPERTS, aux, jnp.where(lane == 16 + which, 1.0, 0.0))
            rows[local, 2 * width : 2 * width + 128] = aux.astype(BF16)
        spot = sublanes((packed.shape[0], count)).astype(F32)
        chosen = jnp.logical_or(spot == place[chunk, 0:1, :], spot == place[chunk, 1:2, :])
        chosen = jnp.where(chosen, 1.0, 0.0).astype(BF16)
        packed[...] = dot(chosen, rows[...]).astype(BF16)
        for expert in range(EXPERTS):
            move_units(table, chunk, expert, packed, slots.at[expert], True)
    for expert in range(EXPERTS):
        clear_units(slots.at[expert], table[expert, 12])


def expert_body(expert, slots, w_in, w_out, up_hid, down_hid, up_exo, down, g_hid, g_exo, out):
    width = w_in.shape[0]
    lane = lanes((1, 128))
    x = slots[:, 0:width]
    dy = slots[:, width : 2 * width].astype(F32)
    aux = slots[:, 2 * width : 2 * width + 128]
    expand = jnp.where(sublanes((128, CODE)) - 16 == lanes((128, CODE)) // RANK, 1.0, 0.0)
    mask = dot(aux, expand.astype(BF16))
    here = jnp.logical_and(lax.rem(lane, EXPERTS) == expert, lane < 2 * EXPERTS)
    gate = jnp.sum(jnp.where(here, aux.astype(F32), 0.0), -1, keepdims=True)
    hcode = (mask * dot_t(x, down[3])).astype(BF16)
    before = dot(x, w_in[...]) + dot(hcode, up_hid[...])
    active, slope = gelu_pair(before)
    active = active.astype(BF16)
    ocode = (mask * dot_t(active, down_hid[...])).astype(BF16)
    returned = dot_t(active, w_out[...]) + dot(ocode, up_exo[...])
    gate_grad = jnp.sum(returned * dy, -1, keepdims=True)
    back = (gate * dy).astype(BF16)
    ocode_grad = (mask * dot_t(back, up_exo[...])).astype(BF16)
    active_grad = dot(back, w_out[...]) + dot(ocode_grad, down_hid[...])
    before_grad = (slope * active_grad).astype(BF16)
    hcode_grad = (mask * dot_t(before_grad, up_hid[...])).astype(BF16)
    x_grad = dot_t(before_grad, w_in[...]) + dot(hcode_grad, down[3])
    g_hid[0] += tdot(hcode, before_grad)
    g_hid[1] += tdot(ocode_grad, active)
    g_exo[0] += tdot(hcode_grad, x)
    g_exo[1] += tdot(ocode, back)
    high = gate_grad.astype(BF16).astype(F32)
    spread = jnp.where(here, jnp.where(lane < EXPERTS, high, gate_grad - high), 0.0)
    out[:, 0:width] = (gate * returned).astype(BF16)
    out[:, width : 2 * width] = x_grad.astype(BF16)
    out[:, 2 * width : 2 * width + 128] = spread.astype(BF16)


def join_weights(parts, owners, target):
    feats = parts[0].shape[2]
    for part, owner in zip(parts, owners):
        rows = pl.ds(pl.multiple_of(owner * feats, feats), feats)
        for kind in range(2):
            target[kind, rows, :] = part[kind, 0]


def weight_owners(size):
    me = lax.axis_index("dp")
    if size == 1:
        return (0,)
    owners = []
    for step in range(size // 2):
        owner = lax.rem(me - 2 * step + size, size)
        owners += [owner, lax.bitwise_xor(owner, 1)]
    return owners


def early_kernel(size, *refs):
    parts, (slots, up_hid, down_hid, up_exo, down, out, g_hid, g_exo, joined) = (
        refs[:size], refs[size:],
    )
    step = pl.program_id(0)

    @pl.when(step == 0)
    def _():
        g_hid[...] = jnp.zeros_like(g_hid)
        g_exo[...] = jnp.zeros_like(g_exo)

    join_weights(parts, weight_owners(size), joined)
    expert_body(
        step, slots.at[0], joined.at[0], joined.at[1], up_hid, down_hid, up_exo, down,
        g_hid, g_exo, out.at[0],
    )


def late_kernel(size, base, *refs):
    parts, refs = refs[:size], refs[size:]
    (
        slots, up_hid, down_hid, up_exo, down, before, g_hid_before, g_exo_before,
        adapter, table, normed, rcode, prob, place, router, up_router,
        mix_keep, mix_send, grad_keep, grad_send, grads_out,
        joined, late, g_hid, g_exo, g_router, packed,
    ) = refs
    step = pl.program_id(0)
    width = down.shape[2]
    lane = lanes((1, 128))

    @pl.when(step == 0)
    def _():
        g_hid[...] = g_hid_before[...]
        g_exo[...] = g_exo_before[...]
        g_router[...] = jnp.zeros_like(g_router)

    join_weights(parts, weight_owners(size), joined)
    expert_body(
        step + base, slots.at[0], joined.at[0], joined.at[1], up_hid, down_hid, up_exo, down,
        g_hid, g_exo, late.at[step],
    )

    @pl.when(step == pl.num_programs(0) - 1)
    def _():
        me = lax.axis_index("tensor")
        count = mix_keep.shape[1]
        images = count // ROWS
        for index in range(4):
            chunk = lax.bitwise_xor(me, index)
            for expert in range(EXPERTS):
                source = before.at[expert] if expert < base else late.at[expert - base]
                move_units(table, chunk, expert, packed, source, False)
            ending = EXPERTS - 1
            clear_units(packed, table[ending, 4 + chunk] + table[ending, chunk])
            mix_out = (mix_keep, mix_send)[index % 2]
            grad_out = (grad_keep, grad_send)[index % 2]
            for image in range(images):
                local = slice(image * ROWS, (image + 1) * ROWS)
                spot = lanes((ROWS, packed.shape[0])).astype(F32)
                chosen = jnp.logical_or(
                    spot == place[chunk, local, 0:1], spot == place[chunk, local, 1:2]
                )
                total = dot(jnp.where(chosen, 1.0, 0.0).astype(BF16), packed[...])
                mask = image_mask(adapter, chunk * images + image)
                mix_out[index // 2, local, :] = total[:, 0:width].astype(BF16)
                gates = total[:, 2 * width : 2 * width + 128]
                probs = jnp.where(lane < 2 * EXPERTS, prob[index, local, :], 0.0)
                mean = jnp.sum(probs * gates, -1, keepdims=True)
                logit = (probs * (gates - jnp.where(lane < EXPERTS, mean, 0.0))).astype(BF16)
                rcode_grad = (mask * dot(logit, up_router[...])).astype(BF16)
                grad = total[:, width : 2 * width] + dot(logit, router[...])
                grad = grad + dot(rcode_grad, down[4])
                grad_out[index // 2, local, :] = grad.astype(BF16)
                g_router[0] += tdot(rcode_grad, normed[index, local, :])
                g_router[1, :, 0:128] += tdot(rcode[index, local, :], logit)
        shared = (g_exo.at[0], g_router.at[0], g_exo.at[1], g_router.at[1])
        if grads_out.dtype == F32:
            for member in range(4):
                grads_out[member] = shared[member][...]
            grads_out[4:6] = g_hid[...]
            return
        for owner in range(8):
            member, at = divmod(owner * 64, CODE)
            grads_out[owner, 0:64, :] = shared[member][at : at + 64, :].astype(BF16)
            member, at = divmod(owner * 32, CODE)
            grads_out[owner, 64:96, :] = g_hid[member, at : at + 32, :].astype(BF16)


def backward_kernel(
    adapter, dy, middle, grad_a, grad_b, gain, weights, up_out,
    normed_in, code_in, qkv_in, prob_in, mixed_in, hcode_in,
    middle_grad_out, proj_grad, code_grad_out, grads_out, mixed_grad, whole,
):
    me = lax.axis_index("tensor")
    images = dy.shape[0] // ROWS
    width = dy.shape[1]
    compact = grads_out.shape[0] == 32

    def keep(image, member, grad):
        if not compact:
            grads_out[member] = grad if image == 0 else grads_out[member] + grad
            return
        whole[member] = grad
        start = pl.multiple_of(adapter[me * images + image] * RANK, RANK)
        rows = whole[member, pl.ds(start, RANK), :].astype(BF16)
        for block in range(4):
            grads_out[member * 4 + block, image * RANK : (image + 1) * RANK, :] = rows[
                :, block * 128 : (block + 1) * 128
            ]

    for image in range(images):
        at = image * ROWS
        rows = slice(at, at + ROWS)
        mask = image_mask(adapter, me * images + image)
        summed = grad_a[rows, :].astype(F32) + grad_b[rows, :].astype(F32)
        middle_grad = dy[rows, :].astype(F32) + norm_back(
            middle[rows, :], gain[1:2, :], summed
        )
        middle_grad_out[rows, :] = middle_grad
        low = middle_grad.astype(BF16)
        hcode_grad = (mask * dot_t(low, up_out[...])).astype(BF16)
        down_heads = weights[4, 3 * CODE : 4 * CODE, :]
        mixed_grad[...] = (dot(low, weights[3]) + dot(hcode_grad, down_heads)).astype(BF16)
        keep(image, 7, tdot(hcode_in[rows, :], low))
        keep(image, 3, tdot(hcode_grad, mixed_in[rows, :]))
        low_half = lanes((1, 128)) < HEAD_DIM
        half = (low_half, jnp.logical_not(low_half))
        for pair in range(HEADS // 2):
            cols = pair * 128
            q = qkv_in[rows, cols : cols + 128].astype(F32) * SCALE
            k = qkv_in[rows, width + cols : width + cols + 128].astype(F32) * SCALE
            v = qkv_in[rows, 2 * width + cols : 2 * width + cols + 128]
            m = mixed_grad[:, cols : cols + 128].astype(F32)
            q_grad = jnp.zeros((ROWS, 128), F32)
            k_grad = jnp.zeros((ROWS, 128), F32)
            v_grad = jnp.zeros((ROWS, 128), F32)
            for head in range(2):
                prob = prob_in[(image * HEADS // 2 + pair) * 2 + head]
                m_head = jnp.where(half[head], m, 0.0).astype(BF16)
                v_grad = v_grad + tdot(prob.astype(BF16), m_head)
                weight_grad = dot_t(m_head, v)
                along = jnp.sum(prob * weight_grad, -1, keepdims=True)
                score = (prob * (weight_grad - along)).astype(BF16)
                q_grad = q_grad + dot(score, jnp.where(half[head], k, 0.0).astype(BF16))
                k_grad = k_grad + tdot(score, jnp.where(half[head], q, 0.0).astype(BF16))
            proj_grad[rows, cols : cols + 128] = q_grad.astype(BF16)
            proj_grad[rows, width + cols : width + cols + 128] = k_grad.astype(BF16)
            proj_grad[rows, 2 * width + cols : 2 * width + cols + 128] = v_grad.astype(BF16)
        normed = normed_in[rows, :]
        for member in range(3):
            grad = proj_grad[rows, member * width : (member + 1) * width]
            up = weights[4, member * CODE : (member + 1) * CODE, :]
            code_grad = (mask * dot_t(grad, up)).astype(BF16)
            code_grad_out[rows, member * CODE : (member + 1) * CODE] = code_grad
            code = code_in[rows, member * CODE : (member + 1) * CODE]
            keep(image, member, tdot(code, grad))
            keep(image, 4 + member, tdot(code_grad, normed))


def early_sum_kernel(came, keep, send, hid):
    me = lax.axis_index("tensor")
    for index in range(4):
        start = pl.multiple_of(lax.bitwise_xor(me, index) * 16, 16)
        total = came[0, pl.ds(start, 16), :].astype(F32)
        for owner in range(1, came.shape[0]):
            total = total + came[owner, pl.ds(start, 16), :].astype(F32)
        (keep, send)[index % 2][index // 2] = total.astype(BF16)
    total = came[0, 64:96, :].astype(F32)
    for owner in range(1, came.shape[0]):
        total = total + came[owner, 64:96, :].astype(F32)
    hid[...] = total.astype(BF16)


def late_sum_kernel(came, ids, hid, rows_a, rows_b, out):
    square = (CODE, CODE)
    total = jnp.zeros(square, F32)
    same = lax.rem(sublanes(square), RANK) == lax.rem(lanes(square), RANK)
    kind = (sublanes(square) // RANK).astype(F32)
    for owner in range(ids.shape[0]):
        chosen = jnp.logical_and(same, kind == ids[owner, 0:1, :].astype(F32))
        total = total + dot(jnp.where(chosen, 1.0, 0.0).astype(BF16), came[owner])
    total = total.astype(BF16)
    rows = (rows_a[...].astype(F32) + rows_b[...].astype(F32)).astype(BF16)
    for owner in range(out.shape[0]):
        out[owner, 0:32, :] = hid[...]
        out[owner, 32:48, :] = rows
        for slab in range(4):
            out[owner, 48:80, slab * 128 : (slab + 1) * 128] = total[
                slab * 32 : (slab + 1) * 32, :
            ]


def unpack_kernel(
    came, own, core, side, both, down_in, up_out, up_exo, router, heads, hid
):
    me = lax.axis_index("tensor")
    for owner in range(8):
        member, at = divmod(owner * 32, CODE)
        hid[member, at : at + 32, :] = came[owner, 0:32, :].astype(F32)
    for member in range(4):
        for slab in range(4):
            heads[member, slab * 32 : (slab + 1) * 32, :] = came[
                member, 48:80, slab * 128 : (slab + 1) * 128
            ].astype(F32)
    late = (down_in.at[0], down_in.at[1], down_in.at[2], up_out)
    early = (down_in.at[3], down_in.at[4], up_exo, router)
    for index, part in enumerate((own, core, side, both)):
        spot = lax.bitwise_xor(me, index)
        cols = pl.ds(pl.multiple_of(spot * 128, 128), 128)
        for member in range(4):
            for slab in range(4):
                late[member][slab * 32 : (slab + 1) * 32, cols] = part[
                    member * 32 : (member + 1) * 32, slab * 128 : (slab + 1) * 128
                ].astype(F32)
        for owner in range(8):
            rows = pl.ds(pl.multiple_of((owner % 2) * 64 + spot * 16, 16), 16)
            early[owner // 2][rows, :] = part[
                128 + owner * 16 : 144 + owner * 16, :
            ].astype(F32)


def input_kernel(
    middle_grad, proj_grad, code_grad, x_in, gain, weights, down, input_grad, wide
):
    images = middle_grad.shape[0] // ROWS
    width = middle_grad.shape[1]
    for image in range(images):
        at = image * ROWS
        rows = slice(at, at + ROWS)
        normed_grad = jnp.zeros((ROWS, width), F32)
        for member in range(3):
            grad = proj_grad[rows, member * width : (member + 1) * width]
            normed_grad = normed_grad + dot_t(grad, weights[member])
            code = code_grad[rows, member * CODE : (member + 1) * CODE]
            normed_grad = normed_grad + dot(code, down[member])
        wide[...] = middle_grad[rows, :] + norm_back(x_in[rows, :], gain[0:1, :], normed_grad)
        input_grad[image * SEQ : (image + 1) * SEQ, :] = wide[0:SEQ, :]


def finish_kernel(middle, part_a, part_b, out, wide):
    images = middle.shape[0] // ROWS
    for image in range(images):
        rows = slice(image * ROWS, (image + 1) * ROWS)
        wide[...] = (
            middle[rows, :] + part_a[rows, :].astype(F32) + part_b[rows, :].astype(F32)
        )
        out[image * SEQ : (image + 1) * SEQ, :] = wide[0:SEQ, :]


def swap(value, bit):
    size = lax.axis_size("tensor")
    return lax.ppermute(value, "tensor", [(at, at ^ bit) for at in range(size)])


def gather_four(value):
    core = swap(value, 1)
    side = swap(value, 2)
    return value, core, side, swap(side, 1)


def after(value, *others):
    return lax.optimization_barrier((value,) + others)[0]


def reduce_pair(keep, send):
    came = swap(send, 1)
    mine = keep[0].astype(F32) + came[0].astype(F32)
    other = (keep[1].astype(F32) + came[1].astype(F32)).astype(BF16)
    return mine.astype(BF16), swap(other, 2)


def gather_projections(shards, ids, others):
    size = lax.axis_size("dp")
    feats = shards.shape[1]
    if size == 8 and feats % 16 == 0:
        block = jnp.concatenate([shards.reshape(-1, 128), ids], 0)
        block = jnp.stack([block, swap(block, 2)])
        parts = [block]
        for step in range(1, size):
            parts.append(
                lax.ppermute(block, "dp", [(at, (at + step) % size) for at in range(size)])
            )
        parts[-1] = after(parts[-1], *others)
        return call(
            partial(assemble_kernel, size),
            (like((2, 4, size * feats, 128), BF16), like((size,) + ids.shape, BF16)),
            cost=cost(2),
        )(*parts)
    whole = lax.all_gather(shards, "dp", axis=1, tiled=True)
    return jnp.stack([whole, swap(whole, 2)]), ids[None]


def gather_experts(first, second):
    size = lax.axis_size("dp")
    if size != 8 or first.shape[2] % 16:
        whole = lambda block: [lax.all_gather(block, "dp", axis=2, tiled=True)]
        return whole(first), whole(second), [()] * 4
    ring = [(at, (at + 2) % size) for at in range(size)]
    pairs = [(at, at ^ 1) for at in range(size)]
    steps = size // 2

    def stage(block, here, parts):
        passed = lax.ppermute(block, "dp", ring) if here < steps - 1 else None
        crossed = lax.ppermute(block, "dp", pairs)
        parts += [block, crossed]
        if passed is None:
            return None, (crossed,)
        return after(passed, crossed), (passed, crossed)

    parts, stages = ([], []), []
    blocks = [first, second]
    done = ()
    for slot in range(steps + 1):
        fresh = ()
        for which in range(2):
            here = slot - which
            if 0 <= here < steps:
                if which == 1 and here == 0:
                    blocks[1] = after(second, *done)
                blocks[which], came = stage(blocks[which], here, parts[which])
                fresh += came
        done = fresh
        stages.append(done)
    return parts[0], parts[1], stages


def per_device(
    tokens,
    cotangent,
    norm_gain,
    qkv_weight,
    out_weight,
    expert_in,
    expert_out,
    router_weight,
    down_in,
    up_heads,
    up_hidden,
    up_router,
    down_heads,
    down_hidden,
    up_attn_out,
    up_expert_out,
    routes,
    priority,
    adapter_index,
):
    width = tokens.shape[1]
    local = tokens.shape[0]
    images = local // SEQ
    group_images = routes.shape[0] // SEQ
    count = images * ROWS
    tall = group_images * ROWS
    hidden = expert_in.shape[2]
    dp = lax.axis_size("dp")
    tensor = lax.axis_size("tensor")

    block = jnp.concatenate([qkv_weight, out_weight[None]], 0)
    ids = jnp.repeat(adapter_index.astype(BF16), CODE // adapter_index.shape[0])
    ids = jnp.broadcast_to(ids[None], (16, CODE))
    extra = jnp.concatenate(
        [
            up_heads.reshape(3 * CODE, up_heads.shape[3]),
            down_heads.swapaxes(1, 2).reshape(CODE, down_heads.shape[1]),
        ],
        0,
    )
    base = EXPERTS // 2
    early_parts, late_parts, stages = gather_experts(
        jnp.stack([expert_in[:base], expert_out[:base]]),
        jnp.stack([expert_in[base:], expert_out[base:]]),
    )
    extras = gather_four(extra)

    down = down_in.swapaxes(2, 3).reshape(5, CODE, width)
    down_hid = down_hidden.swapaxes(1, 2).reshape(CODE, hidden)
    up_hid = up_hidden.reshape(CODE, hidden)
    up_out = up_attn_out.reshape(CODE, width)
    up_exo = up_expert_out.reshape(CODE, width)
    router = jnp.pad(jnp.tile(router_weight.T, (2, 1)), ((0, 128 - 2 * EXPERTS), (0, 0)))
    router_up = up_router.transpose(2, 0, 1).reshape(EXPERTS, CODE)
    router_up = jnp.pad(jnp.tile(router_up, (2, 1)), ((0, 128 - 2 * EXPERTS), (0, 0)))

    spare = ROWS - SEQ
    route_row = jnp.pad(
        routes.T.reshape(2, group_images, SEQ), ((0, 0), (0, 0), (0, spare)), constant_values=-1
    ).reshape(2, tall)
    rank_row = jnp.pad(
        priority.reshape(group_images, SEQ), ((0, 0), (0, spare)), constant_values=1 << 20
    ).reshape(1, tall)
    chunk_units = (2 * count + EXPERTS * (UNIT - 1)) // UNIT
    expert_units = -(-CAP // UNIT) + 4
    by_chunk = lambda value: value.reshape(-1, tensor, count).swapaxes(0, 1)
    dy, place, table = call(
        route_kernel,
        (
            like((count, width), BF16),
            like((tensor, 2, count), F32),
            like((2 * EXPERTS, 128), jnp.int32),
        ),
        scratch=[pltpu.VMEM((count, width), F32)],
        cost=cost(5),
    )(cotangent, route_row, by_chunk(route_row), by_chunk(rank_row), rank_row.T)
    dy_four = gather_four(dy)
    mine, ids = gather_projections(block, ids, (dy,) + stages[0])
    other = swap(mine, 1)

    (
        weights, x, normed, code, qkv, prob, mixed, hcode, middle, normed2,
    ) = call(
        forward_kernel,
        (
            like((5, width, width), BF16),
            like((count, width), F32),
            like((count, width), BF16),
            like((count, 3 * CODE), BF16),
            like((count, 3 * width), BF16),
            like((images * HEADS, ROWS, ROWS), F32),
            like((count, width), BF16),
            like((count, CODE), BF16),
            like((count, width), F32),
            like((count, width), BF16),
        ),
        scratch=[pltpu.VMEM((count, width), F32)],
        smem=1,
        cost=cost(10),
    )(adapter_index, tokens, norm_gain, after(mine, *stages[1]), other, *extras, down, up_out)

    normed2_four = gather_four(normed2)
    normed2_four = (after(normed2, *stages[2]),) + normed2_four[1:]
    row_wide = 2 * width + 128
    chunk_slots = chunk_units * UNIT
    expert_slots = expert_units * UNIT
    slots, rows, rcode, probs = call(
        dispatch_kernel,
        (
            like((EXPERTS, expert_slots, row_wide), BF16),
            like((tensor, count, width), BF16),
            like((tensor, count, CODE), BF16),
            like((tensor, count, 128), F32),
        ),
        scratch=[
            pltpu.VMEM((count, row_wide), BF16),
            pltpu.VMEM((chunk_slots, row_wide), BF16),
        ],
        smem=2,
        cost=cost(17),
    )(adapter_index, table, *normed2_four, *dy_four, place, down, router, router_up)

    whole = lambda *shape: pl.BlockSpec(shape, lambda step: (0,) * len(shape))
    smem = pl.BlockSpec(memory_space=pltpu.SMEM)
    size = len(early_parts)
    feats = early_parts[0].shape[2]
    shard = pl.BlockSpec((2, 1, feats, hidden), lambda step: (0, step, 0, 0))
    small = [
        whole(CODE, hidden), whole(CODE, hidden), whole(CODE, width), whole(5, CODE, width),
    ]
    early_out, g_hid, g_exo = call(
        partial(early_kernel, size),
        (
            like((base, expert_slots, row_wide), BF16),
            like((2, CODE, hidden), F32),
            like((2, CODE, width), F32),
        ),
        scratch=[pltpu.VMEM((2, width, hidden), BF16)],
        grid=(base,),
        in_specs=[shard] * size
        + [pl.BlockSpec((1, expert_slots, row_wide), lambda step: (step, 0, 0))]
        + small,
        out_specs=(
            pl.BlockSpec((1, expert_slots, row_wide), lambda step: (step, 0, 0)),
            whole(2, CODE, hidden),
            whole(2, CODE, width),
        ),
        cost=cost(16),
    )(*early_parts, after(slots, *stages[3][1:]), up_hid, down_hid, up_exo, down)
    half = like((2, count, width), BF16)
    compact = dp == 8 and images == 2 and hidden == width == 512
    (
        mix_keep, mix_send, grad_keep, grad_send, early,
    ) = call(
        partial(late_kernel, size, base),
        (
            half, half, half, half,
            like((8, 96, width), BF16) if compact else like((6, CODE, width), F32),
        ),
        scratch=[
            pltpu.VMEM((2, width, hidden), BF16),
            pltpu.VMEM((EXPERTS - base, expert_slots, row_wide), BF16),
            pltpu.VMEM((2, CODE, hidden), F32),
            pltpu.VMEM((2, CODE, width), F32),
            pltpu.VMEM((2, CODE, width), F32),
            pltpu.VMEM((chunk_slots, row_wide), BF16),
        ],
        grid=(EXPERTS - base,),
        in_specs=[shard] * size
        + [pl.BlockSpec((1, expert_slots, row_wide), lambda step: (step + base, 0, 0))]
        + small
        + [
            whole(base, expert_slots, row_wide),
            whole(2, CODE, hidden),
            whole(2, CODE, width),
            smem,
            smem,
            whole(tensor, count, width),
            whole(tensor, count, CODE),
            whole(tensor, count, 128),
            whole(tensor, count, 2),
            whole(128, width),
            whole(128, CODE),
        ],
        out_specs=(
            whole(2, count, width), whole(2, count, width),
            whole(2, count, width), whole(2, count, width),
            whole(8, 96, width) if compact else whole(6, CODE, width),
        ),
        cost=cost(30),
    )(
        *late_parts, slots, up_hid, down_hid, up_exo, down, early_out, g_hid, g_exo,
        adapter_index, table, rows, rcode, probs, place.swapaxes(1, 2), router, router_up,
    )

    both = ("dp", "tensor")
    if compact:
        early = lax.all_to_all(early, "dp", 0, 0)
    grad_a, grad_b = reduce_pair(grad_keep, grad_send)
    mix_a, mix_b = reduce_pair(mix_keep, after(mix_send, grad_b))

    middle_grad, proj_grad, code_grad, late = call(
        backward_kernel,
        (
            like((count, width), F32),
            like((count, 3 * width), BF16),
            like((count, 3 * CODE), BF16),
            like((32, images * RANK, 128), BF16) if compact else like((8, CODE, width), F32),
        ),
        scratch=[pltpu.VMEM((ROWS, width), BF16), pltpu.VMEM((8, CODE, width), F32)],
        smem=1,
        cost=cost(11),
    )(
        adapter_index, dy, middle, grad_a, grad_b, norm_gain, weights, up_out,
        normed, code, qkv, prob, mixed, hcode,
    )
    if compact:
        came = lax.all_to_all(late, both, 0, 0)
    input_grad = call(
        input_kernel,
        like((local, width), F32),
        scratch=[pltpu.VMEM((ROWS, width), F32)],
        cost=cost(5),
    )(middle_grad, proj_grad, code_grad, x, norm_gain, weights, down)
    block_out = call(
        finish_kernel,
        like((local, width), F32),
        scratch=[pltpu.VMEM((ROWS, width), F32)],
        cost=cost(2),
    )(after(middle, late), mix_a, mix_b)

    if compact:
        keep = like((2, 16, width), BF16)
        keep, send, early_hid = call(
            early_sum_kernel, (keep, keep, like((32, width), BF16)), cost=cost(2)
        )(after(early, late))
        rows_a, rows_b = reduce_pair(keep, send)
        packed = call(late_sum_kernel, like((dp, 80, width), BF16), cost=cost(2))(
            came.reshape(dp, CODE, 128), ids, early_hid, rows_a, rows_b
        )
        came = lax.all_to_all(packed, "dp", 0, 0)
        mine = jnp.concatenate(
            [came[4:, 48:].reshape(128, width), came[:, 32:48].reshape(128, width)], 0
        )
        whole = like((CODE, width), F32)
        grad_down_in, grad_up_out, grad_up_exo, router_grad, late_heads, early_hid = call(
            unpack_kernel,
            (
                like((5, CODE, width), F32), whole, whole, whole,
                like((4, CODE, 128), F32), like((2, CODE, width), F32),
            ),
            cost=cost(2),
        )(came, *gather_four(mine))
    else:
        cols = width // tensor
        early_shared = lax.psum(early[:4], both)
        early_hid = lax.psum(early[4:], "dp")
        late = lax.psum(late, both)
        late_heads = lax.dynamic_slice_in_dim(
            late[:4], lax.axis_index("tensor") * cols, cols, 2
        )
        grad_down_in = jnp.concatenate([late[4:7], early_shared[:2]], 0)
        grad_up_out, grad_up_exo, router_grad = late[7], early_shared[2], early_shared[3]
    split_up = lambda value: value.reshape(value.shape[:-2] + (ADAPTERS, RANK, value.shape[-1]))
    split_down = lambda value: split_up(value).swapaxes(-1, -2)
    grad_down_in = split_down(grad_down_in)
    grad_up_out = split_up(grad_up_out)
    grad_up_exo = split_up(grad_up_exo)
    grad_up_router = split_up(
        router_grad[:, :EXPERTS] + router_grad[:, EXPERTS : 2 * EXPERTS]
    )
    grad_up_heads = split_up(late_heads[:3])
    grad_down_heads = split_down(late_heads[3])
    grad_up_hidden = split_up(early_hid[0])
    grad_down_hidden = split_down(early_hid[1])
    return (
        block_out,
        input_grad,
        grad_down_in,
        grad_up_heads,
        grad_up_hidden,
        grad_up_router,
        grad_down_heads,
        grad_down_hidden,
        grad_up_out,
        grad_up_exo,
    )


def solution(mesh):
    placed = (
        P(("dp", "tensor"), None),
        P(("dp", "tensor"), None),
        P(),
        P(None, "dp", "tensor"),
        P("dp", "tensor"),
        P(None, "dp", "tensor"),
        P(None, "dp", "tensor"),
        P(),
        P(),
        P(None, None, None, "tensor"),
        P(None, None, "tensor"),
        P(),
        P(None, "tensor", None),
        P(None, "tensor", None),
        P(),
        P(),
        P("dp", None),
        P("dp", None),
        P("dp"),
    )
    return jax.shard_map(
        per_device,
        mesh=mesh,
        in_specs=placed,
        out_specs=(
            P(("dp", "tensor"), None),
            P(("dp", "tensor"), None),
            P(),
            P(None, None, None, "tensor"),
            P(None, None, "tensor"),
            P(),
            P(None, "tensor", None),
            P(None, "tensor", None),
            P(),
            P(),
        ),
        check_vma=False,
    )
```

```python
from functools import partial

import jax
import jax.numpy as jnp
from jax import lax
from jax.experimental import pallas as pl
from jax.experimental.pallas import tpu as pltpu
from jax.sharding import PartitionSpec as P

HEADS = 8
RANK = 16
ADAPTERS = 8
SEQ = 197
EXPERTS = 8
HEAD_DIM = 64
CAP = 394

EPS = 1e-06
CODE = ADAPTERS * RANK
ROWS = 208
UNIT = 16
SCALE = HEAD_DIM ** (-0.5)
F32 = jnp.float32
BF16 = jnp.bfloat16
MIB = 1024 * 1024


def dot(left, right):
    return lax.dot_general(left, right, (((1,), (0,)), ((), ())), preferred_element_type=F32)


def dot_t(left, right):
    return lax.dot_general(left, right, (((1,), (1,)), ((), ())), preferred_element_type=F32)


def tdot(left, right):
    return lax.dot_general(left, right, (((0,), (0,)), ((), ())), preferred_element_type=F32)


def lanes(shape):
    return lax.broadcasted_iota(jnp.int32, shape, len(shape) - 1)


def sublanes(shape):
    return lax.broadcasted_iota(jnp.int32, shape, len(shape) - 2)


def norm_rows(value, gain):
    center = value - jnp.mean(value, -1, keepdims=True)
    spread = jnp.mean(center * center, -1, keepdims=True)
    return center * lax.rsqrt(spread + EPS) * gain


def norm_back(value, gain, grad):
    center = value - jnp.mean(value, -1, keepdims=True)
    rate = lax.rsqrt(jnp.mean(center * center, -1, keepdims=True) + EPS)
    unit = center * rate
    grad = grad * gain
    along = jnp.mean(grad * unit, -1, keepdims=True)
    return rate * (grad - jnp.mean(grad, -1, keepdims=True) - unit * along)


def gelu_pair(value):
    square = value * value
    inner = 0.7978845608028654 * value * (1.0 + 0.044715 * square)
    bent = jnp.tanh(inner)
    half = 0.5 * (1.0 + bent)
    slope = half + 0.5 * value * (1.0 - bent * bent) * (
        0.7978845608028654 * (1.0 + 3.0 * 0.044715 * square)
    )
    return value * half, slope


def call(
    body, outs, scratch=(), smem=0, grid=None, in_specs=None, out_specs=None, cost=None, vmem=56
):
    options = {}
    if grid is not None:
        options = dict(grid=grid, in_specs=in_specs, out_specs=out_specs)
    elif smem:
        def build(*args):
            specs = [pl.BlockSpec(memory_space=pltpu.SMEM)] * smem
            specs += [pl.BlockSpec(memory_space=pltpu.VMEM)] * (len(args) - smem)
            return call(body, outs, scratch, 0, (), specs, None, cost, vmem)(*args)

        return build
    if grid == ():
        options = dict(in_specs=in_specs)
    return pl.pallas_call(
        body,
        out_shape=outs,
        scratch_shapes=list(scratch),
        compiler_params=pltpu.CompilerParams(vmem_limit_bytes=vmem * MIB),
        cost_estimate=cost,
        **options,
    )


def like(shape, dtype):
    return jax.ShapeDtypeStruct(shape, dtype)


def cost(micros):
    return pl.CostEstimate(
        flops=int(micros * 1.1e9), bytes_accessed=int(micros * 3.6e6), transcendentals=0
    )


def image_mask(adapter, index):
    return jnp.where(lanes((1, CODE)) // RANK == adapter[index], 1.0, 0.0)


def route_kernel(cot, rflat, rrow, prow, pcol, dy, place_out, table_out, wide):
    images = dy.shape[0] // ROWS
    chunks, unused, count = rrow.shape
    wide[...] = jnp.zeros_like(wide)
    wide[0 : cot.shape[0], :] = cot[...].astype(F32)
    for image in range(images):
        part = wide[image * SEQ : image * SEQ + ROWS, :]
        part = jnp.where(sublanes((ROWS, 1)) < SEQ, part, 0.0)
        dy[image * ROWS : (image + 1) * ROWS, :] = part.astype(BF16)
    kinds = sublanes((2 * EXPERTS, rflat.shape[1]))
    first = jnp.where(rflat[0:1, :] == kinds, 1.0, 0.0)
    second = jnp.where(rflat[1:2, :] == kinds, 1.0, 0.0)
    first_all = jnp.sum(first, axis=1, keepdims=True)
    first = first.astype(BF16)
    second = second.astype(BF16)
    kinds = sublanes((2 * EXPERTS, count))
    above = jnp.where(sublanes((count, count)) < lanes((count, count)), 1.0, 0.0).astype(BF16)
    square = (2 * EXPERTS, 2 * EXPERTS)
    below = jnp.where(lanes(square) < sublanes(square), 1.0, 0.0).astype(BF16)
    lane = lanes((2 * EXPERTS, 128))
    table = jnp.zeros((2 * EXPERTS, 128), F32)
    filled = jnp.zeros((2 * EXPERTS, 1), F32)
    for chunk in range(chunks):
        earlier = jnp.where(pcol[...] < prow[chunk], 1.0, 0.0).astype(BF16)
        is_first = rrow[chunk, 0:1, :] == kinds
        is_second = rrow[chunk, 1:2, :] == kinds
        place = jnp.where(is_first, dot(first, earlier), 1e9)
        place = jnp.where(is_second, dot(second, earlier) + first_all, place)
        kept = place < CAP
        held = jnp.where(kept, 1.0, 0.0)
        rank = dot(held.astype(BF16), above)
        units = jnp.sum(held, axis=1, keepdims=True)
        units = jnp.floor((units + (UNIT - 1)) * (1.0 / UNIT))
        start = dot(below, jnp.broadcast_to(units, (2 * EXPERTS, 128)).astype(BF16))[:, 0:1]
        spot = jnp.where(kept, start * UNIT + rank + 1.0, 0.0)
        place_out[chunk, 0:1, :] = (
            jnp.sum(jnp.where(is_first, spot, 0.0), axis=0, keepdims=True) - 1.0
        )
        place_out[chunk, 1:2, :] = (
            jnp.sum(jnp.where(is_second, spot, 0.0), axis=0, keepdims=True) - 1.0
        )
        table = jnp.where(lane == chunk, units, table)
        table = jnp.where(lane == chunks + chunk, start, table)
        table = jnp.where(lane == 2 * chunks + chunk, filled, table)
        filled = filled + units
    table = jnp.where(lane == 3 * chunks, filled, table)
    table_out[...] = table.astype(jnp.int32)


def assemble_kernel(count, *refs):
    parts, (extra, other_extra, out, ids) = refs[:count], refs[count:]
    feats = out.shape[2] // count
    out[0, 4] = extra[...]
    out[1, 4] = other_extra[...]
    for step, owner in enumerate(block_owners(count)):
        rows = pl.ds(pl.multiple_of(owner * feats, feats), feats)
        for side in range(2):
            for member in range(4):
                out[side, member, rows, :] = parts[step][
                    side, member * feats : (member + 1) * feats, :
                ]
        ids[owner] = parts[step][0, 4 * feats : 4 * feats + 16, :]


def forward_kernel(
    adapter, tokens, gain, mine, other, down, up_out,
    weights, x_out, normed_out, code_out, qkv_out, prob_out, mixed_out, hcode_out,
    middle_out, normed2_out, wide,
):
    me = lax.axis_index("tensor")
    for step in range(4):
        cols = pl.ds(pl.multiple_of(lax.bitwise_xor(me, step) * 128, 128), 128)
        weights[:, :, cols] = (mine, other)[step % 2][step // 2]
    images = x_out.shape[0] // ROWS
    width = tokens.shape[1]
    wide[...] = jnp.zeros_like(wide)
    wide[0 : tokens.shape[0], :] = tokens[...].astype(F32)
    for image in range(images):
        at = image * ROWS
        rows = slice(at, at + ROWS)
        mask = image_mask(adapter, me * images + image)
        real = sublanes((ROWS, 1)) < SEQ
        x = jnp.where(real, wide[image * SEQ : image * SEQ + ROWS, :], 0.0)
        x_out[rows, :] = x
        normed = norm_rows(x, gain[0:1, :]).astype(BF16)
        normed_out[rows, :] = normed
        for member in range(3):
            code = (mask * dot_t(normed, down[member])).astype(BF16)
            code_out[rows, member * CODE : (member + 1) * CODE] = code
            up = weights[4, member * CODE : (member + 1) * CODE, :]
            proj = dot(normed, weights[member]) + dot(code, up)
            qkv_out[rows, member * width : (member + 1) * width] = proj.astype(BF16)
        low_half = lanes((1, 128)) < HEAD_DIM
        half = (low_half, jnp.logical_not(low_half))
        real_key = lanes((1, ROWS)) < SEQ
        for pair in range(HEADS // 2):
            cols = pair * 128
            q = qkv_out[rows, cols : cols + 128].astype(F32) * SCALE
            k = qkv_out[rows, width + cols : width + cols + 128]
            v = qkv_out[rows, 2 * width + cols : 2 * width + cols + 128].astype(F32)
            mixed = jnp.zeros((ROWS, 128), F32)
            for head in range(2):
                score = dot_t(jnp.where(half[head], q, 0.0).astype(BF16), k)
                score = jnp.where(real_key, score, -1e30)
                raised = jnp.exp(score - jnp.max(score, -1, keepdims=True))
                prob = raised / jnp.sum(raised, -1, keepdims=True)
                prob_out[(image * HEADS // 2 + pair) * 2 + head] = prob
                mixed = mixed + dot(
                    prob.astype(BF16), jnp.where(half[head], v, 0.0).astype(BF16)
                )
            mixed_out[rows, cols : cols + 128] = mixed.astype(BF16)
        mixed = mixed_out[rows, :]
        hcode = (mask * dot_t(mixed, weights[4, 3 * CODE : 4 * CODE, :])).astype(BF16)
        hcode_out[rows, :] = hcode
        middle = x + dot_t(mixed, weights[3]) + dot(hcode, up_out[...])
        middle_out[rows, :] = middle
        normed2_out[rows, :] = norm_rows(middle, gain[1:2, :]).astype(BF16)


def row_adapters(adapter, chunk, count):
    images = count // ROWS
    which = jnp.zeros((count, 1), jnp.int32)
    for image in range(images):
        which = jnp.where(
            sublanes((count, 1)) // ROWS == image, adapter[chunk * images + image], which
        )
    return which


def move_units(table, chunk, expert, chunk_ref, expert_ref, forward):
    start = table[expert, 4 + chunk]
    target = table[expert, 8 + chunk]

    def move(unit, carry):
        here = pl.ds(pl.multiple_of((start + unit) * UNIT, UNIT), UNIT)
        there = pl.ds(pl.multiple_of((target + unit) * UNIT, UNIT), UNIT)
        if forward:
            expert_ref[there, :] = chunk_ref[here, :]
        else:
            chunk_ref[here, :] = expert_ref[there, :]
        return carry

    lax.fori_loop(0, table[expert, chunk], move, 0)


def clear_units(ref, start):
    def clear(unit, carry):
        rows = pl.ds(pl.multiple_of(unit * UNIT, UNIT), UNIT)
        ref[rows, :] = jnp.zeros((UNIT, ref.shape[1]), ref.dtype)
        return carry

    lax.fori_loop(start, ref.shape[0] // UNIT, clear, 0)


def dispatch_kernel(
    adapter, table, own, core, side, both, dy_own, dy_core, dy_side, dy_both,
    place, down, router, up_router,
    slots, normed_out, rcode_out, prob_out, rows, packed,
):
    me = lax.axis_index("tensor")
    count = own.shape[0]
    width = own.shape[1]
    lane = lanes((1, 128))
    for index, (part, dy) in enumerate(
        ((own, dy_own), (core, dy_core), (side, dy_side), (both, dy_both))
    ):
        normed_out[index] = part[...]
        rows[index, :, 0:width] = part[...]
        rows[index, :, width : 2 * width] = dy[...]

    def each(index, carry):
        chunk = lax.bitwise_xor(me, index)
        which = row_adapters(adapter, chunk, count)
        mask = jnp.where(lane // RANK == which, 1.0, 0.0)
        normed = rows[index, :, 0:width]
        rcode = (mask * dot_t(normed, down[4])).astype(BF16)
        rcode_out[index] = rcode
        logits = dot_t(normed, router[...]) + dot_t(rcode, up_router[...])
        logits = jnp.where(lane < 2 * EXPERTS, logits, -1e30)
        raised = jnp.exp(logits - jnp.max(logits, -1, keepdims=True))
        mass = jnp.sum(jnp.where(lane < EXPERTS, raised, 0.0), -1, keepdims=True)
        prob = raised / mass
        prob_out[index] = prob
        high = prob.astype(BF16).astype(F32)
        aux = jnp.where(lane < EXPERTS, high, prob - high)
        aux = jnp.where(lane < 2 * EXPERTS, aux, jnp.where(lane == 16 + which, 1.0, 0.0))
        rows[index, :, 2 * width : 2 * width + 128] = aux.astype(BF16)
        spot = sublanes((packed.shape[0], count)).astype(F32)
        chosen = jnp.logical_or(spot == place[chunk, 0:1, :], spot == place[chunk, 1:2, :])
        chosen = jnp.where(chosen, 1.0, 0.0).astype(BF16)
        packed[...] = dot(chosen, rows[index]).astype(BF16)

        def spread(expert, carry):
            move_units(table, chunk, expert, packed, slots.at[expert], True)
            return carry

        return lax.fori_loop(0, EXPERTS, spread, carry)

    lax.fori_loop(0, 4, each, 0)

    def clear(expert, carry):
        clear_units(slots.at[expert], table[expert, 12])
        return carry

    lax.fori_loop(0, EXPERTS, clear, 0)


def expert_body(expert, slots, w_in, w_out, up_hid, down_hid, up_exo, down, g_hid, g_exo, out):
    width = w_in.shape[0]
    lane = lanes((1, 128))
    x = slots[:, 0:width]
    dy = slots[:, width : 2 * width].astype(F32)
    aux = slots[:, 2 * width : 2 * width + 128]
    expand = jnp.where(sublanes((128, CODE)) - 16 == lanes((128, CODE)) // RANK, 1.0, 0.0)
    mask = dot(aux, expand.astype(BF16))
    here = jnp.logical_and(lax.rem(lane, EXPERTS) == expert, lane < 2 * EXPERTS)
    gate = jnp.sum(jnp.where(here, aux.astype(F32), 0.0), -1, keepdims=True)
    hcode = (mask * dot_t(x, down[3])).astype(BF16)
    before = dot(x, w_in[...]) + dot(hcode, up_hid[...])
    active, slope = gelu_pair(before)
    active = active.astype(BF16)
    ocode = (mask * dot_t(active, down_hid[...])).astype(BF16)
    returned = dot_t(active, w_out[...]) + dot(ocode, up_exo[...])
    gate_grad = jnp.sum(returned * dy, -1, keepdims=True)
    back = (gate * dy).astype(BF16)
    ocode_grad = (mask * dot_t(back, up_exo[...])).astype(BF16)
    active_grad = dot(back, w_out[...]) + dot(ocode_grad, down_hid[...])
    before_grad = (slope * active_grad).astype(BF16)
    hcode_grad = (mask * dot_t(before_grad, up_hid[...])).astype(BF16)
    x_grad = dot_t(before_grad, w_in[...]) + dot(hcode_grad, down[3])
    g_hid[0] += tdot(hcode, before_grad)
    g_hid[1] += tdot(ocode_grad, active)
    g_exo[0] += tdot(hcode_grad, x)
    g_exo[1] += tdot(ocode, back)
    high = gate_grad.astype(BF16).astype(F32)
    spread = jnp.where(here, jnp.where(lane < EXPERTS, high, gate_grad - high), 0.0)
    out[:, 0:width] = (gate * returned).astype(BF16)
    out[:, width : 2 * width] = x_grad.astype(BF16)
    out[:, 2 * width : 2 * width + 128] = spread.astype(BF16)


def fetch_weights(parts, joined, sems, step, count):
    owners = block_owners(min(len(parts), 8))
    feats = parts[0].shape[2]
    slot = lax.rem(step, 2)

    def copies(part, expert, slot, place):
        rows = pl.ds(pl.multiple_of(owners[place] * feats, feats), feats)
        return pltpu.make_async_copy(
            part.at[:, expert], joined.at[slot, :, rows, :], sems.at[slot, place]
        )

    def start(expert, slot):
        for place in range(len(owners) - 1):
            copies(parts[place], expert, slot, place).start()
        place = len(owners) - 1
        if len(parts) == len(owners):
            copies(parts[place], expert, slot, place).start()
            return
        half = parts[place].shape[1]

        @pl.when(expert < half)
        def _():
            copies(parts[place], expert, slot, place).start()

        @pl.when(expert >= half)
        def _():
            copies(parts[place + 1], expert - half, slot, place).start()

    @pl.when(step == 0)
    def _():
        start(0, 0)

    @pl.when(step + 1 < count)
    def _():
        start(step + 1, 1 - slot)

    for place in range(len(owners)):
        copies(parts[place], 0, slot, place).wait()
    return joined.at[slot, 0], joined.at[slot, 1]


def block_owners(size):
    me = lax.axis_index("dp")
    if size == 1:
        return (0,)
    owners = []
    for step in range(size // 2):
        owner = lax.rem(me - 2 * step + size, size)
        owners += [owner, lax.bitwise_xor(owner, 1)]
    return owners


def early_kernel(size, count, *refs):
    parts, refs = refs[:size], refs[size:]
    slots, up_hid, down_hid, up_exo, down, out, g_hid, g_exo, joined, sems = refs
    step = pl.program_id(0)

    @pl.when(step == 0)
    def _():
        g_hid[...] = jnp.zeros_like(g_hid)
        g_exo[...] = jnp.zeros_like(g_exo)

    w_in, w_out = fetch_weights(parts, joined, sems, step, count)
    expert_body(
        step, slots.at[0], w_in, w_out, up_hid, down_hid, up_exo, down,
        g_hid, g_exo, out.at[0],
    )


def late_kernel(size, base, *refs):
    parts, refs = refs[:size], refs[size:]
    (
        slots, up_hid, down_hid, up_exo, down, before, g_hid_before, g_exo_before,
        adapter, table, normed, rcode, prob, place, router, up_router,
        mix_keep, mix_send, grad_keep, grad_send, grads_out,
        joined, sems, late, g_hid, g_exo, g_router, packed,
    ) = refs
    step = pl.program_id(0)
    width = down.shape[2]
    lane = lanes((1, 128))

    @pl.when(step == 0)
    def _():
        g_hid[...] = g_hid_before[...]
        g_exo[...] = g_exo_before[...]
        g_router[...] = jnp.zeros_like(g_router)

    w_in, w_out = fetch_weights(parts, joined, sems, step, EXPERTS - base)
    expert_body(
        step + base, slots.at[0], w_in, w_out, up_hid, down_hid, up_exo, down,
        g_hid, g_exo, late.at[step],
    )

    @pl.when(step == pl.num_programs(0) - 1)
    def _():
        me = lax.axis_index("tensor")
        count = mix_keep.shape[1]

        def combine(index, mix_out, grad_out):
            chunk = lax.bitwise_xor(me, index)
            for base_expert, source in ((0, before), (base, late)):

                def collect(expert, carry):
                    move_units(
                        table, chunk, expert + base_expert, packed, source.at[expert], False
                    )
                    return carry

                lax.fori_loop(0, source.shape[0], collect, 0)
            ending = EXPERTS - 1
            clear_units(packed, table[ending, 4 + chunk] + table[ending, chunk])
            spot = lanes((count, packed.shape[0])).astype(F32)
            chosen = jnp.logical_or(
                spot == place[chunk, :, 0:1], spot == place[chunk, :, 1:2]
            )
            total = dot(jnp.where(chosen, 1.0, 0.0).astype(BF16), packed[...])
            mask = jnp.where(lane // RANK == row_adapters(adapter, chunk, count), 1.0, 0.0)
            mix_out[...] = total[:, 0:width].astype(BF16)
            gates = total[:, 2 * width : 2 * width + 128]
            probs = jnp.where(lane < 2 * EXPERTS, prob[index], 0.0)
            mean = jnp.sum(probs * gates, -1, keepdims=True)
            logit = (probs * (gates - jnp.where(lane < EXPERTS, mean, 0.0))).astype(BF16)
            rcode_grad = (mask * dot(logit, up_router[...])).astype(BF16)
            grad = total[:, width : 2 * width] + dot(logit, router[...])
            grad = grad + dot(rcode_grad, down[4])
            grad_out[...] = grad.astype(BF16)
            g_router[0] += tdot(rcode_grad, normed[index])
            g_router[1, :, 0:128] += tdot(logit, rcode[index])

        def pair(half, carry):
            combine(2 * half, mix_keep.at[half], grad_keep.at[half])
            combine(2 * half + 1, mix_send.at[half], grad_send.at[half])
            return carry

        lax.fori_loop(0, 2, pair, 0)
        shared = (g_exo.at[0], g_router.at[0], g_exo.at[1], g_router.at[1])
        if grads_out.dtype == F32:
            for member in range(4):
                grads_out[member] = shared[member][...]
            grads_out[4:6] = g_hid[...]
            return
        for owner in range(8):
            member, at = divmod(owner * 64, CODE)
            grads_out[owner, 0:64, :] = shared[member][at : at + 64, :].astype(BF16)
            member, at = divmod(owner * 32, CODE)
            grads_out[owner, 64:96, :] = g_hid[member, at : at + 32, :].astype(BF16)


def backward_kernel(
    adapter, dy, middle, grad_a, grad_b, grad_c, gain, weights, up_out,
    normed_in, code_in, qkv_in, prob_in, mixed_in, hcode_in,
    middle_grad_out, proj_grad, code_grad_out, grads_out, mixed_grad, whole,
):
    me = lax.axis_index("tensor")
    images = dy.shape[0] // ROWS
    width = dy.shape[1]
    compact = grads_out.shape[0] == 32

    def keep(image, member, grad):
        if not compact:
            grads_out[member] = grad if image == 0 else grads_out[member] + grad
            return
        whole[member] = grad
        start = pl.multiple_of(adapter[me * images + image] * RANK, RANK)
        rows = whole[member, pl.ds(start, RANK), :].astype(BF16)
        for block in range(4):
            grads_out[member * 4 + block, image * RANK : (image + 1) * RANK, :] = rows[
                :, block * 128 : (block + 1) * 128
            ]

    for image in range(images):
        at = image * ROWS
        rows = slice(at, at + ROWS)
        mask = image_mask(adapter, me * images + image)
        summed = grad_a[0, rows, :].astype(F32) + grad_b[0, rows, :].astype(F32)
        summed = summed + grad_c[rows, :].astype(F32)
        middle_grad = dy[rows, :].astype(F32) + norm_back(
            middle[rows, :], gain[1:2, :], summed
        )
        middle_grad_out[rows, :] = middle_grad
        low = middle_grad.astype(BF16)
        hcode_grad = (mask * dot_t(low, up_out[...])).astype(BF16)
        down_heads = weights[4, 3 * CODE : 4 * CODE, :]
        mixed_grad[...] = (dot(low, weights[3]) + dot(hcode_grad, down_heads)).astype(BF16)
        keep(image, 7, tdot(hcode_in[rows, :], low))
        keep(image, 3, tdot(hcode_grad, mixed_in[rows, :]))
        low_half = lanes((1, 128)) < HEAD_DIM
        half = (low_half, jnp.logical_not(low_half))
        for pair in range(HEADS // 2):
            cols = pair * 128
            q = qkv_in[rows, cols : cols + 128].astype(F32) * SCALE
            k = qkv_in[rows, width + cols : width + cols + 128].astype(F32) * SCALE
            v = qkv_in[rows, 2 * width + cols : 2 * width + cols + 128]
            m = mixed_grad[:, cols : cols + 128].astype(F32)
            q_grad = jnp.zeros((ROWS, 128), F32)
            k_grad = jnp.zeros((ROWS, 128), F32)
            v_grad = jnp.zeros((ROWS, 128), F32)
            for head in range(2):
                prob = prob_in[(image * HEADS // 2 + pair) * 2 + head]
                m_head = jnp.where(half[head], m, 0.0).astype(BF16)
                v_grad = v_grad + tdot(prob.astype(BF16), m_head)
                weight_grad = dot_t(m_head, v)
                along = jnp.sum(prob * weight_grad, -1, keepdims=True)
                score = (prob * (weight_grad - along)).astype(BF16)
                q_grad = q_grad + dot(score, jnp.where(half[head], k, 0.0).astype(BF16))
                k_grad = k_grad + tdot(score, jnp.where(half[head], q, 0.0).astype(BF16))
            proj_grad[rows, cols : cols + 128] = q_grad.astype(BF16)
            proj_grad[rows, width + cols : width + cols + 128] = k_grad.astype(BF16)
            proj_grad[rows, 2 * width + cols : 2 * width + cols + 128] = v_grad.astype(BF16)
        normed = normed_in[rows, :]
        for member in range(3):
            grad = proj_grad[rows, member * width : (member + 1) * width]
            up = weights[4, member * CODE : (member + 1) * CODE, :]
            code_grad = (mask * dot_t(grad, up)).astype(BF16)
            code_grad_out[rows, member * CODE : (member + 1) * CODE] = code_grad
            code = code_in[rows, member * CODE : (member + 1) * CODE]
            keep(image, member, tdot(code, grad))
            keep(image, 4 + member, tdot(code_grad, normed))


def early_sum_kernel(came, keep, send, hid):
    me = lax.axis_index("tensor")
    for index in range(4):
        start = pl.multiple_of(lax.bitwise_xor(me, index) * 16, 16)
        total = came[0, pl.ds(start, 16), :].astype(F32)
        for owner in range(1, came.shape[0]):
            total = total + came[owner, pl.ds(start, 16), :].astype(F32)
        (keep, send)[index % 2][index // 2] = total.astype(BF16)
    total = came[0, 64:96, :].astype(F32)
    for owner in range(1, came.shape[0]):
        total = total + came[owner, 64:96, :].astype(F32)
    hid[...] = total.astype(BF16)


def late_sum_kernel(came, ids, hid, rows_a, rows_b, rows_c, out):
    square = (CODE, CODE)
    total = jnp.zeros(square, F32)
    same = lax.rem(sublanes(square), RANK) == lax.rem(lanes(square), RANK)
    kind = (sublanes(square) // RANK).astype(F32)
    for owner in range(ids.shape[0]):
        chosen = jnp.logical_and(same, kind == ids[owner, 0:1, :].astype(F32))
        total = total + dot(jnp.where(chosen, 1.0, 0.0).astype(BF16), came[owner])
    total = total.astype(BF16)
    rows = rows_a[0].astype(F32) + rows_b[0].astype(F32) + rows_c[...].astype(F32)
    rows = rows.astype(BF16)
    for owner in range(out.shape[0]):
        out[owner, 0:32, :] = hid[...]
        out[owner, 32:48, :] = rows
        for slab in range(4):
            out[owner, 48:80, slab * 128 : (slab + 1) * 128] = total[
                slab * 32 : (slab + 1) * 32, :
            ]


def unpack_kernel(
    came, own, core, side, both,
    down_in, up_out, up_exo, router_out, heads, down_heads, up_hid, down_hid, router,
):
    me = lax.axis_index("tensor")
    for owner in range(8):
        member, at = divmod(owner * 32, CODE)
        (up_hid, down_hid)[member][at : at + 32, :] = came[owner, 0:32, :].astype(F32)
    for member in range(4):
        target = down_heads if member == 3 else heads.at[member]
        for slab in range(4):
            target[slab * 32 : (slab + 1) * 32, :] = came[
                member, 48:80, slab * 128 : (slab + 1) * 128
            ].astype(F32)
    late = (down_in.at[0], down_in.at[1], down_in.at[2], up_out)
    early = (down_in.at[3], down_in.at[4], up_exo, router)
    for index, part in enumerate((own, core, side, both)):
        spot = lax.bitwise_xor(me, index)
        cols = pl.ds(pl.multiple_of(spot * 128, 128), 128)
        for member in range(4):
            for slab in range(4):
                late[member][slab * 32 : (slab + 1) * 32, cols] = part[
                    member * 32 : (member + 1) * 32, slab * 128 : (slab + 1) * 128
                ].astype(F32)
        for owner in range(8):
            rows = pl.ds(pl.multiple_of((owner % 2) * 64 + spot * 16, 16), 16)
            early[owner // 2][rows, :] = part[
                128 + owner * 16 : 144 + owner * 16, :
            ].astype(F32)
    router_out[...] = router[0:EXPERTS, 0:CODE] + router[EXPERTS : 2 * EXPERTS, 0:CODE]


def input_kernel(
    middle_grad, proj_grad, code_grad, x_in, gain, weights, down, input_grad, wide
):
    images = middle_grad.shape[0] // ROWS
    width = middle_grad.shape[1]
    for image in range(images):
        at = image * ROWS
        rows = slice(at, at + ROWS)
        normed_grad = jnp.zeros((ROWS, width), F32)
        for member in range(3):
            grad = proj_grad[rows, member * width : (member + 1) * width]
            normed_grad = normed_grad + dot_t(grad, weights[member])
            code = code_grad[rows, member * CODE : (member + 1) * CODE]
            normed_grad = normed_grad + dot(code, down[member])
        wide[...] = middle_grad[rows, :] + norm_back(x_in[rows, :], gain[0:1, :], normed_grad)
        input_grad[image * SEQ : (image + 1) * SEQ, :] = wide[0:SEQ, :]


def finish_kernel(middle, part_a, part_b, part_c, out, wide):
    images = middle.shape[0] // ROWS
    for image in range(images):
        rows = slice(image * ROWS, (image + 1) * ROWS)
        part = part_a[0, rows, :].astype(F32) + part_b[0, rows, :].astype(F32)
        wide[...] = middle[rows, :] + (part + part_c[rows, :].astype(F32))
        out[image * SEQ : (image + 1) * SEQ, :] = wide[0:SEQ, :]


def swap(value, bit):
    size = lax.axis_size("tensor")
    return lax.ppermute(value, "tensor", [(at, at ^ bit) for at in range(size)])


def gather_four(value):
    core = swap(value, 1)
    side = swap(value, 2)
    return value, core, side, swap(side, 1)


def after(value, *others):
    return lax.optimization_barrier((value,) + others)[0]


def reduce_pair(keep, send):
    came = swap(send, 1)
    other = (keep[1].astype(F32) + came[1].astype(F32)).astype(BF16)
    return keep, came, swap(other, 2)


def gather_projections(shards, extra, ids, others):
    size = lax.axis_size("dp")
    feats = shards.shape[1]
    if size == 8 and feats % 16 == 0:
        block = jnp.concatenate([shards.reshape(-1, 128), ids], 0)
        ring = Ring(jnp.stack([block, swap(block, 2)]))
        begun = ()
        for step in range(size // 2 - 1):
            ring.step(*(others[1:] if step == 2 else ()))
            begun += (ring.done,)
        parts = ring.finish()
        others = others[:1]
        return begun, *call(
            partial(assemble_kernel, size),
            (like((2, 5, size * feats, 128), BF16), like((size,) + ids.shape, BF16)),
            cost=cost(2),
        )(*parts, after(extra, *others), swap(extra, 2))
    whole = lax.all_gather(shards, "dp", axis=1, tiled=True)
    whole = jnp.concatenate([whole, extra[None]], 0)
    return ((),) * 3, jnp.stack([whole, swap(whole, 2)]), ids[None]


class Ring:
    def __init__(self, block):
        self.size = lax.axis_size("dp")
        self.block, self.parts, self.done = block, [], ()

    def along(self, value):
        size = self.size
        return lax.ppermute(value, "dp", [(at, (at + 2) % size) for at in range(size)])

    def across(self, value):
        return lax.ppermute(value, "dp", [(at, at ^ 1) for at in range(self.size)])

    def step(self, *waits, across=()):
        block = after(self.block, *self.done, *waits)
        self.done = self.along(block), self.across(after(block, *across))
        self.parts += [block, self.done[1]]
        self.block = self.done[0]

    def finish(self, *waits, split=None):
        if split is None:
            block = after(self.block, *self.done, *waits)
            return self.parts + [block, self.across(block)]
        passed, crossed = (after(value, *waits) for value in self.done)
        halves = self.across(passed[:, :split]), self.along(crossed[:, split:])
        return self.parts + [passed, *halves]


class Whole:
    def __init__(self, block):
        self.parts = [lax.all_gather(block, "dp", axis=2, tiled=True)]
        self.done = ()

    def step(self, *waits, across=()):
        pass

    def finish(self, *waits, split=None):
        return self.parts


def per_device(
    tokens,
    cotangent,
    norm_gain,
    qkv_weight,
    out_weight,
    expert_in,
    expert_out,
    router_weight,
    down_in,
    up_heads,
    up_hidden,
    up_router,
    down_heads,
    down_hidden,
    up_attn_out,
    up_expert_out,
    routes,
    priority,
    adapter_index,
):
    width = tokens.shape[1]
    local = tokens.shape[0]
    images = local // SEQ
    group_images = routes.shape[0] // SEQ
    count = images * ROWS
    tall = group_images * ROWS
    hidden = expert_in.shape[2]
    dp = lax.axis_size("dp")
    tensor = lax.axis_size("tensor")

    block = jnp.concatenate([qkv_weight, out_weight[None]], 0)
    ids = jnp.repeat(adapter_index.astype(BF16), CODE // adapter_index.shape[0])
    ids = jnp.broadcast_to(ids[None], (16, CODE))
    extra = jnp.concatenate(
        [
            up_heads.reshape(3 * CODE, up_heads.shape[3]),
            down_heads.swapaxes(1, 2).reshape(CODE, down_heads.shape[1]),
        ],
        0,
    )
    base = EXPERTS // 2
    fits = dp == 8 and expert_in.shape[1] % 16 == 0
    gather = Ring if fits else Whole
    early_ring = gather(jnp.stack([expert_in[:base], expert_out[:base]]))
    early_ring.step()
    late_block = jnp.stack([expert_in[base:], expert_out[base:]])

    down = down_in.swapaxes(2, 3).reshape(5, CODE, width)
    down_hid = down_hidden.swapaxes(1, 2).reshape(CODE, hidden)
    up_hid = up_hidden.reshape(CODE, hidden)
    up_out = up_attn_out.reshape(CODE, width)
    up_exo = up_expert_out.reshape(CODE, width)
    router = jnp.pad(jnp.tile(router_weight.T, (2, 1)), ((0, 128 - 2 * EXPERTS), (0, 0)))
    router_up = up_router.transpose(2, 0, 1).reshape(EXPERTS, CODE)
    router_up = jnp.pad(jnp.tile(router_up, (2, 1)), ((0, 128 - 2 * EXPERTS), (0, 0)))

    spare = ROWS - SEQ
    route_row = jnp.pad(
        routes.T.reshape(2, group_images, SEQ), ((0, 0), (0, 0), (0, spare)), constant_values=-1
    ).reshape(2, tall)
    rank_row = jnp.pad(
        priority.reshape(group_images, SEQ), ((0, 0), (0, spare)), constant_values=1 << 20
    ).reshape(1, tall)
    chunk_units = (2 * count + EXPERTS * (UNIT - 1)) // UNIT
    expert_units = -(-CAP // UNIT) + 4
    by_chunk = lambda value: value.reshape(-1, tensor, count).swapaxes(0, 1)
    dy, place, table = call(
        route_kernel,
        (
            like((count, width), BF16),
            like((tensor, 2, count), F32),
            like((2 * EXPERTS, 128), jnp.int32),
        ),
        scratch=[pltpu.VMEM((count, width), F32)],
        cost=cost(5),
    )(cotangent, route_row, by_chunk(route_row), by_chunk(rank_row), rank_row.T)
    dy_four = gather_four(dy)
    begun, mine, ids = gather_projections(block, extra, ids, (dy_four[2],) + early_ring.done)
    early_ring.step(*begun[1])
    late_ring = gather(after(late_block, *begun[2]))
    late_ring.step()
    other = swap(mine, 1)

    (
        weights, x, normed, code, qkv, prob, mixed, hcode, middle, normed2,
    ) = call(
        forward_kernel,
        (
            like((5, width, width), BF16),
            like((count, width), F32),
            like((count, width), BF16),
            like((count, 3 * CODE), BF16),
            like((count, 3 * width), BF16),
            like((images * HEADS, ROWS, ROWS), F32),
            like((count, width), BF16),
            like((count, CODE), BF16),
            like((count, width), F32),
            like((count, width), BF16),
        ),
        scratch=[pltpu.VMEM((count, width), F32)],
        smem=1,
        cost=cost(10),
        vmem=56,
    )(adapter_index, tokens, norm_gain, mine, other, down, up_out)

    normed2_four = gather_four(normed2)
    normed2_four = (after(normed2, *early_ring.done),) + normed2_four[1:]
    early_ring.step(normed2)
    late_ring.step(normed2_four[2])
    row_wide = 2 * width + 128
    chunk_slots = chunk_units * UNIT
    expert_slots = expert_units * UNIT
    slots, rows, rcode, probs = call(
        dispatch_kernel,
        (
            like((EXPERTS, expert_slots, row_wide), BF16),
            like((tensor, count, width), BF16),
            like((tensor, count, CODE), BF16),
            like((tensor, count, 128), F32),
        ),
        scratch=[
            pltpu.VMEM((tensor, count, row_wide), BF16),
            pltpu.VMEM((chunk_slots, row_wide), BF16),
        ],
        smem=2,
        cost=cost(17),
    )(adapter_index, table, *normed2_four, *dy_four, place, down, router, router_up)

    early_parts = early_ring.finish(slots, split=base // 2)
    ready = late_ring.done
    late_ring.step(slots, across=early_parts[7:])
    whole = lambda *shape: pl.BlockSpec(shape, lambda step: (0,) * len(shape))
    smem = pl.BlockSpec(memory_space=pltpu.SMEM)
    size = len(early_parts)
    shard = pl.BlockSpec(memory_space=pltpu.HBM)
    joined = [
        pltpu.VMEM((2, 2, width, hidden), BF16),
        pltpu.SemaphoreType.DMA((2, min(size, 8))),
    ]
    small = [
        whole(CODE, hidden), whole(CODE, hidden), whole(CODE, width), whole(5, CODE, width),
    ]
    early_out, g_hid, g_exo = call(
        partial(early_kernel, size, base),
        (
            like((base, expert_slots, row_wide), BF16),
            like((2, CODE, hidden), F32),
            like((2, CODE, width), F32),
        ),
        scratch=joined,
        grid=(base,),
        in_specs=[shard] * size
        + [pl.BlockSpec((1, expert_slots, row_wide), lambda step: (step, 0, 0))]
        + small,
        out_specs=(
            pl.BlockSpec((1, expert_slots, row_wide), lambda step: (step, 0, 0)),
            whole(2, CODE, hidden),
            whole(2, CODE, width),
        ),
        cost=cost(16),
    )(*early_parts, after(slots, *ready), up_hid, down_hid, up_exo, down)
    late_parts = late_ring.finish(early_out, split=base // 2)
    half = like((2, count, width), BF16)
    compact = dp == 8 and images == 2 and hidden == width == 512
    (
        mix_keep, mix_send, grad_keep, grad_send, early,
    ) = call(
        partial(late_kernel, size, base),
        (
            half, half, half, half,
            like((8, 96, width), BF16) if compact else like((6, CODE, width), F32),
        ),
        scratch=joined
        + [
            pltpu.VMEM((EXPERTS - base, expert_slots, row_wide), BF16),
            pltpu.VMEM((2, CODE, hidden), F32),
            pltpu.VMEM((2, CODE, width), F32),
            pltpu.VMEM((2, CODE, width), F32),
            pltpu.VMEM((chunk_slots, row_wide), BF16),
        ],
        grid=(EXPERTS - base,),
        in_specs=[shard] * size
        + [pl.BlockSpec((1, expert_slots, row_wide), lambda step: (step + base, 0, 0))]
        + small
        + [
            whole(base, expert_slots, row_wide),
            whole(2, CODE, hidden),
            whole(2, CODE, width),
            smem,
            smem,
            whole(tensor, count, width),
            whole(tensor, count, CODE),
            whole(tensor, count, 128),
            whole(tensor, count, 2),
            whole(128, width),
            whole(128, CODE),
        ],
        out_specs=(
            whole(2, count, width), whole(2, count, width),
            whole(2, count, width), whole(2, count, width),
            whole(8, 96, width) if compact else whole(6, CODE, width),
        ),
        cost=cost(30),
    )(
        *late_parts, slots, up_hid, down_hid, up_exo, down, early_out, g_hid, g_exo,
        adapter_index, table, rows, rcode, probs, place.swapaxes(1, 2), router, router_up,
    )

    both = ("dp", "tensor")
    if compact:
        early = lax.all_to_all(early, "dp", 0, 0)
    grads = reduce_pair(grad_keep, grad_send)
    mixes = reduce_pair(mix_keep, after(mix_send, grads[2]))

    middle_grad, proj_grad, code_grad, late = call(
        backward_kernel,
        (
            like((count, width), F32),
            like((count, 3 * width), BF16),
            like((count, 3 * CODE), BF16),
            like((32, images * RANK, 128), BF16) if compact else like((8, CODE, width), F32),
        ),
        scratch=[pltpu.VMEM((ROWS, width), BF16), pltpu.VMEM((8, CODE, width), F32)],
        smem=1,
        cost=cost(11),
        vmem=56,
    )(
        adapter_index, dy, middle, *grads, norm_gain, weights, up_out,
        normed, code, qkv, prob, mixed, hcode,
    )
    if compact:
        came = lax.all_to_all(late, both, 0, 0)
    input_grad = call(
        input_kernel,
        like((local, width), F32),
        scratch=[pltpu.VMEM((ROWS, width), F32)],
        cost=cost(5),
        vmem=56,
    )(middle_grad, proj_grad, code_grad, x, norm_gain, weights, down)
    block_out = call(
        finish_kernel,
        like((local, width), F32),
        scratch=[pltpu.VMEM((ROWS, width), F32)],
        cost=cost(2),
    )(after(middle, late), *mixes)

    if compact:
        keep = like((2, 16, width), BF16)
        keep, send, early_hid = call(
            early_sum_kernel, (keep, keep, like((32, width), BF16)), cost=cost(2)
        )(after(early, late))
        sums = reduce_pair(keep, send)
        packed = call(late_sum_kernel, like((dp, 80, width), BF16), cost=cost(2))(
            came.reshape(dp, CODE, 128), ids, early_hid, *sums
        )
        came = lax.all_to_all(packed, "dp", 0, 0)
        came = after(came, input_grad, block_out)
        mine = jnp.concatenate(
            [came[4:, 48:].reshape(128, width), came[:, 32:48].reshape(128, width)], 0
        )
        whole = like((CODE, width), F32)
        (
            grad_down_in, grad_up_out, grad_up_exo, router_grad,
            grad_up_heads, grad_down_heads, grad_up_hidden, grad_down_hidden,
        ) = call(
            unpack_kernel,
            (
                like((5, CODE, width), F32), whole, whole, like((EXPERTS, CODE), F32),
                like((3, CODE, 128), F32), like((CODE, 128), F32), whole, whole,
            ),
            scratch=[pltpu.VMEM((CODE, width), F32)],
            cost=cost(3),
        )(came, *gather_four(mine))
    else:
        cols = width // tensor
        early_shared = lax.psum(early[:4], both)
        early_hid = lax.psum(early[4:], "dp")
        late = lax.psum(late, both)
        late_heads = lax.dynamic_slice_in_dim(
            late[:4], lax.axis_index("tensor") * cols, cols, 2
        )
        grad_down_in = jnp.concatenate([late[4:7], early_shared[:2]], 0)
        grad_up_out, grad_up_exo = late[7], early_shared[2]
        router_grad = early_shared[3, :, :CODE]
        router_grad = router_grad[:EXPERTS] + router_grad[EXPERTS : 2 * EXPERTS]
        grad_up_heads, grad_down_heads = late_heads[:3], late_heads[3]
        grad_up_hidden, grad_down_hidden = early_hid[0], early_hid[1]
    split_up = lambda value: value.reshape(value.shape[:-2] + (ADAPTERS, RANK, value.shape[-1]))
    split_down = lambda value: split_up(value).swapaxes(-1, -2)
    grad_down_in = split_down(grad_down_in)
    grad_up_out = split_up(grad_up_out)
    grad_up_exo = split_up(grad_up_exo)
    grad_up_router = router_grad.reshape(EXPERTS, ADAPTERS, RANK).transpose(1, 2, 0)
    grad_up_heads = split_up(grad_up_heads)
    grad_down_heads = split_down(grad_down_heads)
    grad_up_hidden = split_up(grad_up_hidden)
    grad_down_hidden = split_down(grad_down_hidden)
    return (
        block_out,
        input_grad,
        grad_down_in,
        grad_up_heads,
        grad_up_hidden,
        grad_up_router,
        grad_down_heads,
        grad_down_hidden,
        grad_up_out,
        grad_up_exo,
    )


def solution(mesh):
    placed = (
        P(("dp", "tensor"), None),
        P(("dp", "tensor"), None),
        P(),
        P(None, "dp", "tensor"),
        P("dp", "tensor"),
        P(None, "dp", "tensor"),
        P(None, "dp", "tensor"),
        P(),
        P(),
        P(None, None, None, "tensor"),
        P(None, None, "tensor"),
        P(),
        P(None, "tensor", None),
        P(None, "tensor", None),
        P(),
        P(),
        P("dp", None),
        P("dp", None),
        P("dp"),
    )
    return jax.shard_map(
        per_device,
        mesh=mesh,
        in_specs=placed,
        out_specs=(
            P(("dp", "tensor"), None),
            P(("dp", "tensor"), None),
            P(),
            P(None, None, None, "tensor"),
            P(None, None, "tensor"),
            P(),
            P(None, "tensor", None),
            P(None, "tensor", None),
            P(),
            P(),
        ),
        check_vma=False,
    )
```

```python
from functools import partial

import jax
import jax.numpy as jnp
from jax import lax
from jax.experimental import pallas as pl
from jax.experimental.pallas import tpu as pltpu
from jax.sharding import PartitionSpec as P

HEADS = 8
RANK = 16
ADAPTERS = 8
SEQ = 197
EXPERTS = 8
HEAD_DIM = 64
CAP = 394

EPS = 1e-06
CODE = ADAPTERS * RANK
ROWS = 208
UNIT = 16
SCALE = HEAD_DIM ** (-0.5)
F32 = jnp.float32
BF16 = jnp.bfloat16
MIB = 1024 * 1024


def dot(left, right):
    return lax.dot_general(left, right, (((1,), (0,)), ((), ())), preferred_element_type=F32)


def dot_t(left, right):
    return lax.dot_general(left, right, (((1,), (1,)), ((), ())), preferred_element_type=F32)


def tdot(left, right):
    return lax.dot_general(left, right, (((0,), (0,)), ((), ())), preferred_element_type=F32)


def lanes(shape):
    return lax.broadcasted_iota(jnp.int32, shape, len(shape) - 1)


def sublanes(shape):
    return lax.broadcasted_iota(jnp.int32, shape, len(shape) - 2)


def norm_rows(value, gain):
    center = value - jnp.mean(value, -1, keepdims=True)
    spread = jnp.mean(center * center, -1, keepdims=True)
    return center * lax.rsqrt(spread + EPS) * gain


def norm_back(value, gain, grad):
    center = value - jnp.mean(value, -1, keepdims=True)
    rate = lax.rsqrt(jnp.mean(center * center, -1, keepdims=True) + EPS)
    unit = center * rate
    grad = grad * gain
    along = jnp.mean(grad * unit, -1, keepdims=True)
    return rate * (grad - jnp.mean(grad, -1, keepdims=True) - unit * along)


def gelu_pair(value):
    square = value * value
    inner = 0.7978845608028654 * value * (1.0 + 0.044715 * square)
    bent = jnp.tanh(inner)
    half = 0.5 * (1.0 + bent)
    slope = half + 0.5 * value * (1.0 - bent * bent) * (
        0.7978845608028654 * (1.0 + 3.0 * 0.044715 * square)
    )
    return value * half, slope


def call(
    body, outs, scratch=(), smem=0, grid=None, in_specs=None, out_specs=None, cost=None, vmem=56
):
    options = {}
    if grid is not None:
        options = dict(grid=grid, in_specs=in_specs, out_specs=out_specs)
    elif in_specs is not None:
        options = dict(in_specs=in_specs, out_specs=out_specs)
    elif smem:
        def build(*args):
            specs = [pl.BlockSpec(memory_space=pltpu.SMEM)] * smem
            specs += [pl.BlockSpec(memory_space=pltpu.VMEM)] * (len(args) - smem)
            if isinstance(outs, tuple):
                ends = (pl.BlockSpec(memory_space=pltpu.VMEM),) * len(outs)
            else:
                ends = pl.BlockSpec(memory_space=pltpu.VMEM)
            return call(body, outs, scratch, 0, None, specs, ends, cost, vmem)(*args)

        return build
    return pl.pallas_call(
        body,
        out_shape=outs,
        scratch_shapes=list(scratch),
        compiler_params=pltpu.CompilerParams(vmem_limit_bytes=vmem * MIB),
        cost_estimate=cost,
        **options,
    )


def like(shape, dtype):
    return jax.ShapeDtypeStruct(shape, dtype)


def cost(micros):
    return pl.CostEstimate(
        flops=int(micros * 1.1e9), bytes_accessed=int(micros * 3.6e6), transcendentals=0
    )


def image_mask(adapter, index):
    return jnp.where(lanes((1, CODE)) // RANK == adapter[index], 1.0, 0.0)


def route_kernel(cot, rflat, rrow, prow, pcol, dy, place_out, table_out, wide):
    images = dy.shape[0] // ROWS
    chunks, unused, count = rrow.shape
    wide[...] = jnp.zeros_like(wide)
    wide[0 : cot.shape[0], :] = cot[...].astype(F32)
    for image in range(images):
        part = wide[image * SEQ : image * SEQ + ROWS, :]
        part = jnp.where(sublanes((ROWS, 1)) < SEQ, part, 0.0)
        dy[image * ROWS : (image + 1) * ROWS, :] = part.astype(BF16)
    kinds = sublanes((2 * EXPERTS, rflat.shape[1]))
    first = jnp.where(rflat[0:1, :] == kinds, 1.0, 0.0)
    second = jnp.where(rflat[1:2, :] == kinds, 1.0, 0.0)
    first_all = jnp.sum(first, axis=1, keepdims=True)
    first = first.astype(BF16)
    second = second.astype(BF16)
    kinds = sublanes((2 * EXPERTS, count))
    above = jnp.where(sublanes((count, count)) < lanes((count, count)), 1.0, 0.0).astype(BF16)
    square = (2 * EXPERTS, 2 * EXPERTS)
    below = jnp.where(lanes(square) < sublanes(square), 1.0, 0.0).astype(BF16)
    lane = lanes((2 * EXPERTS, 128))
    table = jnp.zeros((2 * EXPERTS, 128), F32)
    filled = jnp.zeros((2 * EXPERTS, 1), F32)
    for chunk in range(chunks):
        earlier = jnp.where(pcol[...] < prow[chunk], 1.0, 0.0).astype(BF16)
        is_first = rrow[chunk, 0:1, :] == kinds
        is_second = rrow[chunk, 1:2, :] == kinds
        place = jnp.where(is_first, dot(first, earlier), 1e9)
        place = jnp.where(is_second, dot(second, earlier) + first_all, place)
        kept = place < CAP
        held = jnp.where(kept, 1.0, 0.0)
        rank = dot(held.astype(BF16), above)
        units = jnp.sum(held, axis=1, keepdims=True)
        units = jnp.floor((units + (UNIT - 1)) * (1.0 / UNIT))
        start = dot(below, jnp.broadcast_to(units, (2 * EXPERTS, 128)).astype(BF16))[:, 0:1]
        spot = jnp.where(kept, start * UNIT + rank + 1.0, 0.0)
        place_out[chunk, 0:1, :] = (
            jnp.sum(jnp.where(is_first, spot, 0.0), axis=0, keepdims=True) - 1.0
        )
        place_out[chunk, 1:2, :] = (
            jnp.sum(jnp.where(is_second, spot, 0.0), axis=0, keepdims=True) - 1.0
        )
        table = jnp.where(lane == chunk, units, table)
        table = jnp.where(lane == chunks + chunk, start, table)
        table = jnp.where(lane == 2 * chunks + chunk, filled, table)
        filled = filled + units
    table = jnp.where(lane == 3 * chunks, filled, table)
    table_out[...] = table.astype(jnp.int32)


def assemble_kernel(count, *refs):
    parts, (extra, other_extra, out, ids) = refs[:count], refs[count:]
    feats = out.shape[2] // count
    out[0, 4] = extra[...]
    out[1, 4] = other_extra[...]
    for step, owner in enumerate(block_owners(count)):
        rows = pl.ds(pl.multiple_of(owner * feats, feats), feats)
        for side in range(2):
            for member in range(4):
                out[side, member, rows, :] = parts[step][
                    side, member * feats : (member + 1) * feats, :
                ]
        ids[owner] = parts[step][0, 4 * feats : 4 * feats + 16, :]


def forward_kernel(
    adapter, tokens, gain, mine, other, down, up_out,
    weights, x_out, normed_out, code_out, qkv_out, prob_out, mixed_out, hcode_out,
    middle_out, normed2_out, wide,
):
    me = lax.axis_index("tensor")
    for step in range(4):
        cols = pl.ds(pl.multiple_of(lax.bitwise_xor(me, step) * 128, 128), 128)
        weights[:, :, cols] = (mine, other)[step % 2][step // 2]
    images = x_out.shape[0] // ROWS
    width = tokens.shape[1]
    wide[...] = jnp.zeros_like(wide)
    wide[0 : tokens.shape[0], :] = tokens[...].astype(F32)
    for image in range(images):
        at = image * ROWS
        rows = slice(at, at + ROWS)
        mask = image_mask(adapter, me * images + image)
        real = sublanes((ROWS, 1)) < SEQ
        x = jnp.where(real, wide[image * SEQ : image * SEQ + ROWS, :], 0.0)
        x_out[rows, :] = x
        normed = norm_rows(x, gain[0:1, :]).astype(BF16)
        normed_out[rows, :] = normed
        for member in range(3):
            code = (mask * dot_t(normed, down[member])).astype(BF16)
            code_out[rows, member * CODE : (member + 1) * CODE] = code
            up = weights[4, member * CODE : (member + 1) * CODE, :]
            proj = dot(normed, weights[member]) + dot(code, up)
            qkv_out[rows, member * width : (member + 1) * width] = proj.astype(BF16)
        low_half = lanes((1, 128)) < HEAD_DIM
        half = (low_half, jnp.logical_not(low_half))
        real_key = lanes((1, ROWS)) < SEQ
        for pair in range(HEADS // 2):
            cols = pair * 128
            q = qkv_out[rows, cols : cols + 128].astype(F32) * SCALE
            k = qkv_out[rows, width + cols : width + cols + 128]
            v = qkv_out[rows, 2 * width + cols : 2 * width + cols + 128].astype(F32)
            mixed = jnp.zeros((ROWS, 128), F32)
            for head in range(2):
                score = dot_t(jnp.where(half[head], q, 0.0).astype(BF16), k)
                score = jnp.where(real_key, score, -1e30)
                raised = jnp.exp(score - jnp.max(score, -1, keepdims=True))
                prob = raised / jnp.sum(raised, -1, keepdims=True)
                prob_out[(image * HEADS // 2 + pair) * 2 + head] = prob
                mixed = mixed + dot(
                    prob.astype(BF16), jnp.where(half[head], v, 0.0).astype(BF16)
                )
            mixed_out[rows, cols : cols + 128] = mixed.astype(BF16)
        mixed = mixed_out[rows, :]
        hcode = (mask * dot_t(mixed, weights[4, 3 * CODE : 4 * CODE, :])).astype(BF16)
        hcode_out[rows, :] = hcode
        middle = x + dot_t(mixed, weights[3]) + dot(hcode, up_out[...])
        middle_out[rows, :] = middle
        normed2_out[rows, :] = norm_rows(middle, gain[1:2, :]).astype(BF16)


def row_adapters(adapter, chunk, count):
    images = count // ROWS
    which = jnp.zeros((count, 1), jnp.int32)
    for image in range(images):
        which = jnp.where(
            sublanes((count, 1)) // ROWS == image, adapter[chunk * images + image], which
        )
    return which


def move_units(table, chunk, expert, chunk_ref, expert_ref, forward):
    start = table[expert, 4 + chunk]
    target = table[expert, 8 + chunk]

    count = table[expert, chunk]

    def move(unit, units):
        here = pl.ds(pl.multiple_of((start + unit) * UNIT, UNIT), units * UNIT)
        there = pl.ds(pl.multiple_of((target + unit) * UNIT, UNIT), units * UNIT)
        if forward:
            expert_ref[there, :] = chunk_ref[here, :]
        else:
            chunk_ref[here, :] = expert_ref[there, :]

    def four(step, carry):
        move(4 * step, 4)
        return carry

    lax.fori_loop(0, lax.shift_right_logical(count, 2), four, 0)

    @pl.when(lax.bitwise_and(count, 2) != 0)
    def _():
        move(count - lax.bitwise_and(count, 3), 2)

    @pl.when(lax.bitwise_and(count, 1) != 0)
    def _():
        move(count - 1, 1)


def clear_units(ref, start):
    def clear(unit, carry):
        rows = pl.ds(pl.multiple_of(unit * UNIT, UNIT), UNIT)
        ref[rows, :] = jnp.zeros((UNIT, ref.shape[1]), ref.dtype)
        return carry

    lax.fori_loop(start, ref.shape[0] // UNIT, clear, 0)


def dispatch_kernel(
    adapter, table, own, core, side, both, dy_own, dy_core, dy_side, dy_both,
    place, down, router, up_router,
    slots, normed_out, rcode_out, prob_out, rows, packed,
):
    me = lax.axis_index("tensor")
    count = own.shape[0]
    width = own.shape[1]
    lane = lanes((1, 128))
    for index, (part, dy) in enumerate(
        ((own, dy_own), (core, dy_core), (side, dy_side), (both, dy_both))
    ):
        normed_out[index] = part[...]
        rows[index, :, 0:width] = part[...]
        rows[index, :, width : 2 * width] = dy[...]

    def each(index, carry):
        chunk = lax.bitwise_xor(me, index)
        which = row_adapters(adapter, chunk, count)
        mask = jnp.where(lane // RANK == which, 1.0, 0.0)
        normed = rows[index, :, 0:width]
        rcode = (mask * dot_t(normed, down[4])).astype(BF16)
        rcode_out[index] = rcode
        logits = dot_t(normed, router[...]) + dot_t(rcode, up_router[...])
        logits = jnp.where(lane < 2 * EXPERTS, logits, -1e30)
        raised = jnp.exp(logits - jnp.max(logits, -1, keepdims=True))
        mass = jnp.sum(jnp.where(lane < EXPERTS, raised, 0.0), -1, keepdims=True)
        prob = raised / mass
        prob_out[index] = prob
        high = prob.astype(BF16).astype(F32)
        aux = jnp.where(lane < EXPERTS, high, prob - high)
        aux = jnp.where(lane < 2 * EXPERTS, aux, jnp.where(lane == 16 + which, 1.0, 0.0))
        rows[index, :, 2 * width : 2 * width + 128] = aux.astype(BF16)
        spot = sublanes((packed.shape[0], count)).astype(F32)
        chosen = jnp.logical_or(spot == place[chunk, 0:1, :], spot == place[chunk, 1:2, :])
        chosen = jnp.where(chosen, 1.0, 0.0).astype(BF16)
        packed[...] = dot(chosen, rows[index]).astype(BF16)

        def spread(expert, carry):
            move_units(table, chunk, expert, packed, slots.at[expert], True)
            return carry

        return lax.fori_loop(0, EXPERTS, spread, carry)

    lax.fori_loop(0, 4, each, 0)

    def clear(expert, carry):
        clear_units(slots.at[expert], table[expert, 12])
        return carry

    lax.fori_loop(0, EXPERTS, clear, 0)


def expert_body(
    expert, slots, w_in, w_out, up_hid, down_hid, up_exo, down, g_hid, g_exo, grad_out, mix_out
):
    width = w_in.shape[0]
    lane = lanes((1, 128))
    x = slots[:, 0:width]
    dy = slots[:, width : 2 * width].astype(F32)
    aux = slots[:, 2 * width : 2 * width + 128]
    expand = jnp.where(sublanes((128, CODE)) - 16 == lanes((128, CODE)) // RANK, 1.0, 0.0)
    mask = dot(aux, expand.astype(BF16))
    here = jnp.logical_and(lax.rem(lane, EXPERTS) == expert, lane < 2 * EXPERTS)
    gate = jnp.sum(jnp.where(here, aux.astype(F32), 0.0), -1, keepdims=True)
    hcode = (mask * dot_t(x, down[3])).astype(BF16)
    before = dot(x, w_in[...]) + dot(hcode, up_hid[...])
    active, slope = gelu_pair(before)
    active = active.astype(BF16)
    ocode = (mask * dot_t(active, down_hid[...])).astype(BF16)
    returned = dot_t(active, w_out[...]) + dot(ocode, up_exo[...])
    gate_grad = jnp.sum(returned * dy, -1, keepdims=True)
    back = (gate * dy).astype(BF16)
    ocode_grad = (mask * dot_t(back, up_exo[...])).astype(BF16)
    active_grad = dot(back, w_out[...]) + dot(ocode_grad, down_hid[...])
    before_grad = (slope * active_grad).astype(BF16)
    hcode_grad = (mask * dot_t(before_grad, up_hid[...])).astype(BF16)
    x_grad = dot_t(before_grad, w_in[...]) + dot(hcode_grad, down[3])
    g_hid[0] += tdot(hcode, before_grad)
    g_hid[1] += tdot(ocode_grad, active)
    g_exo[0] += tdot(hcode_grad, x)
    g_exo[1] += tdot(ocode, back)
    high = gate_grad.astype(BF16).astype(F32)
    spread = jnp.where(here, jnp.where(lane < EXPERTS, high, gate_grad - high), 0.0)
    mix_out[...] = (gate * returned).astype(BF16)
    grad_out[:, 0:width] = x_grad.astype(BF16)
    grad_out[:, width : width + 128] = spread.astype(BF16)


def fetch_weights(parts, pieces, joined, sems, step, count, first):
    common = len(parts) - len(pieces)
    owners = block_owners(common + 1 if pieces else common)
    feats = parts[0].shape[2]
    slot = lax.rem(step, 2)

    def copies(part, expert, slot, place):
        rows = pl.ds(pl.multiple_of(owners[place] * feats, feats), feats)
        return pltpu.make_async_copy(
            part.at[:, expert], joined.at[slot, :, rows, :], sems.at[slot, place]
        )

    def start(expert, slot):
        for place in range(common):
            copies(parts[place], expert, slot, place).start()
        for part, begin in zip(parts[common:], pieces):

            @pl.when(jnp.logical_and(expert >= begin, expert < begin + part.shape[1]))
            def _():
                copies(part, expert - begin, slot, common).start()

    @pl.when(step == 0)
    def _():
        start(step + first, 0)

    @pl.when(step + 1 < count)
    def _():
        start(step + 1 + first, 1 - slot)

    for place in range(len(owners)):
        copies(parts[place], 0, slot, place).wait()
    return joined.at[slot, 0], joined.at[slot, 1]


def block_owners(size):
    me = lax.axis_index("dp")
    if size == 1:
        return (0,)
    owners = []
    for step in range(size // 2):
        owner = lax.rem(me - 2 * step + size, size)
        owners += [owner, lax.bitwise_xor(owner, 1)]
    return owners


def expert_kernel(size, pieces, count, first, base, *refs):
    parts, refs = refs[:size], refs[size:]
    slots, up_hid, down_hid, up_exo, down, *before, grad_out, mix_out = refs[:-4]
    g_hid, g_exo, joined, sems = refs[-4:]
    step = pl.program_id(0)

    @pl.when(step == 0)
    def _():
        g_hid[...] = before[0][...] if before else jnp.zeros_like(g_hid)
        g_exo[...] = before[1][...] if before else jnp.zeros_like(g_exo)

    w_in, w_out = fetch_weights(parts, pieces, joined, sems, step, count, first)
    expert_body(
        step + base, slots.at[0], w_in, w_out, up_hid, down_hid, up_exo, down,
        g_hid, g_exo, grad_out.at[0], mix_out.at[0],
    )


def collect_chunk(table, chunk, sources, packed):
    base = 0
    for source in sources:

        def collect(expert, carry, source=source, base=base):
            move_units(table, chunk, expert + base, packed, source.at[expert], False)
            return carry

        lax.fori_loop(0, source.shape[0], collect, 0)
        base += source.shape[0]
    ending = EXPERTS - 1
    clear_units(packed, table[ending, 4 + chunk] + table[ending, chunk])


def chosen_slots(place, chunk, packed):
    shape = (place.shape[1], packed.shape[0])
    spot = lanes(shape).astype(F32)
    chosen = jnp.logical_or(spot == place[chunk, :, 0:1], spot == place[chunk, :, 1:2])
    return jnp.where(chosen, 1.0, 0.0).astype(BF16)


def last_kernel(size, pieces, count, first, base, *refs):
    parts, refs = refs[:size], refs[size:]
    (
        slots, up_hid, down_hid, up_exo, down, g_hid_before, g_exo_before,
        adapter, table, place, router, up_router, *waiting,
    ) = refs[:-15]
    (
        mix_out, grad_keep, grad_send, grads_out,
        joined, sems, collected, g_hid, g_exo, g_router, packed, normed, rcode, prob, came,
    ) = refs[-15:]
    step = pl.program_id(0)
    width = down.shape[2]
    lane = lanes((1, 128))
    targets, at = [], 0
    for source in waiting[:-3]:
        targets.append(collected.at[at : at + source.shape[0]])
        at += source.shape[0]
    targets += [normed, rcode, prob]
    arrivals = [
        pltpu.make_async_copy(source, target, came.at[index])
        for index, (source, target) in enumerate(zip(waiting, targets))
    ]

    @pl.when(step == 0)
    def _():
        g_hid[...] = g_hid_before[...]
        g_exo[...] = g_exo_before[...]
        g_router[...] = jnp.zeros_like(g_router)
        for arrival in arrivals:
            arrival.start()

    w_in, w_out = fetch_weights(parts, pieces, joined, sems, step, count, first)
    expert_body(
        step + base, slots.at[0], w_in, w_out, up_hid, down_hid, up_exo, down,
        g_hid, g_exo, collected.at[step + base], mix_out.at[0],
    )

    @pl.when(step == count - 1)
    def _():
        me = lax.axis_index("tensor")
        tall = normed.shape[1]
        for arrival in arrivals:
            arrival.wait()

        def combine(index, grad_out):
            chunk = lax.bitwise_xor(me, index)
            collect_chunk(table, chunk, [collected], packed)
            total = dot(chosen_slots(place, chunk, packed), packed[...])
            mask = jnp.where(lane // RANK == row_adapters(adapter, chunk, tall), 1.0, 0.0)
            gates = total[:, width : width + 128]
            probs = jnp.where(lane < 2 * EXPERTS, prob[index], 0.0)
            mean = jnp.sum(probs * gates, -1, keepdims=True)
            logit = (probs * (gates - jnp.where(lane < EXPERTS, mean, 0.0))).astype(BF16)
            rcode_grad = (mask * dot(logit, up_router[...])).astype(BF16)
            grad = total[:, 0:width] + dot(logit, router[...])
            grad = grad + dot(rcode_grad, down[4])
            grad_out[...] = grad.astype(BF16)
            g_router[0] += tdot(rcode_grad, normed[index])
            g_router[1, :, 0:128] += tdot(logit, rcode[index])

        def pair(half, carry):
            combine(2 * half, grad_keep.at[half])
            combine(2 * half + 1, grad_send.at[half])
            return carry

        lax.fori_loop(0, 2, pair, 0)
        shared = (g_exo.at[0], g_router.at[0], g_exo.at[1], g_router.at[1])
        if grads_out.dtype == F32:
            for member in range(4):
                grads_out[member] = shared[member][...]
            grads_out[4:6] = g_hid[...]
            return
        for owner in range(8):
            member, at = divmod(owner * 64, CODE)
            grads_out[owner, 0:64, :] = shared[member][at : at + 64, :].astype(BF16)
            member, at = divmod(owner * 32, CODE)
            grads_out[owner, 64:96, :] = g_hid[member, at : at + 32, :].astype(BF16)


def mix_kernel(table, place, *refs):
    sources, (mix_keep, mix_send, packed) = refs[:-3], refs[-3:]
    me = lax.axis_index("tensor")

    def combine(index, mix_out):
        chunk = lax.bitwise_xor(me, index)
        collect_chunk(table, chunk, sources, packed)
        mix_out[...] = dot(chosen_slots(place, chunk, packed), packed[...]).astype(BF16)

    def pair(half, carry):
        combine(2 * half, mix_keep.at[half])
        combine(2 * half + 1, mix_send.at[half])
        return carry

    lax.fori_loop(0, 2, pair, 0)


def backward_kernel(
    adapter, dy, middle, grad_a, grad_b, grad_c, gain, weights, up_out,
    normed_in, code_in, qkv_in, prob_in, mixed_in, hcode_in,
    middle_grad_out, proj_grad, code_grad_out, grads_out, mixed_grad, whole,
):
    me = lax.axis_index("tensor")
    images = dy.shape[0] // ROWS
    width = dy.shape[1]
    compact = grads_out.shape[0] == 32

    def keep(image, member, grad):
        if not compact:
            grads_out[member] = grad if image == 0 else grads_out[member] + grad
            return
        whole[member] = grad
        start = pl.multiple_of(adapter[me * images + image] * RANK, RANK)
        rows = whole[member, pl.ds(start, RANK), :].astype(BF16)
        for block in range(4):
            grads_out[member * 4 + block, image * RANK : (image + 1) * RANK, :] = rows[
                :, block * 128 : (block + 1) * 128
            ]

    for image in range(images):
        at = image * ROWS
        rows = slice(at, at + ROWS)
        mask = image_mask(adapter, me * images + image)
        summed = grad_a[0, rows, :].astype(F32) + grad_b[0, rows, :].astype(F32)
        summed = summed + grad_c[rows, :].astype(F32)
        middle_grad = dy[rows, :].astype(F32) + norm_back(
            middle[rows, :], gain[1:2, :], summed
        )
        middle_grad_out[rows, :] = middle_grad
        low = middle_grad.astype(BF16)
        hcode_grad = (mask * dot_t(low, up_out[...])).astype(BF16)
        down_heads = weights[4, 3 * CODE : 4 * CODE, :]
        mixed_grad[...] = (dot(low, weights[3]) + dot(hcode_grad, down_heads)).astype(BF16)
        keep(image, 7, tdot(hcode_in[rows, :], low))
        keep(image, 3, tdot(hcode_grad, mixed_in[rows, :]))
        low_half = lanes((1, 128)) < HEAD_DIM
        half = (low_half, jnp.logical_not(low_half))
        for pair in range(HEADS // 2):
            cols = pair * 128
            q = qkv_in[rows, cols : cols + 128].astype(F32) * SCALE
            k = qkv_in[rows, width + cols : width + cols + 128].astype(F32) * SCALE
            v = qkv_in[rows, 2 * width + cols : 2 * width + cols + 128]
            m = mixed_grad[:, cols : cols + 128].astype(F32)
            q_grad = jnp.zeros((ROWS, 128), F32)
            k_grad = jnp.zeros((ROWS, 128), F32)
            v_grad = jnp.zeros((ROWS, 128), F32)
            for head in range(2):
                prob = prob_in[(image * HEADS // 2 + pair) * 2 + head]
                m_head = jnp.where(half[head], m, 0.0).astype(BF16)
                v_grad = v_grad + tdot(prob.astype(BF16), m_head)
                weight_grad = dot_t(m_head, v)
                along = jnp.sum(prob * weight_grad, -1, keepdims=True)
                score = (prob * (weight_grad - along)).astype(BF16)
                q_grad = q_grad + dot(score, jnp.where(half[head], k, 0.0).astype(BF16))
                k_grad = k_grad + tdot(score, jnp.where(half[head], q, 0.0).astype(BF16))
            proj_grad[rows, cols : cols + 128] = q_grad.astype(BF16)
            proj_grad[rows, width + cols : width + cols + 128] = k_grad.astype(BF16)
            proj_grad[rows, 2 * width + cols : 2 * width + cols + 128] = v_grad.astype(BF16)
        normed = normed_in[rows, :]
        for member in range(3):
            grad = proj_grad[rows, member * width : (member + 1) * width]
            up = weights[4, member * CODE : (member + 1) * CODE, :]
            code_grad = (mask * dot_t(grad, up)).astype(BF16)
            code_grad_out[rows, member * CODE : (member + 1) * CODE] = code_grad
            code = code_in[rows, member * CODE : (member + 1) * CODE]
            keep(image, member, tdot(code, grad))
            keep(image, 4 + member, tdot(code_grad, normed))


def early_sum_kernel(came, keep, send, hid):
    me = lax.axis_index("tensor")
    for index in range(4):
        start = pl.multiple_of(lax.bitwise_xor(me, index) * 16, 16)
        total = came[0, pl.ds(start, 16), :].astype(F32)
        for owner in range(1, came.shape[0]):
            total = total + came[owner, pl.ds(start, 16), :].astype(F32)
        (keep, send)[index % 2][index // 2] = total.astype(BF16)
    total = came[0, 64:96, :].astype(F32)
    for owner in range(1, came.shape[0]):
        total = total + came[owner, 64:96, :].astype(F32)
    hid[...] = total.astype(BF16)


def late_sum_kernel(came, ids, hid, rows_a, rows_b, rows_c, out):
    square = (CODE, CODE)
    total = jnp.zeros(square, F32)
    same = lax.rem(sublanes(square), RANK) == lax.rem(lanes(square), RANK)
    kind = (sublanes(square) // RANK).astype(F32)
    for owner in range(ids.shape[0]):
        chosen = jnp.logical_and(same, kind == ids[owner, 0:1, :].astype(F32))
        total = total + dot(jnp.where(chosen, 1.0, 0.0).astype(BF16), came[owner])
    total = total.astype(BF16)
    rows = rows_a[0].astype(F32) + rows_b[0].astype(F32) + rows_c[...].astype(F32)
    rows = rows.astype(BF16)
    for owner in range(out.shape[0]):
        out[owner, 0:32, :] = hid[...]
        out[owner, 32:48, :] = rows
        for slab in range(4):
            out[owner, 48:80, slab * 128 : (slab + 1) * 128] = total[
                slab * 32 : (slab + 1) * 32, :
            ]


def unpack_kernel(
    came, own, core, side, both,
    down_in, up_out, up_exo, router_out, heads, down_heads, up_hid, down_hid, router,
):
    me = lax.axis_index("tensor")
    for owner in range(8):
        member, at = divmod(owner * 32, CODE)
        (up_hid, down_hid)[member][at : at + 32, :] = came[owner, 0:32, :].astype(F32)
    for member in range(4):
        target = down_heads if member == 3 else heads.at[member]
        for slab in range(4):
            target[slab * 32 : (slab + 1) * 32, :] = came[
                member, 48:80, slab * 128 : (slab + 1) * 128
            ].astype(F32)
    late = (down_in.at[0], down_in.at[1], down_in.at[2], up_out)
    early = (down_in.at[3], down_in.at[4], up_exo, router)
    for index, part in enumerate((own, core, side, both)):
        spot = lax.bitwise_xor(me, index)
        cols = pl.ds(pl.multiple_of(spot * 128, 128), 128)
        for member in range(4):
            for slab in range(4):
                late[member][slab * 32 : (slab + 1) * 32, cols] = part[
                    member * 32 : (member + 1) * 32, slab * 128 : (slab + 1) * 128
                ].astype(F32)
        for owner in range(8):
            rows = pl.ds(pl.multiple_of((owner % 2) * 64 + spot * 16, 16), 16)
            early[owner // 2][rows, :] = part[
                128 + owner * 16 : 144 + owner * 16, :
            ].astype(F32)
    total = router[0:EXPERTS, 0:CODE] + router[EXPERTS : 2 * EXPERTS, 0:CODE]
    for adapter in range(ADAPTERS):
        router_out[adapter] = total[:, adapter * RANK : (adapter + 1) * RANK]


def input_kernel(
    middle_grad, proj_grad, code_grad, x_in, gain, weights, down, input_grad, wide
):
    images = middle_grad.shape[0] // ROWS
    width = middle_grad.shape[1]
    for image in range(images):
        at = image * ROWS
        rows = slice(at, at + ROWS)
        normed_grad = jnp.zeros((ROWS, width), F32)
        for member in range(3):
            grad = proj_grad[rows, member * width : (member + 1) * width]
            normed_grad = normed_grad + dot_t(grad, weights[member])
            code = code_grad[rows, member * CODE : (member + 1) * CODE]
            normed_grad = normed_grad + dot(code, down[member])
        wide[...] = middle_grad[rows, :] + norm_back(x_in[rows, :], gain[0:1, :], normed_grad)
        input_grad[image * SEQ : (image + 1) * SEQ, :] = wide[0:SEQ, :]


def finish_kernel(middle, part_a, part_b, part_c, out, wide):
    images = middle.shape[0] // ROWS
    for image in range(images):
        rows = slice(image * ROWS, (image + 1) * ROWS)
        part = part_a[0, rows, :].astype(F32) + part_b[0, rows, :].astype(F32)
        wide[...] = middle[rows, :] + (part + part_c[rows, :].astype(F32))
        out[image * SEQ : (image + 1) * SEQ, :] = wide[0:SEQ, :]


def swap(value, bit):
    size = lax.axis_size("tensor")
    return lax.ppermute(value, "tensor", [(at, at ^ bit) for at in range(size)])


def gather_four(value):
    core = swap(value, 1)
    side = swap(value, 2)
    return value, core, side, swap(side, 1)


def after(value, *others):
    return lax.optimization_barrier((value,) + others)[0]


def reduce_pair(keep, send):
    came = swap(send, 1)
    other = (keep[1].astype(F32) + came[1].astype(F32)).astype(BF16)
    return (keep, came, swap(other, 2)), other


def gather_projections(shards, extra, ids, others):
    size = lax.axis_size("dp")
    feats = shards.shape[1]
    if size == 8 and feats % 16 == 0:
        block = jnp.concatenate([shards.reshape(-1, 128), ids], 0)
        ring = Ring(jnp.stack([block, swap(block, 2)]))
        begun = ()
        for step in range(size // 2 - 1):
            ring.step(*(others[1:] if step == 2 else ()))
            begun += (ring.done,)
        parts = ring.finish()
        others = others[:1]
        return begun, *call(
            partial(assemble_kernel, size),
            (like((2, 5, size * feats, 128), BF16), like((size,) + ids.shape, BF16)),
            cost=cost(2),
        )(*parts, after(extra, *others), swap(extra, 2))
    whole = lax.all_gather(shards, "dp", axis=1, tiled=True)
    whole = jnp.concatenate([whole, extra[None]], 0)
    return ((),) * 3, jnp.stack([whole, swap(whole, 2)]), ids[None]


class Ring:
    def __init__(self, block):
        self.size = lax.axis_size("dp")
        self.block, self.parts, self.done = block, [], ()

    def along(self, value):
        size = self.size
        return lax.ppermute(value, "dp", [(at, (at + 2) % size) for at in range(size)])

    def across(self, value):
        return lax.ppermute(value, "dp", [(at, at ^ 1) for at in range(self.size)])

    def step(self, *waits, across=()):
        block = after(self.block, *self.done, *waits)
        self.done = self.along(block), self.across(after(block, *across))
        self.parts += [block, self.done[1]]
        self.block = self.done[0]

    def finish(self, *waits, split=None):
        if split is None:
            block = after(self.block, *self.done, *waits)
            return self.parts + [block, self.across(block)]
        passed, crossed = self.done
        return (
            self.parts + [passed],
            self.across(after(passed, *waits[:1])[:, :split]),
            lambda *waits: self.along(after(crossed, *waits)[:, split:]),
        )


class Whole:
    def __init__(self, block):
        self.parts = [lax.all_gather(block, "dp", axis=2, tiled=True)]
        self.done = ()

    def step(self, *waits, across=()):
        pass

    def finish(self, *waits, split=None):
        return self.parts, None, lambda *waits: None


def per_device(
    tokens,
    cotangent,
    norm_gain,
    qkv_weight,
    out_weight,
    expert_in,
    expert_out,
    router_weight,
    down_in,
    up_heads,
    up_hidden,
    up_router,
    down_heads,
    down_hidden,
    up_attn_out,
    up_expert_out,
    routes,
    priority,
    adapter_index,
):
    width = tokens.shape[1]
    local = tokens.shape[0]
    images = local // SEQ
    group_images = routes.shape[0] // SEQ
    count = images * ROWS
    tall = group_images * ROWS
    hidden = expert_in.shape[2]
    dp = lax.axis_size("dp")
    tensor = lax.axis_size("tensor")

    block = jnp.concatenate([qkv_weight, out_weight[None]], 0)
    ids = jnp.repeat(adapter_index.astype(BF16), CODE // adapter_index.shape[0])
    ids = jnp.broadcast_to(ids[None], (16, CODE))
    extra = jnp.concatenate(
        [
            up_heads.reshape(3 * CODE, up_heads.shape[3]),
            down_heads.swapaxes(1, 2).reshape(CODE, down_heads.shape[1]),
        ],
        0,
    )
    base = EXPERTS // 2
    fits = dp == 8 and expert_in.shape[1] % 16 == 0
    gather = Ring if fits else Whole
    early_ring = gather(jnp.stack([expert_in[:base], expert_out[:base]]))
    early_ring.step()
    late_block = jnp.stack([expert_in[base:], expert_out[base:]])

    down = down_in.swapaxes(2, 3).reshape(5, CODE, width)
    down_hid = down_hidden.swapaxes(1, 2).reshape(CODE, hidden)
    up_hid = up_hidden.reshape(CODE, hidden)
    up_out = up_attn_out.reshape(CODE, width)
    up_exo = up_expert_out.reshape(CODE, width)
    router = jnp.pad(jnp.tile(router_weight.T, (2, 1)), ((0, 128 - 2 * EXPERTS), (0, 0)))
    router_up = up_router.transpose(2, 0, 1).reshape(EXPERTS, CODE)
    router_up = jnp.pad(jnp.tile(router_up, (2, 1)), ((0, 128 - 2 * EXPERTS), (0, 0)))

    spare = ROWS - SEQ
    route_row = jnp.pad(
        routes.T.reshape(2, group_images, SEQ), ((0, 0), (0, 0), (0, spare)), constant_values=-1
    ).reshape(2, tall)
    rank_row = jnp.pad(
        priority.reshape(group_images, SEQ), ((0, 0), (0, spare)), constant_values=1 << 20
    ).reshape(1, tall)
    chunk_units = (2 * count + EXPERTS * (UNIT - 1)) // UNIT
    expert_units = -(-CAP // UNIT) + 4
    by_chunk = lambda value: value.reshape(-1, tensor, count).swapaxes(0, 1)
    dy, place, table = call(
        route_kernel,
        (
            like((count, width), BF16),
            like((tensor, 2, count), F32),
            like((2 * EXPERTS, 128), jnp.int32),
        ),
        scratch=[pltpu.VMEM((count, width), F32)],
        cost=cost(5),
    )(cotangent, route_row, by_chunk(route_row), by_chunk(rank_row), rank_row.T)
    dy_four = gather_four(dy)
    begun, mine, ids = gather_projections(block, extra, ids, (dy_four[2],) + early_ring.done)
    early_ring.step(*begun[1])
    late_ring = gather(after(late_block, *begun[2]))
    late_ring.step()
    other = swap(mine, 1)

    (
        weights, x, normed, code, qkv, prob, mixed, hcode, middle, normed2,
    ) = call(
        forward_kernel,
        (
            like((5, width, width), BF16),
            like((count, width), F32),
            like((count, width), BF16),
            like((count, 3 * CODE), BF16),
            like((count, 3 * width), BF16),
            like((images * HEADS, ROWS, ROWS), F32),
            like((count, width), BF16),
            like((count, CODE), BF16),
            like((count, width), F32),
            like((count, width), BF16),
        ),
        scratch=[pltpu.VMEM((count, width), F32)],
        smem=1,
        cost=cost(10),
        vmem=56,
    )(adapter_index, tokens, norm_gain, mine, other, down, up_out)

    normed2_four = gather_four(normed2)
    normed2_four = (after(normed2, *early_ring.done),) + normed2_four[1:]
    early_ring.step(normed2)
    late_ring.step(normed2_four[2])
    row_wide = 2 * width + 128
    chunk_slots = chunk_units * UNIT
    expert_slots = expert_units * UNIT
    slots, rows, rcode, probs = call(
        dispatch_kernel,
        (
            like((EXPERTS, expert_slots, row_wide), BF16),
            like((tensor, count, width), BF16),
            like((tensor, count, CODE), BF16),
            like((tensor, count, 128), F32),
        ),
        scratch=[
            pltpu.VMEM((tensor, count, row_wide), BF16),
            pltpu.VMEM((chunk_slots, row_wide), BF16),
        ],
        smem=2,
        cost=cost(17),
    )(adapter_index, table, *normed2_four, *dy_four, place, down, router, router_up)

    part = base // 2
    common, near, far = early_ring.finish(slots, split=part)
    far = far(slots)
    ready = late_ring.done
    late_ring.step(slots, across=(near, far) if fits else ())
    whole = lambda *shape: pl.BlockSpec(shape, lambda step: (0,) * len(shape))
    smem = pl.BlockSpec(memory_space=pltpu.SMEM)
    vmem = pl.BlockSpec(memory_space=pltpu.VMEM)
    hbm = pl.BlockSpec(memory_space=pltpu.HBM)
    joined = [
        pltpu.VMEM((2, 2, width, hidden), BF16),
        pltpu.SemaphoreType.DMA((2, 8 if fits else 1)),
    ]
    each = lambda wide, first: pl.BlockSpec(
        (1, expert_slots, wide), lambda step: (step + first, 0, 0)
    )
    small = [
        whole(CODE, hidden), whole(CODE, hidden), whole(CODE, width), whole(5, CODE, width),
    ]
    sums = [whole(2, CODE, hidden), whole(2, CODE, width)]
    grad_wide = width + 128

    def experts(parts, pieces, count, first, at, slots, before=()):
        return call(
            partial(expert_kernel, len(parts), pieces, count, first, at),
            (
                like((count, expert_slots, grad_wide), BF16),
                like((count, expert_slots, width), BF16),
                like((2, CODE, hidden), F32),
                like((2, CODE, width), F32),
            ),
            scratch=joined,
            grid=(count,),
            in_specs=[hbm] * len(parts) + [each(row_wide, at)] + small + sums[: len(before)],
            out_specs=(each(grad_wide, 0), each(width, 0), *sums),
            cost=cost(4 * count),
        )(*parts, slots, up_hid, down_hid, up_exo, down, *before)

    near, pieces = ([near], (0,)) if fits else ([], ())
    grad_a, mix_a, *before = experts(
        common + near, pieces, part, 0, 0, after(slots, *ready)
    )
    far, pieces = ([far], (part,)) if fits else ([], ())
    grad_b, mix_b, *before = experts(
        common + far, pieces, base - part, part, part, after(slots, *late_ring.done), before
    )
    common, near, far = late_ring.finish(grad_a, split=part)
    halves, pieces = ([near, far(grad_a)], (0, part)) if fits else ([], ())
    count_last = EXPERTS - base
    half = like((2, count, width), BF16)
    compact = dp == 8 and images == 2 and hidden == width == 512
    place = place.swapaxes(1, 2)
    last_parts = common + halves
    mix_c, grad_keep, grad_send, early = call(
        partial(last_kernel, len(last_parts), pieces, count_last, 0, base),
        (
            like((count_last, expert_slots, width), BF16),
            half, half,
            like((8, 96, width), BF16) if compact else like((6, CODE, width), F32),
        ),
        scratch=joined
        + [
            pltpu.VMEM((EXPERTS, expert_slots, grad_wide), BF16),
            pltpu.VMEM((2, CODE, hidden), F32),
            pltpu.VMEM((2, CODE, width), F32),
            pltpu.VMEM((2, CODE, width), F32),
            pltpu.VMEM((chunk_slots, grad_wide), BF16),
            pltpu.VMEM((tensor, count, width), BF16),
            pltpu.VMEM((tensor, count, CODE), BF16),
            pltpu.VMEM((tensor, count, 128), F32),
            pltpu.SemaphoreType.DMA((5,)),
        ],
        grid=(count_last,),
        in_specs=[hbm] * len(last_parts)
        + [each(row_wide, base)]
        + small
        + sums
        + [smem] * 2
        + [whole(tensor, count, 2), whole(128, width), whole(128, CODE)]
        + [hbm] * 5,
        out_specs=(
            each(width, 0), whole(2, count, width), whole(2, count, width),
            whole(8, 96, width) if compact else whole(6, CODE, width),
        ),
        cost=cost(25),
    )(
        *last_parts, slots, up_hid, down_hid, up_exo, down, *before,
        adapter_index, table, place, router, router_up, grad_a, grad_b, rows, rcode, probs,
    )
    mix_keep, mix_send = call(
        mix_kernel,
        (half, half),
        scratch=[pltpu.VMEM((chunk_slots, width), BF16)],
        in_specs=[smem] + [vmem] * 4,
        out_specs=(vmem, vmem),
        cost=cost(7),
    )(table, place, mix_a, mix_b, mix_c)

    both = ("dp", "tensor")
    grads, begun = reduce_pair(grad_keep, grad_send)
    if compact:
        early = lax.all_to_all(after(early, begun), "dp", 0, 0)

    middle_grad, proj_grad, code_grad, late = call(
        backward_kernel,
        (
            like((count, width), F32),
            like((count, 3 * width), BF16),
            like((count, 3 * CODE), BF16),
            like((32, images * RANK, 128), BF16) if compact else like((8, CODE, width), F32),
        ),
        scratch=[pltpu.VMEM((ROWS, width), BF16), pltpu.VMEM((8, CODE, width), F32)],
        smem=1,
        cost=cost(11),
        vmem=56,
    )(
        adapter_index, after(dy, mix_send), middle, *grads, norm_gain, weights, up_out,
        normed, code, qkv, prob, mixed, hcode,
    )
    if compact:
        came = lax.all_to_all(late, both, 0, 0)
    mixes, unused = reduce_pair(mix_keep, after(mix_send, late))
    input_grad = call(
        input_kernel,
        like((local, width), F32),
        scratch=[pltpu.VMEM((ROWS, width), F32)],
        cost=cost(5),
        vmem=56,
    )(middle_grad, proj_grad, code_grad, x, norm_gain, weights, down)
    block_out = call(
        finish_kernel,
        like((local, width), F32),
        scratch=[pltpu.VMEM((ROWS, width), F32)],
        cost=cost(2),
    )(after(middle, late), *mixes)

    if compact:
        keep = like((2, 16, width), BF16)
        keep, send, early_hid = call(
            early_sum_kernel, (keep, keep, like((32, width), BF16)), cost=cost(2)
        )(after(early, late))
        sums, unused = reduce_pair(keep, send)
        packed = call(late_sum_kernel, like((dp, 80, width), BF16), cost=cost(2))(
            came.reshape(dp, CODE, 128), ids, early_hid, *sums
        )
        came = lax.all_to_all(packed, "dp", 0, 0)
        came = after(came, input_grad, block_out)
        mine = jnp.concatenate(
            [came[4:, 48:].reshape(128, width), came[:, 32:48].reshape(128, width)], 0
        )
        whole = like((CODE, width), F32)
        (
            grad_down_in, grad_up_out, grad_up_exo, router_grad,
            grad_up_heads, grad_down_heads, grad_up_hidden, grad_down_hidden,
        ) = call(
            unpack_kernel,
            (
                like((5, CODE, width), F32), whole, whole, like((ADAPTERS, EXPERTS, RANK), F32),
                like((3, CODE, 128), F32), like((CODE, 128), F32), whole, whole,
            ),
            scratch=[pltpu.VMEM((CODE, width), F32)],
            cost=cost(3),
        )(came, *gather_four(mine))
    else:
        cols = width // tensor
        early_shared = lax.psum(early[:4], both)
        early_hid = lax.psum(early[4:], "dp")
        late = lax.psum(late, both)
        late_heads = lax.dynamic_slice_in_dim(
            late[:4], lax.axis_index("tensor") * cols, cols, 2
        )
        grad_down_in = jnp.concatenate([late[4:7], early_shared[:2]], 0)
        grad_up_out, grad_up_exo = late[7], early_shared[2]
        router_grad = early_shared[3, :, :CODE]
        router_grad = router_grad[:EXPERTS] + router_grad[EXPERTS : 2 * EXPERTS]
        router_grad = router_grad.reshape(EXPERTS, ADAPTERS, RANK).swapaxes(0, 1)
        grad_up_heads, grad_down_heads = late_heads[:3], late_heads[3]
        grad_up_hidden, grad_down_hidden = early_hid[0], early_hid[1]
    split_up = lambda value: value.reshape(value.shape[:-2] + (ADAPTERS, RANK, value.shape[-1]))
    split_down = lambda value: split_up(value).swapaxes(-1, -2)
    grad_down_in = split_down(grad_down_in)
    grad_up_out = split_up(grad_up_out)
    grad_up_exo = split_up(grad_up_exo)
    grad_up_router = router_grad.swapaxes(1, 2)
    grad_up_heads = split_up(grad_up_heads)
    grad_down_heads = split_down(grad_down_heads)
    grad_up_hidden = split_up(grad_up_hidden)
    grad_down_hidden = split_down(grad_down_hidden)
    return (
        block_out,
        input_grad,
        grad_down_in,
        grad_up_heads,
        grad_up_hidden,
        grad_up_router,
        grad_down_heads,
        grad_down_hidden,
        grad_up_out,
        grad_up_exo,
    )


def solution(mesh):
    placed = (
        P(("dp", "tensor"), None),
        P(("dp", "tensor"), None),
        P(),
        P(None, "dp", "tensor"),
        P("dp", "tensor"),
        P(None, "dp", "tensor"),
        P(None, "dp", "tensor"),
        P(),
        P(),
        P(None, None, None, "tensor"),
        P(None, None, "tensor"),
        P(),
        P(None, "tensor", None),
        P(None, "tensor", None),
        P(),
        P(),
        P("dp", None),
        P("dp", None),
        P("dp"),
    )
    return jax.shard_map(
        per_device,
        mesh=mesh,
        in_specs=placed,
        out_specs=(
            P(("dp", "tensor"), None),
            P(("dp", "tensor"), None),
            P(),
            P(None, None, None, "tensor"),
            P(None, None, "tensor"),
            P(),
            P(None, "tensor", None),
            P(None, "tensor", None),
            P(),
            P(),
        ),
        check_vma=False,
    )
```

```python
from functools import partial

import jax
import jax.numpy as jnp
from jax import lax
from jax.experimental import pallas as pl
from jax.experimental.pallas import tpu as pltpu
from jax.sharding import PartitionSpec as P

HEADS = 8
RANK = 16
ADAPTERS = 8
SEQ = 197
EXPERTS = 8
HEAD_DIM = 64
CAP = 394

EPS = 1e-06
CODE = ADAPTERS * RANK
ROWS = 208
UNIT = 16
SCALE = HEAD_DIM ** (-0.5)
F32 = jnp.float32
BF16 = jnp.bfloat16
MIB = 1024 * 1024


def dot(left, right):
    return lax.dot_general(left, right, (((1,), (0,)), ((), ())), preferred_element_type=F32)


def dot_t(left, right):
    return lax.dot_general(left, right, (((1,), (1,)), ((), ())), preferred_element_type=F32)


def tdot(left, right):
    return lax.dot_general(left, right, (((0,), (0,)), ((), ())), preferred_element_type=F32)


def lanes(shape):
    return lax.broadcasted_iota(jnp.int32, shape, len(shape) - 1)


def sublanes(shape):
    return lax.broadcasted_iota(jnp.int32, shape, len(shape) - 2)


def norm_rows(value, gain):
    center = value - jnp.mean(value, -1, keepdims=True)
    spread = jnp.mean(center * center, -1, keepdims=True)
    return center * lax.rsqrt(spread + EPS) * gain


def norm_back(value, gain, grad):
    center = value - jnp.mean(value, -1, keepdims=True)
    rate = lax.rsqrt(jnp.mean(center * center, -1, keepdims=True) + EPS)
    unit = center * rate
    grad = grad * gain
    along = jnp.mean(grad * unit, -1, keepdims=True)
    return rate * (grad - jnp.mean(grad, -1, keepdims=True) - unit * along)


def gelu_pair(value):
    square = value * value
    inner = 0.7978845608028654 * value * (1.0 + 0.044715 * square)
    bent = jnp.tanh(inner)
    half = 0.5 * (1.0 + bent)
    slope = half + 0.5 * value * (1.0 - bent * bent) * (
        0.7978845608028654 * (1.0 + 3.0 * 0.044715 * square)
    )
    return value * half, slope


def call(
    body, outs, scratch=(), smem=0, grid=None, in_specs=None, out_specs=None, cost=None, vmem=16
):
    options = {}
    if grid is not None:
        options = dict(grid=grid, in_specs=in_specs, out_specs=out_specs)
    elif in_specs is not None:
        options = dict(in_specs=in_specs, out_specs=out_specs)
    elif smem:
        def build(*args):
            specs = [pl.BlockSpec(memory_space=pltpu.SMEM)] * smem
            specs += [pl.BlockSpec(memory_space=pltpu.VMEM)] * (len(args) - smem)
            if isinstance(outs, tuple):
                ends = (pl.BlockSpec(memory_space=pltpu.VMEM),) * len(outs)
            else:
                ends = pl.BlockSpec(memory_space=pltpu.VMEM)
            return call(body, outs, scratch, 0, None, specs, ends, cost, vmem)(*args)

        return build
    return pl.pallas_call(
        body,
        out_shape=outs,
        scratch_shapes=list(scratch),
        compiler_params=pltpu.CompilerParams(vmem_limit_bytes=vmem * MIB),
        cost_estimate=cost,
        **options,
    )


def like(shape, dtype):
    return jax.ShapeDtypeStruct(shape, dtype)


def cost(micros):
    return pl.CostEstimate(
        flops=int(micros * 1.1e9), bytes_accessed=int(micros * 3.6e6), transcendentals=0
    )


def image_mask(adapter, index):
    return jnp.where(lanes((1, CODE)) // RANK == adapter[index], 1.0, 0.0)


def route_kernel(cot, rflat, rrow, prow, pcol, dy, place_out, table_out, wide):
    images = dy.shape[0] // ROWS
    chunks, unused, count = rrow.shape
    wide[...] = jnp.zeros_like(wide)
    wide[0 : cot.shape[0], :] = cot[...].astype(F32)
    for image in range(images):
        part = wide[image * SEQ : image * SEQ + ROWS, :]
        part = jnp.where(sublanes((ROWS, 1)) < SEQ, part, 0.0)
        dy[image * ROWS : (image + 1) * ROWS, :] = part.astype(BF16)
    kinds = sublanes((2 * EXPERTS, rflat.shape[1]))
    first = jnp.where(rflat[0:1, :] == kinds, 1.0, 0.0)
    second = jnp.where(rflat[1:2, :] == kinds, 1.0, 0.0)
    first_all = jnp.sum(first, axis=1, keepdims=True)
    first = first.astype(BF16)
    second = second.astype(BF16)
    kinds = sublanes((2 * EXPERTS, count))
    above = jnp.where(sublanes((count, count)) < lanes((count, count)), 1.0, 0.0).astype(BF16)
    square = (2 * EXPERTS, 2 * EXPERTS)
    below = jnp.where(lanes(square) < sublanes(square), 1.0, 0.0).astype(BF16)
    lane = lanes((2 * EXPERTS, 128))
    table = jnp.zeros((2 * EXPERTS, 128), F32)
    filled = jnp.zeros((2 * EXPERTS, 1), F32)
    for chunk in range(chunks):
        earlier = jnp.where(pcol[...] < prow[chunk], 1.0, 0.0).astype(BF16)
        is_first = rrow[chunk, 0:1, :] == kinds
        is_second = rrow[chunk, 1:2, :] == kinds
        place = jnp.where(is_first, dot(first, earlier), 1e9)
        place = jnp.where(is_second, dot(second, earlier) + first_all, place)
        kept = place < CAP
        held = jnp.where(kept, 1.0, 0.0)
        rank = dot(held.astype(BF16), above)
        units = jnp.sum(held, axis=1, keepdims=True)
        units = jnp.floor((units + (UNIT - 1)) * (1.0 / UNIT))
        start = dot(below, jnp.broadcast_to(units, (2 * EXPERTS, 128)).astype(BF16))[:, 0:1]
        spot = jnp.where(kept, start * UNIT + rank + 1.0, 0.0)
        place_out[chunk, 0:1, :] = (
            jnp.sum(jnp.where(is_first, spot, 0.0), axis=0, keepdims=True) - 1.0
        )
        place_out[chunk, 1:2, :] = (
            jnp.sum(jnp.where(is_second, spot, 0.0), axis=0, keepdims=True) - 1.0
        )
        table = jnp.where(lane == chunk, units, table)
        table = jnp.where(lane == chunks + chunk, start, table)
        table = jnp.where(lane == 2 * chunks + chunk, filled, table)
        filled = filled + units
    table = jnp.where(lane == 3 * chunks, filled, table)
    table_out[...] = table.astype(jnp.int32)


def assemble_kernel(count, *refs):
    parts, (extra, other_extra, out, ids) = refs[:count], refs[count:]
    feats = out.shape[2] // count
    out[0, 4] = extra[...]
    out[1, 4] = other_extra[...]
    for step, owner in enumerate(block_owners(count)):
        rows = pl.ds(pl.multiple_of(owner * feats, feats), feats)
        for side in range(2):
            for member in range(4):
                out[side, member, rows, :] = parts[step][
                    side, member * feats : (member + 1) * feats, :
                ]
        ids[owner] = parts[step][0, 4 * feats : 4 * feats + 16, :]


def forward_kernel(
    adapter, tokens, gain, mine, other, down, up_out,
    weights, x_out, normed_out, code_out, qkv_out, prob_out, mixed_out, hcode_out,
    middle_out, normed2_out, wide,
):
    me = lax.axis_index("tensor")
    for step in range(4):
        cols = pl.ds(pl.multiple_of(lax.bitwise_xor(me, step) * 128, 128), 128)
        weights[:, :, cols] = (mine, other)[step % 2][step // 2]
    images = x_out.shape[0] // ROWS
    width = tokens.shape[1]
    wide[...] = jnp.zeros_like(wide)
    wide[0 : tokens.shape[0], :] = tokens[...].astype(F32)
    for image in range(images):
        at = image * ROWS
        rows = slice(at, at + ROWS)
        mask = image_mask(adapter, me * images + image)
        real = sublanes((ROWS, 1)) < SEQ
        x = jnp.where(real, wide[image * SEQ : image * SEQ + ROWS, :], 0.0)
        x_out[rows, :] = x
        normed = norm_rows(x, gain[0:1, :]).astype(BF16)
        normed_out[rows, :] = normed
        for member in range(3):
            code = (mask * dot_t(normed, down[member])).astype(BF16)
            code_out[rows, member * CODE : (member + 1) * CODE] = code
            up = weights[4, member * CODE : (member + 1) * CODE, :]
            proj = dot(normed, weights[member]) + dot(code, up)
            qkv_out[rows, member * width : (member + 1) * width] = proj.astype(BF16)
        low_half = lanes((1, 128)) < HEAD_DIM
        half = (low_half, jnp.logical_not(low_half))
        real_key = lanes((1, ROWS)) < SEQ
        for pair in range(HEADS // 2):
            cols = pair * 128
            q = qkv_out[rows, cols : cols + 128].astype(F32) * SCALE
            k = qkv_out[rows, width + cols : width + cols + 128]
            v = qkv_out[rows, 2 * width + cols : 2 * width + cols + 128].astype(F32)
            mixed = jnp.zeros((ROWS, 128), F32)
            for head in range(2):
                score = dot_t(jnp.where(half[head], q, 0.0).astype(BF16), k)
                score = jnp.where(real_key, score, -1e30)
                raised = jnp.exp(score - jnp.max(score, -1, keepdims=True))
                prob = raised / jnp.sum(raised, -1, keepdims=True)
                prob_out[(image * HEADS // 2 + pair) * 2 + head] = prob
                mixed = mixed + dot(
                    prob.astype(BF16), jnp.where(half[head], v, 0.0).astype(BF16)
                )
            mixed_out[rows, cols : cols + 128] = mixed.astype(BF16)
        mixed = mixed_out[rows, :]
        hcode = (mask * dot_t(mixed, weights[4, 3 * CODE : 4 * CODE, :])).astype(BF16)
        hcode_out[rows, :] = hcode
        middle = x + dot_t(mixed, weights[3]) + dot(hcode, up_out[...])
        middle_out[rows, :] = middle
        normed2_out[rows, :] = norm_rows(middle, gain[1:2, :]).astype(BF16)


def row_adapters(adapter, chunk, count):
    images = count // ROWS
    which = jnp.zeros((count, 1), jnp.int32)
    for image in range(images):
        which = jnp.where(
            sublanes((count, 1)) // ROWS == image, adapter[chunk * images + image], which
        )
    return which


def move_units(table, chunk, expert, chunk_ref, expert_ref, forward):
    start = table[expert, 4 + chunk]
    target = table[expert, 8 + chunk]

    count = table[expert, chunk]

    def move(unit, units):
        here = pl.ds(pl.multiple_of((start + unit) * UNIT, UNIT), units * UNIT)
        there = pl.ds(pl.multiple_of((target + unit) * UNIT, UNIT), units * UNIT)
        if forward:
            expert_ref[there, :] = chunk_ref[here, :]
        else:
            chunk_ref[here, :] = expert_ref[there, :]

    def four(step, carry):
        move(4 * step, 4)
        return carry

    lax.fori_loop(0, lax.shift_right_logical(count, 2), four, 0)

    @pl.when(lax.bitwise_and(count, 2) != 0)
    def _():
        move(count - lax.bitwise_and(count, 3), 2)

    @pl.when(lax.bitwise_and(count, 1) != 0)
    def _():
        move(count - 1, 1)


def clear_units(ref, start):
    def clear(unit, carry):
        rows = pl.ds(pl.multiple_of(unit * UNIT, UNIT), UNIT)
        ref[rows, :] = jnp.zeros((UNIT, ref.shape[1]), ref.dtype)
        return carry

    lax.fori_loop(start, ref.shape[0] // UNIT, clear, 0)


def dispatch_kernel(
    adapter, table, own, core, side, both, dy_near, dy_far,
    place, down, router, up_router,
    slots, normed_out, rcode_out, prob_out, rows, packed,
):
    me = lax.axis_index("tensor")
    count = own.shape[0]
    width = own.shape[1]
    lane = lanes((1, 128))
    for index, (part, dy) in enumerate(
        (
            (own, dy_near.at[0]), (core, dy_far.at[0]),
            (side, dy_near.at[1]), (both, dy_far.at[1]),
        )
    ):
        normed_out[index] = part[...]
        rows[index, :, 0:width] = part[...]
        rows[index, :, width : 2 * width] = dy[...]

    def each(index, carry):
        chunk = lax.bitwise_xor(me, index)
        which = row_adapters(adapter, chunk, count)
        mask = jnp.where(lane // RANK == which, 1.0, 0.0)
        normed = rows[index, :, 0:width]
        rcode = (mask * dot_t(normed, down[4])).astype(BF16)
        rcode_out[index] = rcode
        logits = dot_t(normed, router[...]) + dot_t(rcode, up_router[...])
        logits = jnp.where(lane < 2 * EXPERTS, logits, -1e30)
        raised = jnp.exp(logits - jnp.max(logits, -1, keepdims=True))
        mass = jnp.sum(jnp.where(lane < EXPERTS, raised, 0.0), -1, keepdims=True)
        prob = raised / mass
        prob_out[index] = prob
        high = prob.astype(BF16).astype(F32)
        aux = jnp.where(lane < EXPERTS, high, prob - high)
        aux = jnp.where(lane < 2 * EXPERTS, aux, jnp.where(lane == 16 + which, 1.0, 0.0))
        rows[index, :, 2 * width : 2 * width + 128] = aux.astype(BF16)
        spot = sublanes((packed.shape[0], count)).astype(F32)
        chosen = jnp.logical_or(spot == place[chunk, 0:1, :], spot == place[chunk, 1:2, :])
        chosen = jnp.where(chosen, 1.0, 0.0).astype(BF16)
        packed[...] = dot(chosen, rows[index]).astype(BF16)

        def spread(expert, carry):
            move_units(table, chunk, expert, packed, slots.at[expert], True)
            return carry

        return lax.fori_loop(0, EXPERTS, spread, carry)

    lax.fori_loop(0, 4, each, 0)

    def clear(expert, carry):
        clear_units(slots.at[expert], table[expert, 12])
        return carry

    lax.fori_loop(0, EXPERTS, clear, 0)


def expert_body(
    expert, slots, w_in, w_out, up_hid, down_hid, up_exo, down, g_hid, g_exo, grad_out, mix_out
):
    width = w_in.shape[0]
    lane = lanes((1, 128))
    x = slots[:, 0:width]
    dy = slots[:, width : 2 * width].astype(F32)
    aux = slots[:, 2 * width : 2 * width + 128]
    expand = jnp.where(sublanes((128, CODE)) - 16 == lanes((128, CODE)) // RANK, 1.0, 0.0)
    mask = dot(aux, expand.astype(BF16))
    here = jnp.logical_and(lax.rem(lane, EXPERTS) == expert, lane < 2 * EXPERTS)
    gate = jnp.sum(jnp.where(here, aux.astype(F32), 0.0), -1, keepdims=True)
    hcode = (mask * dot_t(x, down[3])).astype(BF16)
    before = dot(x, w_in[...]) + dot(hcode, up_hid[...])
    active, slope = gelu_pair(before)
    active = active.astype(BF16)
    ocode = (mask * dot_t(active, down_hid[...])).astype(BF16)
    returned = dot_t(active, w_out[...]) + dot(ocode, up_exo[...])
    gate_grad = jnp.sum(returned * dy, -1, keepdims=True)
    back = (gate * dy).astype(BF16)
    ocode_grad = (mask * dot_t(back, up_exo[...])).astype(BF16)
    active_grad = dot(back, w_out[...]) + dot(ocode_grad, down_hid[...])
    before_grad = (slope * active_grad).astype(BF16)
    hcode_grad = (mask * dot_t(before_grad, up_hid[...])).astype(BF16)
    x_grad = dot_t(before_grad, w_in[...]) + dot(hcode_grad, down[3])
    g_hid[0] += tdot(hcode, before_grad)
    g_hid[1] += tdot(ocode_grad, active)
    g_exo[0] += tdot(hcode_grad, x)
    g_exo[1] += tdot(ocode, back)
    high = gate_grad.astype(BF16).astype(F32)
    spread = jnp.where(here, jnp.where(lane < EXPERTS, high, gate_grad - high), 0.0)
    mix_out[...] = (gate * returned).astype(BF16)
    grad_out[:, 0:width] = x_grad.astype(BF16)
    grad_out[:, width : width + 128] = spread.astype(BF16)


def fetch_weights(parts, pieces, joined, sems, step, count, first):
    common = len(parts) - len(pieces)
    owners = block_owners(common + 1 if pieces else common)
    feats = parts[0].shape[2]
    slot = lax.rem(step, 2)

    def copies(part, expert, slot, place):
        rows = pl.ds(pl.multiple_of(owners[place] * feats, feats), feats)
        return pltpu.make_async_copy(
            part.at[:, expert], joined.at[slot, :, rows, :], sems.at[slot, place]
        )

    def start(expert, slot):
        for place in range(common):
            copies(parts[place], expert, slot, place).start()
        for part, begin in zip(parts[common:], pieces):

            @pl.when(jnp.logical_and(expert >= begin, expert < begin + part.shape[1]))
            def _():
                copies(part, expert - begin, slot, common).start()

    @pl.when(step == 0)
    def _():
        start(step + first, 0)

    @pl.when(step + 1 < count)
    def _():
        start(step + 1 + first, 1 - slot)

    for place in range(len(owners)):
        copies(parts[place], 0, slot, place).wait()
    return joined.at[slot, 0], joined.at[slot, 1]


def block_owners(size):
    me = lax.axis_index("dp")
    if size == 1:
        return (0,)
    owners = []
    for step in range(size // 2):
        owner = lax.rem(me - 2 * step + size, size)
        owners += [owner, lax.bitwise_xor(owner, 1)]
    return owners


def expert_kernel(size, pieces, count, first, base, *refs):
    parts, refs = refs[:size], refs[size:]
    slots, up_hid, down_hid, up_exo, down, *before, grad_out, mix_out = refs[:-4]
    g_hid, g_exo, joined, sems = refs[-4:]
    step = pl.program_id(0)

    @pl.when(step == 0)
    def _():
        g_hid[...] = before[0][...] if before else jnp.zeros_like(g_hid)
        g_exo[...] = before[1][...] if before else jnp.zeros_like(g_exo)

    w_in, w_out = fetch_weights(parts, pieces, joined, sems, step, count, first)
    expert_body(
        step + base, slots.at[0], w_in, w_out, up_hid, down_hid, up_exo, down,
        g_hid, g_exo, grad_out.at[0], mix_out.at[0],
    )


def collect_chunk(table, chunk, sources, packed):
    base = 0
    for source in sources:

        def collect(expert, carry, source=source, base=base):
            move_units(table, chunk, expert + base, packed, source.at[expert], False)
            return carry

        lax.fori_loop(0, source.shape[0], collect, 0)
        base += source.shape[0]
    ending = EXPERTS - 1
    clear_units(packed, table[ending, 4 + chunk] + table[ending, chunk])


def chosen_slots(place, chunk, packed):
    shape = (place.shape[1], packed.shape[0])
    spot = lanes(shape).astype(F32)
    chosen = jnp.logical_or(spot == place[chunk, :, 0:1], spot == place[chunk, :, 1:2])
    return jnp.where(chosen, 1.0, 0.0).astype(BF16)


def last_kernel(size, pieces, count, first, base, *refs):
    parts, refs = refs[:size], refs[size:]
    (
        slots, up_hid, down_hid, up_exo, down, g_hid_before, g_exo_before,
        adapter, table, place, router, up_router, *waiting,
    ) = refs[:-15]
    (
        mix_out, grad_keep, grad_send, grads_out,
        joined, sems, collected, g_hid, g_exo, g_router, packed, normed, rcode, prob, came,
    ) = refs[-15:]
    step = pl.program_id(0)
    width = down.shape[2]
    lane = lanes((1, 128))
    targets, at = [], 0
    for source in waiting[:-3]:
        targets.append(collected.at[at : at + source.shape[0]])
        at += source.shape[0]
    targets += [normed, rcode, prob]
    arrivals = [
        pltpu.make_async_copy(source, target, came.at[index])
        for index, (source, target) in enumerate(zip(waiting, targets))
    ]

    @pl.when(step == 0)
    def _():
        g_hid[...] = g_hid_before[...]
        g_exo[...] = g_exo_before[...]
        g_router[...] = jnp.zeros_like(g_router)
        for arrival in arrivals:
            arrival.start()

    w_in, w_out = fetch_weights(parts, pieces, joined, sems, step, count, first)
    expert_body(
        step + base, slots.at[0], w_in, w_out, up_hid, down_hid, up_exo, down,
        g_hid, g_exo, collected.at[step + base], mix_out.at[0],
    )

    @pl.when(step == count - 1)
    def _():
        me = lax.axis_index("tensor")
        tall = normed.shape[1]
        for arrival in arrivals:
            arrival.wait()

        def combine(index, grad_out):
            chunk = lax.bitwise_xor(me, index)
            collect_chunk(table, chunk, [collected], packed)
            total = dot(chosen_slots(place, chunk, packed), packed[...])
            mask = jnp.where(lane // RANK == row_adapters(adapter, chunk, tall), 1.0, 0.0)
            gates = total[:, width : width + 128]
            probs = jnp.where(lane < 2 * EXPERTS, prob[index], 0.0)
            mean = jnp.sum(probs * gates, -1, keepdims=True)
            logit = (probs * (gates - jnp.where(lane < EXPERTS, mean, 0.0))).astype(BF16)
            rcode_grad = (mask * dot(logit, up_router[...])).astype(BF16)
            grad = total[:, 0:width] + dot(logit, router[...])
            grad = grad + dot(rcode_grad, down[4])
            grad_out[...] = grad.astype(BF16)
            g_router[0] += tdot(rcode_grad, normed[index])
            g_router[1, :, 0:128] += tdot(logit, rcode[index])

        def pair(half, carry):
            combine(2 * half, grad_keep.at[half])
            combine(2 * half + 1, grad_send.at[half])
            return carry

        lax.fori_loop(0, 2, pair, 0)
        shared = (g_exo.at[0], g_router.at[0], g_exo.at[1], g_router.at[1])
        if grads_out.dtype == F32:
            for member in range(4):
                grads_out[member] = shared[member][...]
            grads_out[4:6] = g_hid[...]
            return
        for owner in range(8):
            member, at = divmod(owner * 64, CODE)
            grads_out[owner, 0:64, :] = shared[member][at : at + 64, :].astype(BF16)
            member, at = divmod(owner * 32, CODE)
            grads_out[owner, 64:96, :] = g_hid[member, at : at + 32, :].astype(BF16)


def mix_kernel(table, place, *refs):
    sources, (mix_keep, mix_send, packed) = refs[:-3], refs[-3:]
    me = lax.axis_index("tensor")

    def combine(index, mix_out):
        chunk = lax.bitwise_xor(me, index)
        collect_chunk(table, chunk, sources, packed)
        mix_out[...] = dot(chosen_slots(place, chunk, packed), packed[...]).astype(BF16)

    def pair(half, carry):
        combine(2 * half, mix_keep.at[half])
        combine(2 * half + 1, mix_send.at[half])
        return carry

    lax.fori_loop(0, 2, pair, 0)


def backward_kernel(
    adapter, dy, middle, grad_a, grad_b, grad_c, gain, weights, up_out,
    normed_in, code_in, qkv_in, prob_in, mixed_in, hcode_in,
    middle_grad_out, proj_grad, code_grad_out, grads_out, mixed_grad, whole,
):
    me = lax.axis_index("tensor")
    images = dy.shape[0] // ROWS
    width = dy.shape[1]
    compact = grads_out.shape[0] == 32

    def keep(image, member, grad):
        if not compact:
            grads_out[member] = grad if image == 0 else grads_out[member] + grad
            return
        whole[member] = grad
        start = pl.multiple_of(adapter[me * images + image] * RANK, RANK)
        rows = whole[member, pl.ds(start, RANK), :].astype(BF16)
        for block in range(4):
            grads_out[member * 4 + block, image * RANK : (image + 1) * RANK, :] = rows[
                :, block * 128 : (block + 1) * 128
            ]

    for image in range(images):
        at = image * ROWS
        rows = slice(at, at + ROWS)
        mask = image_mask(adapter, me * images + image)
        summed = grad_a[0, rows, :].astype(F32) + grad_b[0, rows, :].astype(F32)
        summed = summed + grad_c[rows, :].astype(F32)
        middle_grad = dy[rows, :].astype(F32) + norm_back(
            middle[rows, :], gain[1:2, :], summed
        )
        middle_grad_out[rows, :] = middle_grad
        low = middle_grad.astype(BF16)
        hcode_grad = (mask * dot_t(low, up_out[...])).astype(BF16)
        down_heads = weights[4, 3 * CODE : 4 * CODE, :]
        mixed_grad[...] = (dot(low, weights[3]) + dot(hcode_grad, down_heads)).astype(BF16)
        keep(image, 7, tdot(hcode_in[rows, :], low))
        keep(image, 3, tdot(hcode_grad, mixed_in[rows, :]))
        low_half = lanes((1, 128)) < HEAD_DIM
        half = (low_half, jnp.logical_not(low_half))
        for pair in range(HEADS // 2):
            cols = pair * 128
            q = qkv_in[rows, cols : cols + 128].astype(F32) * SCALE
            k = qkv_in[rows, width + cols : width + cols + 128].astype(F32) * SCALE
            v = qkv_in[rows, 2 * width + cols : 2 * width + cols + 128]
            m = mixed_grad[:, cols : cols + 128].astype(F32)
            q_grad = jnp.zeros((ROWS, 128), F32)
            k_grad = jnp.zeros((ROWS, 128), F32)
            v_grad = jnp.zeros((ROWS, 128), F32)
            for head in range(2):
                prob = prob_in[(image * HEADS // 2 + pair) * 2 + head]
                m_head = jnp.where(half[head], m, 0.0).astype(BF16)
                v_grad = v_grad + tdot(prob.astype(BF16), m_head)
                weight_grad = dot_t(m_head, v)
                along = jnp.sum(prob * weight_grad, -1, keepdims=True)
                score = (prob * (weight_grad - along)).astype(BF16)
                q_grad = q_grad + dot(score, jnp.where(half[head], k, 0.0).astype(BF16))
                k_grad = k_grad + tdot(score, jnp.where(half[head], q, 0.0).astype(BF16))
            proj_grad[rows, cols : cols + 128] = q_grad.astype(BF16)
            proj_grad[rows, width + cols : width + cols + 128] = k_grad.astype(BF16)
            proj_grad[rows, 2 * width + cols : 2 * width + cols + 128] = v_grad.astype(BF16)
        normed = normed_in[rows, :]
        for member in range(3):
            grad = proj_grad[rows, member * width : (member + 1) * width]
            up = weights[4, member * CODE : (member + 1) * CODE, :]
            code_grad = (mask * dot_t(grad, up)).astype(BF16)
            code_grad_out[rows, member * CODE : (member + 1) * CODE] = code_grad
            code = code_in[rows, member * CODE : (member + 1) * CODE]
            keep(image, member, tdot(code, grad))
            keep(image, 4 + member, tdot(code_grad, normed))


def early_sum_kernel(came, keep, send, hid):
    me = lax.axis_index("tensor")
    for index in range(4):
        start = pl.multiple_of(lax.bitwise_xor(me, index) * 16, 16)
        total = came[0, pl.ds(start, 16), :].astype(F32)
        for owner in range(1, came.shape[0]):
            total = total + came[owner, pl.ds(start, 16), :].astype(F32)
        (keep, send)[index % 2][index // 2] = total.astype(BF16)
    total = came[0, 64:96, :].astype(F32)
    for owner in range(1, came.shape[0]):
        total = total + came[owner, 64:96, :].astype(F32)
    hid[...] = total.astype(BF16)


def late_sum_kernel(came, ids, hid, rows_a, rows_b, rows_c, out):
    square = (CODE, CODE)
    total = jnp.zeros(square, F32)
    same = lax.rem(sublanes(square), RANK) == lax.rem(lanes(square), RANK)
    kind = (sublanes(square) // RANK).astype(F32)
    for owner in range(ids.shape[0]):
        chosen = jnp.logical_and(same, kind == ids[owner, 0:1, :].astype(F32))
        total = total + dot(jnp.where(chosen, 1.0, 0.0).astype(BF16), came[owner])
    total = total.astype(BF16)
    rows = rows_a[0].astype(F32) + rows_b[0].astype(F32) + rows_c[...].astype(F32)
    rows = rows.astype(BF16)
    for owner in range(out.shape[0]):
        out[owner, 0:32, :] = hid[...]
        out[owner, 32:48, :] = rows
        for slab in range(4):
            out[owner, 48:80, slab * 128 : (slab + 1) * 128] = total[
                slab * 32 : (slab + 1) * 32, :
            ]


def unpack_kernel(
    came, own, core, side, both,
    down_in, up_out, up_exo, router_out, heads, down_heads, up_hid, down_hid, router,
):
    me = lax.axis_index("tensor")
    for owner in range(8):
        member, at = divmod(owner * 32, CODE)
        (up_hid, down_hid)[member][at : at + 32, :] = came[owner, 0:32, :].astype(F32)
    for member in range(4):
        target = down_heads if member == 3 else heads.at[member]
        for slab in range(4):
            target[slab * 32 : (slab + 1) * 32, :] = came[
                member, 48:80, slab * 128 : (slab + 1) * 128
            ].astype(F32)
    late = (down_in.at[0], down_in.at[1], down_in.at[2], up_out)
    early = (down_in.at[3], down_in.at[4], up_exo, router)
    for index, part in enumerate((own, core, side, both)):
        spot = lax.bitwise_xor(me, index)
        cols = pl.ds(pl.multiple_of(spot * 128, 128), 128)
        for member in range(4):
            for slab in range(4):
                late[member][slab * 32 : (slab + 1) * 32, cols] = part[
                    member * 32 : (member + 1) * 32, slab * 128 : (slab + 1) * 128
                ].astype(F32)
        for owner in range(8):
            rows = pl.ds(pl.multiple_of((owner % 2) * 64 + spot * 16, 16), 16)
            early[owner // 2][rows, :] = part[
                128 + owner * 16 : 144 + owner * 16, :
            ].astype(F32)
    total = router[0:EXPERTS, 0:CODE] + router[EXPERTS : 2 * EXPERTS, 0:CODE]
    for adapter in range(ADAPTERS):
        router_out[adapter] = total[:, adapter * RANK : (adapter + 1) * RANK]


def input_kernel(
    middle_grad, proj_grad, code_grad, x_in, gain, weights, down, input_grad, wide
):
    images = middle_grad.shape[0] // ROWS
    width = middle_grad.shape[1]
    for image in range(images):
        at = image * ROWS
        rows = slice(at, at + ROWS)
        normed_grad = jnp.zeros((ROWS, width), F32)
        for member in range(3):
            grad = proj_grad[rows, member * width : (member + 1) * width]
            normed_grad = normed_grad + dot_t(grad, weights[member])
            code = code_grad[rows, member * CODE : (member + 1) * CODE]
            normed_grad = normed_grad + dot(code, down[member])
        wide[...] = middle_grad[rows, :] + norm_back(x_in[rows, :], gain[0:1, :], normed_grad)
        input_grad[image * SEQ : (image + 1) * SEQ, :] = wide[0:SEQ, :]


def finish_kernel(middle, part_a, part_b, part_c, out, wide):
    images = middle.shape[0] // ROWS
    for image in range(images):
        rows = slice(image * ROWS, (image + 1) * ROWS)
        part = part_a[0, rows, :].astype(F32) + part_b[0, rows, :].astype(F32)
        wide[...] = middle[rows, :] + (part + part_c[rows, :].astype(F32))
        out[image * SEQ : (image + 1) * SEQ, :] = wide[0:SEQ, :]


def swap(value, bit):
    size = lax.axis_size("tensor")
    return lax.ppermute(value, "tensor", [(at, at ^ bit) for at in range(size)])


def gather_four(value):
    core = swap(value, 1)
    side = swap(value, 2)
    return value, core, side, swap(side, 1)


def after(value, *others):
    return lax.optimization_barrier((value,) + others)[0]


def reduce_pair(keep, send):
    came = swap(send, 1)
    other = (keep[1].astype(F32) + came[1].astype(F32)).astype(BF16)
    return (keep, came, swap(other, 2)), other


def gather_projections(shards, extra, ids, others):
    size = lax.axis_size("dp")
    feats = shards.shape[1]
    if size == 8 and feats % 16 == 0:
        block = jnp.concatenate([shards.reshape(-1, 128), ids], 0)
        ring = Ring(jnp.stack([block, swap(block, 2)]))
        begun = ()
        for step in range(size // 2 - 1):
            ring.step(*(others[1:] if step == 2 else ()))
            begun += (ring.done,)
        parts = ring.finish()
        others = others[:1]
        return begun, *call(
            partial(assemble_kernel, size),
            (like((2, 5, size * feats, 128), BF16), like((size,) + ids.shape, BF16)),
            cost=cost(2),
        )(*parts, after(extra, *others), swap(extra, 2))
    whole = lax.all_gather(shards, "dp", axis=1, tiled=True)
    whole = jnp.concatenate([whole, extra[None]], 0)
    return ((),) * 3, jnp.stack([whole, swap(whole, 2)]), ids[None]


class Ring:
    def __init__(self, block):
        self.size = lax.axis_size("dp")
        self.block, self.parts, self.done = block, [], ()

    def along(self, value):
        size = self.size
        return lax.ppermute(value, "dp", [(at, (at + 2) % size) for at in range(size)])

    def across(self, value):
        return lax.ppermute(value, "dp", [(at, at ^ 1) for at in range(self.size)])

    def step(self, *waits, across=()):
        block = after(self.block, *self.done, *waits)
        self.done = self.along(block), self.across(after(block, *across))
        self.parts += [block, self.done[1]]
        self.block = self.done[0]

    def finish(self, *waits, split=None):
        if split is None:
            block = after(self.block, *self.done, *waits)
            return self.parts + [block, self.across(block)]
        passed, crossed = self.done
        return (
            self.parts + [passed],
            self.across(after(passed, *waits[:1])[:, :split]),
            lambda *waits: self.along(after(crossed, *waits)[:, split:]),
        )


class Whole:
    def __init__(self, block):
        self.parts = [lax.all_gather(block, "dp", axis=2, tiled=True)]
        self.done = ()

    def step(self, *waits, across=()):
        pass

    def finish(self, *waits, split=None):
        return self.parts, None, lambda *waits: None


def per_device(
    tokens,
    cotangent,
    norm_gain,
    qkv_weight,
    out_weight,
    expert_in,
    expert_out,
    router_weight,
    down_in,
    up_heads,
    up_hidden,
    up_router,
    down_heads,
    down_hidden,
    up_attn_out,
    up_expert_out,
    routes,
    priority,
    adapter_index,
):
    width = tokens.shape[1]
    local = tokens.shape[0]
    images = local // SEQ
    group_images = routes.shape[0] // SEQ
    count = images * ROWS
    tall = group_images * ROWS
    hidden = expert_in.shape[2]
    dp = lax.axis_size("dp")
    tensor = lax.axis_size("tensor")

    block = jnp.concatenate([qkv_weight, out_weight[None]], 0)
    ids = jnp.repeat(adapter_index.astype(BF16), CODE // adapter_index.shape[0])
    ids = jnp.broadcast_to(ids[None], (16, CODE))
    extra = jnp.concatenate(
        [
            up_heads.reshape(3 * CODE, up_heads.shape[3]),
            down_heads.swapaxes(1, 2).reshape(CODE, down_heads.shape[1]),
        ],
        0,
    )
    base = EXPERTS // 2
    fits = dp == 8 and expert_in.shape[1] % 16 == 0
    gather = Ring if fits else Whole
    early_ring = gather(jnp.stack([expert_in[:base], expert_out[:base]]))
    early_ring.step()
    late_block = jnp.stack([expert_in[base:], expert_out[base:]])

    down = down_in.swapaxes(2, 3).reshape(5, CODE, width)
    down_hid = down_hidden.swapaxes(1, 2).reshape(CODE, hidden)
    up_hid = up_hidden.reshape(CODE, hidden)
    up_out = up_attn_out.reshape(CODE, width)
    up_exo = up_expert_out.reshape(CODE, width)
    router = jnp.pad(jnp.tile(router_weight.T, (2, 1)), ((0, 128 - 2 * EXPERTS), (0, 0)))
    router_up = up_router.transpose(2, 0, 1).reshape(EXPERTS, CODE)
    router_up = jnp.pad(jnp.tile(router_up, (2, 1)), ((0, 128 - 2 * EXPERTS), (0, 0)))

    spare = ROWS - SEQ
    route_row = jnp.pad(
        routes.T.reshape(2, group_images, SEQ), ((0, 0), (0, 0), (0, spare)), constant_values=-1
    ).reshape(2, tall)
    rank_row = jnp.pad(
        priority.reshape(group_images, SEQ), ((0, 0), (0, spare)), constant_values=1 << 20
    ).reshape(1, tall)
    chunk_units = (2 * count + EXPERTS * (UNIT - 1)) // UNIT
    expert_units = -(-CAP // UNIT) + 4
    by_chunk = lambda value: value.reshape(-1, tensor, count).swapaxes(0, 1)
    dy, place, table = call(
        route_kernel,
        (
            like((count, width), BF16),
            like((tensor, 2, count), F32),
            like((2 * EXPERTS, 128), jnp.int32),
        ),
        scratch=[pltpu.VMEM((count, width), F32)],
        cost=cost(5),
    )(cotangent, route_row, by_chunk(route_row), by_chunk(rank_row), rank_row.T)
    dy_side = swap(dy, 2)
    dy_near = jnp.stack([dy, dy_side])
    dy_far = swap(dy_near, 1)
    begun, mine, ids = gather_projections(block, extra, ids, (dy_side,) + early_ring.done)
    early_ring.step(*begun[1])
    late_ring = gather(after(late_block, *begun[2]))
    late_ring.step()
    other = swap(mine, 1)

    (
        weights, x, normed, code, qkv, prob, mixed, hcode, middle, normed2,
    ) = call(
        forward_kernel,
        (
            like((5, width, width), BF16),
            like((count, width), F32),
            like((count, width), BF16),
            like((count, 3 * CODE), BF16),
            like((count, 3 * width), BF16),
            like((images * HEADS, ROWS, ROWS), F32),
            like((count, width), BF16),
            like((count, CODE), BF16),
            like((count, width), F32),
            like((count, width), BF16),
        ),
        scratch=[pltpu.VMEM((count, width), F32)],
        smem=1,
        cost=cost(10),
        vmem=56,
    )(adapter_index, tokens, norm_gain, mine, other, down, up_out)

    normed2_four = gather_four(normed2)
    normed2_four = (after(normed2, *early_ring.done),) + normed2_four[1:]
    early_ring.step(normed2)
    late_ring.step(normed2_four[2])
    row_wide = 2 * width + 128
    chunk_slots = chunk_units * UNIT
    expert_slots = expert_units * UNIT
    slots, rows, rcode, probs = call(
        dispatch_kernel,
        (
            like((EXPERTS, expert_slots, row_wide), BF16),
            like((tensor, count, width), BF16),
            like((tensor, count, CODE), BF16),
            like((tensor, count, 128), F32),
        ),
        scratch=[
            pltpu.VMEM((tensor, count, row_wide), BF16),
            pltpu.VMEM((chunk_slots, row_wide), BF16),
        ],
        smem=2,
        cost=cost(17),
        vmem=56,
    )(adapter_index, table, *normed2_four, dy_near, dy_far, place, down, router, router_up)

    part = base // 2
    common, near, far = early_ring.finish(slots, split=part)
    far = far(slots)
    ready = late_ring.done
    late_ring.step(slots, across=(near, far) if fits else ())
    whole = lambda *shape: pl.BlockSpec(shape, lambda step: (0,) * len(shape))
    smem = pl.BlockSpec(memory_space=pltpu.SMEM)
    vmem = pl.BlockSpec(memory_space=pltpu.VMEM)
    hbm = pl.BlockSpec(memory_space=pltpu.HBM)
    joined = [
        pltpu.VMEM((2, 2, width, hidden), BF16),
        pltpu.SemaphoreType.DMA((2, 8 if fits else 1)),
    ]
    each = lambda wide, first: pl.BlockSpec(
        (1, expert_slots, wide), lambda step: (step + first, 0, 0)
    )
    small = [
        whole(CODE, hidden), whole(CODE, hidden), whole(CODE, width), whole(5, CODE, width),
    ]
    sums = [whole(2, CODE, hidden), whole(2, CODE, width)]
    grad_wide = width + 128

    def experts(parts, pieces, count, first, at, slots, before=()):
        return call(
            partial(expert_kernel, len(parts), pieces, count, first, at),
            (
                like((count, expert_slots, grad_wide), BF16),
                like((count, expert_slots, width), BF16),
                like((2, CODE, hidden), F32),
                like((2, CODE, width), F32),
            ),
            scratch=joined,
            grid=(count,),
            in_specs=[hbm] * len(parts) + [each(row_wide, at)] + small + sums[: len(before)],
            out_specs=(each(grad_wide, 0), each(width, 0), *sums),
            cost=cost(4 * count),
            vmem=56,
        )(*parts, slots, up_hid, down_hid, up_exo, down, *before)

    near, pieces = ([near], (0,)) if fits else ([], ())
    grad_a, mix_a, *before = experts(
        common + near, pieces, part, 0, 0, after(slots, *ready)
    )
    far, pieces = ([far], (part,)) if fits else ([], ())
    grad_b, mix_b, *before = experts(
        common + far, pieces, base - part, part, part, after(slots, *late_ring.done), before
    )
    common, near, far = late_ring.finish(grad_a, split=part)
    halves, pieces = ([near, far(grad_a)], (0, part)) if fits else ([], ())
    count_last = EXPERTS - base
    half = like((2, count, width), BF16)
    compact = dp == 8 and images == 2 and hidden == width == 512
    place = place.swapaxes(1, 2)
    last_parts = common + halves
    mix_c, grad_keep, grad_send, early = call(
        partial(last_kernel, len(last_parts), pieces, count_last, 0, base),
        (
            like((count_last, expert_slots, width), BF16),
            half, half,
            like((8, 96, width), BF16) if compact else like((6, CODE, width), F32),
        ),
        scratch=joined
        + [
            pltpu.VMEM((EXPERTS, expert_slots, grad_wide), BF16),
            pltpu.VMEM((2, CODE, hidden), F32),
            pltpu.VMEM((2, CODE, width), F32),
            pltpu.VMEM((2, CODE, width), F32),
            pltpu.VMEM((chunk_slots, grad_wide), BF16),
            pltpu.VMEM((tensor, count, width), BF16),
            pltpu.VMEM((tensor, count, CODE), BF16),
            pltpu.VMEM((tensor, count, 128), F32),
            pltpu.SemaphoreType.DMA((5,)),
        ],
        grid=(count_last,),
        in_specs=[hbm] * len(last_parts)
        + [each(row_wide, base)]
        + small
        + sums
        + [smem] * 2
        + [whole(tensor, count, 2), whole(128, width), whole(128, CODE)]
        + [hbm] * 5,
        out_specs=(
            each(width, 0), whole(2, count, width), whole(2, count, width),
            whole(8, 96, width) if compact else whole(6, CODE, width),
        ),
        cost=cost(25),
        vmem=56,
    )(
        *last_parts, slots, up_hid, down_hid, up_exo, down, *before,
        adapter_index, table, place, router, router_up, grad_a, grad_b, rows, rcode, probs,
    )
    mix_keep, mix_send = call(
        mix_kernel,
        (half, half),
        scratch=[pltpu.VMEM((chunk_slots, width), BF16)],
        in_specs=[smem] + [vmem] * 4,
        out_specs=(vmem, vmem),
        cost=cost(7),
        vmem=56,
    )(table, place, mix_a, mix_b, mix_c)

    both = ("dp", "tensor")
    grads, begun = reduce_pair(grad_keep, grad_send)
    if compact:
        early = lax.all_to_all(after(early, begun), "dp", 0, 0)

    middle_grad, proj_grad, code_grad, late = call(
        backward_kernel,
        (
            like((count, width), F32),
            like((count, 3 * width), BF16),
            like((count, 3 * CODE), BF16),
            like((32, images * RANK, 128), BF16) if compact else like((8, CODE, width), F32),
        ),
        scratch=[pltpu.VMEM((ROWS, width), BF16), pltpu.VMEM((8, CODE, width), F32)],
        smem=1,
        cost=cost(11),
        vmem=56,
    )(
        adapter_index, after(dy, mix_send), middle, *grads, norm_gain, weights, up_out,
        normed, code, qkv, prob, mixed, hcode,
    )
    if compact:
        came = lax.all_to_all(late, both, 0, 0)
    mixes, unused = reduce_pair(mix_keep, after(mix_send, late))
    input_grad = call(
        input_kernel,
        like((local, width), F32),
        scratch=[pltpu.VMEM((ROWS, width), F32)],
        cost=cost(5),
        vmem=56,
    )(middle_grad, proj_grad, code_grad, x, norm_gain, weights, down)
    block_out = call(
        finish_kernel,
        like((local, width), F32),
        scratch=[pltpu.VMEM((ROWS, width), F32)],
        cost=cost(2),
    )(after(middle, late), *mixes)

    if compact:
        keep = like((2, 16, width), BF16)
        keep, send, early_hid = call(
            early_sum_kernel, (keep, keep, like((32, width), BF16)), cost=cost(2)
        )(after(early, late))
        sums, unused = reduce_pair(keep, send)
        packed = call(late_sum_kernel, like((dp, 80, width), BF16), cost=cost(2))(
            came.reshape(dp, CODE, 128), ids, early_hid, *sums
        )
        came = lax.all_to_all(packed, "dp", 0, 0)
        came = after(came, input_grad, block_out)
        mine = jnp.concatenate(
            [came[4:, 48:].reshape(128, width), came[:, 32:48].reshape(128, width)], 0
        )
        whole = like((CODE, width), F32)
        (
            grad_down_in, grad_up_out, grad_up_exo, router_grad,
            grad_up_heads, grad_down_heads, grad_up_hidden, grad_down_hidden,
        ) = call(
            unpack_kernel,
            (
                like((5, CODE, width), F32), whole, whole, like((ADAPTERS, EXPERTS, RANK), F32),
                like((3, CODE, 128), F32), like((CODE, 128), F32), whole, whole,
            ),
            scratch=[pltpu.VMEM((CODE, width), F32)],
            cost=cost(3),
        )(came, *gather_four(mine))
    else:
        cols = width // tensor
        early_shared = lax.psum(early[:4], both)
        early_hid = lax.psum(early[4:], "dp")
        late = lax.psum(late, both)
        late_heads = lax.dynamic_slice_in_dim(
            late[:4], lax.axis_index("tensor") * cols, cols, 2
        )
        grad_down_in = jnp.concatenate([late[4:7], early_shared[:2]], 0)
        grad_up_out, grad_up_exo = late[7], early_shared[2]
        router_grad = early_shared[3, :, :CODE]
        router_grad = router_grad[:EXPERTS] + router_grad[EXPERTS : 2 * EXPERTS]
        router_grad = router_grad.reshape(EXPERTS, ADAPTERS, RANK).swapaxes(0, 1)
        grad_up_heads, grad_down_heads = late_heads[:3], late_heads[3]
        grad_up_hidden, grad_down_hidden = early_hid[0], early_hid[1]
    split_up = lambda value: value.reshape(value.shape[:-2] + (ADAPTERS, RANK, value.shape[-1]))
    split_down = lambda value: split_up(value).swapaxes(-1, -2)
    grad_down_in = split_down(grad_down_in)
    grad_up_out = split_up(grad_up_out)
    grad_up_exo = split_up(grad_up_exo)
    grad_up_router = router_grad.swapaxes(1, 2)
    grad_up_heads = split_up(grad_up_heads)
    grad_down_heads = split_down(grad_down_heads)
    grad_up_hidden = split_up(grad_up_hidden)
    grad_down_hidden = split_down(grad_down_hidden)
    return (
        block_out,
        input_grad,
        grad_down_in,
        grad_up_heads,
        grad_up_hidden,
        grad_up_router,
        grad_down_heads,
        grad_down_hidden,
        grad_up_out,
        grad_up_exo,
    )


def solution(mesh):
    placed = (
        P(("dp", "tensor"), None),
        P(("dp", "tensor"), None),
        P(),
        P(None, "dp", "tensor"),
        P("dp", "tensor"),
        P(None, "dp", "tensor"),
        P(None, "dp", "tensor"),
        P(),
        P(),
        P(None, None, None, "tensor"),
        P(None, None, "tensor"),
        P(),
        P(None, "tensor", None),
        P(None, "tensor", None),
        P(),
        P(),
        P("dp", None),
        P("dp", None),
        P("dp"),
    )
    return jax.shard_map(
        per_device,
        mesh=mesh,
        in_specs=placed,
        out_specs=(
            P(("dp", "tensor"), None),
            P(("dp", "tensor"), None),
            P(),
            P(None, None, None, "tensor"),
            P(None, None, "tensor"),
            P(),
            P(None, "tensor", None),
            P(None, "tensor", None),
            P(),
            P(),
        ),
        check_vma=False,
    )
```
